128 devices in a mesh: case: 2 (over core), space: 64 (over y, x, z).
Axes of the slice: x: 4, y: 4, z: 4, core: 2. Of those that a mesh axis runs over, the one named last changes fastest.
Arguments:
- design: float32 [512, 40, 128], P('space'), may hold values from 0.05 to 1
- passive: int32 [512, 40, 128], P('space'), may hold values from 0 to 2, as said below
- fixed_mask: int32 [512, 40, 128], P('space'), may hold values 0 or 1
- load_index: int32 [4, 4096], P('case'), may hold values from 0 to 2621439
Outputs:
- state: float32 [4, 512, 40, 128], P('case', 'space')
- sensitivity: float32 [512, 40, 128], P('space')
The draws below stay inside these ranges and needn't reach their ends.
Inputs may be any that keep to these rules, and one draw needn't show every extreme that they name: `passive`: 0 marks a design voxel, 1 a voxel held solid, 2 a voxel held void.
All inputs are finite; a program needn't handle non-finite values. No bound on the sum of `fixed_mask` on one device may be relied on, other than what follows from the above.
Results may differ from the reference program's by a relative error of at most 0.0001.
Values sent between devices are 32-bit elements; how exact they have to be, the bound alone decides.
No kernel may reach another device: no remote copies, remote signals or barrier semaphores. Data moves between devices by JAX's collectives and lax.ppermute only.
A program may use at most 128 MiB of HBM per device.

```python
import jax
import jax.numpy as jnp
from jax import lax

NX = 128
NY = 40
CASES = 4
NLOADS = 4096
LEVELS = 3
COARSE_SWEEPS = 8
ITERS = 3
NZ = 512


def draw_passive(key, part):
    key = jax.random.fold_in(key, 7)
    rolled = jax.random.randint(key, (NZ, NY, NX), 0, 10)
    return jnp.where(rolled == 0, 1, jnp.where(rolled == 1, 2, 0)).astype(jnp.int32)


def touch_ends(array, stream_key, least, high):
    longest = array.shape.index(max(array.shape))
    spots = []
    for shift in (0, 1):
        where = [jax.random.randint(jax.random.fold_in(stream_key, axis), (), 0, length) for axis, length in enumerate(array.shape)]
        where[longest] = (where[longest] + shift) % array.shape[longest]
        spots.append(tuple(where))
    return array.at[spots[0]].set(least).at[spots[1]].set(high)


def level_of(rng, shape, pieces, low, high):
    loudness = 1.0
    for dim, parts in pieces:
        heights = jax.random.uniform(jax.random.fold_in(jax.random.fold_in(rng, 6), dim), (parts,), jnp.float32, low / len(pieces), high / len(pieces))
        loudness = loudness * jnp.repeat(jnp.exp(heights), shape[dim] // parts).reshape((-1,) + (1,) * (len(shape) - 1 - dim))
    return loudness


def setup_inputs(seed: int = 0) -> dict:
    arg_keys = jax.random.split(jax.random.key(seed), 5)
    return {
        "design": jnp.clip(0.05 + 0.95 * jax.random.uniform(arg_keys[0], (NZ, NY, NX), jnp.float32) ** level_of(arg_keys[0], (NZ, NY, NX), ((0, 64),), -0.2, 0.2), 0.05, 1.0),
        "passive": draw_passive(jax.random.fold_in(arg_keys[4], 71), 0),
        "fixed_mask": touch_ends((jax.random.randint(arg_keys[2], (NZ, NY, NX), 0, 50) < 1).astype(jnp.int32), jax.random.fold_in(arg_keys[2], 1), 0, 1),
        "load_index": touch_ends(jax.random.randint(arg_keys[3], (CASES, NLOADS), 0, NX * NY * NZ), jax.random.fold_in(arg_keys[3], 1), 0, (NX * NY * NZ) - 1).astype(jnp.int32),
    }


E_MIN = 0.01
OMEGA = 0.8
HEAT_SOURCE = 0.05
EDGE_WEIGHT = 1.5 - 2.0 ** 0.5

def cone_filter(padded):
    framed = jnp.pad(padded, [(0, 0)] * (padded.ndim - 2) + [(1, 1), (1, 1)])
    depth_z = padded.shape[-3] - 2
    rows_y = padded.shape[-2]
    cols_x = padded.shape[-1]
    summed = 1.5 * framed[..., 1:1 + depth_z, 1:1 + rows_y, 1:1 + cols_x]
    for offset_z in (-1, 0, 1):
        for offset_y in (-1, 0, 1):
            for offset_x in (-1, 0, 1):
                distance = offset_z * offset_z + offset_y * offset_y + offset_x * offset_x
                if distance == 1:
                    weight = 0.5
                elif distance == 2:
                    weight = EDGE_WEIGHT
                else:
                    continue
                summed = summed + weight * framed[..., 1 + offset_z:1 + offset_z + depth_z, 1 + offset_y:1 + offset_y + rows_y, 1 + offset_x:1 + offset_x + cols_x]
    return summed

def edges(values, dimension, before, behind):
    widths = [(0, 0)] * values.ndim
    widths[dimension] = (before, behind)
    return jnp.pad(values, widths)

def conductances(modulus):
    along_x = jnp.sqrt(modulus[..., :, :, 1:] * modulus[..., :, :, :-1])
    along_y = jnp.sqrt(modulus[..., :, 1:, :] * modulus[..., :, :-1, :])
    along_z = jnp.sqrt(modulus[..., 1:, :, :] * modulus[..., :-1, :, :])
    return (along_x, along_y, along_z)

def face_total(couplings):
    along_x, along_y, along_z = couplings
    result = edges(along_x, -1, 1, 0) + edges(along_x, -1, 0, 1)
    result = result + edges(along_y, -2, 1, 0) + edges(along_y, -2, 0, 1)
    return result + edges(along_z, -3, 1, 0) + edges(along_z, -3, 0, 1)

def laplace(values, couplings):
    along_x, along_y, along_z = couplings
    flux_x = along_x * (values[..., 1:] - values[..., :-1])
    flux_y = along_y * (values[..., 1:, :] - values[..., :-1, :])
    flux_z = along_z * (values[..., 1:, :, :] - values[..., :-1, :, :])
    result = edges(flux_x, -1, 1, 0) - edges(flux_x, -1, 0, 1)
    result = result + edges(flux_y, -2, 1, 0) - edges(flux_y, -2, 0, 1)
    return result + edges(flux_z, -3, 1, 0) - edges(flux_z, -3, 0, 1)

def cell_energy(values, couplings):
    along_x, along_y, along_z = couplings
    power_x = along_x * (values[..., 1:] - values[..., :-1]) ** 2
    power_y = along_y * (values[..., 1:, :] - values[..., :-1, :]) ** 2
    power_z = along_z * (values[..., 1:, :, :] - values[..., :-1, :, :]) ** 2
    result = edges(power_x, -1, 1, 0) + edges(power_x, -1, 0, 1)
    result = result + edges(power_y, -2, 1, 0) + edges(power_y, -2, 0, 1)
    return result + edges(power_z, -3, 1, 0) + edges(power_z, -3, 0, 1)

def build_level(modulus, freedom, factor):
    couplings = conductances(modulus)
    diagonal = freedom * factor * face_total(couplings) + (1.0 - freedom)
    return (freedom, couplings, factor, diagonal)

def operate(values, level):
    freedom, couplings, factor, diagonal = level
    return freedom * factor * laplace(freedom * values, couplings) + (1.0 - freedom) * values

def children(values):
    leading = values.shape[:-3]
    depth_z, rows_y, cols_x = values.shape[-3:]
    return values.reshape(leading + (depth_z // 2, 2, rows_y // 2, 2, cols_x // 2, 2))

def restrict(values):
    return lax.optimization_barrier(jnp.sum(children(values), axis=(-5, -3, -1)))

def coarsen_mean(values):
    return 0.125 * lax.optimization_barrier(jnp.sum(children(values), axis=(-5, -3, -1)))

def coarsen_any(values):
    return lax.optimization_barrier(jnp.max(children(values), axis=(-5, -3, -1)))

def prolong(values):
    return jnp.repeat(jnp.repeat(jnp.repeat(values, 2, axis=-3), 2, axis=-2), 2, axis=-1)

def sweep(values, forcing, level):
    return values + OMEGA * (forcing - operate(values, level)) / level[3]

def vcycle(forcing, levels, tier_index):
    level = levels[tier_index]
    smoothed = OMEGA * forcing / level[3]
    if tier_index == LEVELS:
        for repeat in range(COARSE_SWEEPS - 1):
            smoothed = sweep(smoothed, forcing, level)
        return smoothed
    relaxed = sweep(smoothed, forcing, level)
    leftover = forcing - operate(relaxed, level)
    correction = vcycle(restrict(leftover), levels, tier_index + 1)
    corrected = relaxed + prolong(correction)
    return sweep(sweep(corrected, forcing, level), forcing, level)

def conjugate(forcing, levels):
    solution = jnp.zeros_like(forcing)
    residual = forcing
    precond = vcycle(residual, levels, 0)
    product = jnp.sum(residual * precond)
    direction = precond
    for iteration in range(ITERS):
        applied = operate(direction, levels[0])
        step_size = product / jnp.sum(direction * applied)
        solution = solution + step_size * direction
        residual = residual - step_size * applied
        if iteration + 1 < ITERS:
            precond = vcycle(residual, levels, 0)
            product_next = jnp.sum(residual * precond)
            direction = precond + product_next / product * direction
            product = product_next
    return solution

def reference(design, passive, fixed_mask, load_index):
    zpad = ((1, 1), (0, 0), (0, 0))
    weights = cone_filter(jnp.pad(jnp.ones((NZ, NY, NX), jnp.float32), zpad))
    filtered = cone_filter(jnp.pad(design, zpad)) / weights
    density = jnp.where(passive == 1, 1.0, jnp.where(passive == 2, 0.0, filtered))
    modulus = E_MIN + (1.0 - E_MIN) * density ** 3
    freedom = (1 - fixed_mask).astype(jnp.float32)
    levels = []
    current_mod = modulus
    current_free = freedom
    for tier_index in range(LEVELS + 1):
        levels.append(build_level(current_mod, current_free, 2.0 ** tier_index))
        if tier_index < LEVELS:
            current_mod = coarsen_mean(current_mod)
            current_free = coarsen_any(current_free)
    voxels = NZ * NY * NX
    case_rows = jnp.broadcast_to(jnp.arange(CASES, dtype=jnp.int32)[:, None], load_index.shape)
    sources = jnp.zeros((CASES, voxels), jnp.float32).at[case_rows, load_index].add(1.0)
    sources = (HEAT_SOURCE + sources.reshape(CASES, NZ, NY, NX)) * freedom

    def solve_case(forcing):
        return conjugate(forcing, levels)
    state = lax.map(solve_case, sources)
    energy = jnp.zeros((NZ, NY, NX), jnp.float32)
    for case_number in range(CASES):
        energy = energy + cell_energy(state[case_number] * freedom, levels[0][1])
    gradient = -1.5 * (1.0 - E_MIN) * density ** 2 * energy / modulus
    gradient = jnp.where(passive == 0, gradient, 0.0)
    sensitivity = jnp.where(passive == 0, cone_filter(jnp.pad(gradient / weights, zpad)), 0.0)
    return (state, sensitivity)
```

```python
import functools

import jax
import jax.numpy as jnp
from jax import lax
from jax.experimental import pallas as pl
from jax.experimental.pallas import tpu as pltpu
from jax.sharding import PartitionSpec as P

ITERS = 3
E_MIN = 0.01
OMEGA = 0.8
HEAT_SOURCE = 0.05
EDGE_WEIGHT = 1.5 - 2.0**0.5

F32 = jnp.float32
NY, NX = 40, 128
BLOCK = 8
HALO = 7
WINDOW = BLOCK + 2 * HALO
Q1, R1 = 10, 24
REACH = 11
ND = 2 * REACH + 1
R2 = 16
R3 = 8
TALK = 24
CPARAMS = pltpu.CompilerParams(vmem_limit_bytes=40 * 1024 * 1024)


def iota(shape, dim):
    return lax.broadcasted_iota(jnp.int32, shape, dim)


def roll(v, by, dim):
    return pltpu.roll(v, by % v.shape[dim], dim)


def dot(a, b):
    return lax.dot_general(
        a, b, (((1,), (0,)), ((), ())), precision=lax.Precision.HIGHEST, preferred_element_type=F32
    )


def planes(lo, hi, body, group=2):
    count = (hi - lo) // group

    def step(i, carry):
        for k in range(group):
            body(lo + i * group + k)
        return carry

    lax.fori_loop(0, count, step, 0)
    for j in range(lo + count * group, hi):
        body(j)


def fine_to_half(case):
    i, j = iota((128, 128), 0), iota((128, 128), 1)
    return (j == 64 * case + (i >> 1)).astype(F32)


def half_to_fine(case):
    i, j = iota((128, 128), 0), iota((128, 128), 1)
    return (i == 64 * case + (j >> 1)).astype(F32)


def half_to_quarter(low):
    i, j = iota((128, 128), 0), iota((128, 128), 1)
    return (j == 64 * low + 32 * (i >> 6) + ((i & 63) >> 1)).astype(F32)


def quarter_to_half(low):
    i, j = iota((128, 128), 0), iota((128, 128), 1)
    return (i == 64 * low + 32 * (j >> 6) + ((j & 63) >> 1)).astype(F32)


def quarter_to_eighth():
    i, j = iota((128, 128), 0), iota((128, 128), 1)
    return (j == 16 * ((i >> 5) & 1) + ((i & 31) >> 1)).astype(F32)


def eighth_to_quarter():
    i, j = iota((128, 128), 0), iota((128, 128), 1)
    return (i == 16 * ((j >> 5) & 1) + ((j & 31) >> 1)).astype(F32)


def z_prev(v):
    return jnp.concatenate([jnp.zeros_like(v[:1]), v[:-1]], axis=0)


def z_next(v):
    return jnp.concatenate([v[1:], jnp.zeros_like(v[:1])], axis=0)


def z_prev2(v):
    turned = roll(v, 64, 2)
    return jnp.where(iota(v.shape, 2) >= 64, turned, z_prev(turned))


def z_next2(v):
    turned = roll(v, 64, 2)
    return jnp.where(iota(v.shape, 2) < 64, turned, z_next(turned))


def couple(m, f, factor, width, zp, zn):
    lead = (iota(m.shape, 2) & (width - 1)) > 0
    first = iota(m.shape, 1) > 0
    sides = (
        (lambda v: roll(v, 1, 2), lambda v: roll(v, -1, 2), lead),
        (lambda v: roll(v, 1, 1), lambda v: roll(v, -1, 1), first),
        (zp, zn, None),
    )
    total = jnp.zeros_like(m)
    held = jnp.zeros_like(m)
    coupling = []
    for prev, after, mask in sides:
        k = jnp.sqrt(m * prev(m))
        if mask is not None:
            k = jnp.where(mask, k, 0.0)
        ka = after(k)
        total = total + k + ka
        held = held + k * (1.0 - prev(f)) + ka * (1.0 - after(f))
        coupling.append(factor * k * f * prev(f))
    rest = f * factor * held + (1.0 - f)
    weight = OMEGA / (f * factor * total + (1.0 - f))
    return coupling[0], coupling[1], coupling[2], rest, weight


def apply(v, c, zp, zn):
    kx, ky, kz, rest = c[:4]
    fx = kx * (v - roll(v, 1, 2))
    fy = ky * (v - roll(v, 1, 1))
    fz = kz * (v - zp(v))
    return rest * v + (fx - roll(fx, -1, 2)) + (fy - roll(fy, -1, 1)) + (fz - zn(fz))


def cut(c, lo, hi):
    return tuple(x[lo:hi] for x in c)


def apply_plane(v_ref, case, j, c_ref):
    v = v_ref[case, j]
    fx = c_ref[0, j] * (v - roll(v, 1, 1))
    fy = c_ref[1, j] * (v - roll(v, 1, 0))
    out = c_ref[3, j] * v + (fx - roll(fx, -1, 1)) + (fy - roll(fy, -1, 0))
    return out + c_ref[2, j] * (v - v_ref[case, j - 1]) + c_ref[2, j + 1] * (v - v_ref[case, j + 1])


def pairs_of_rows(v, scratch):
    n, rows, _ = v.shape
    scratch[: n * rows, :] = v.reshape(n * rows, 128)
    half = n * rows // 2
    even = scratch[pl.ds(0, half, stride=2), :]
    odd = scratch[pl.ds(1, half, stride=2), :]
    return (even + odd).reshape(n, rows // 2, 128)


def rows_twice(v, scratch):
    n, rows, _ = v.shape
    flat = v.reshape(n * rows, 128)
    scratch[pl.ds(0, n * rows, stride=2), :] = flat
    scratch[pl.ds(1, n * rows, stride=2), :] = flat
    return scratch[: 2 * n * rows, :].reshape(n, 2 * rows, 128)


def flat_dot(v, matrix):
    n, rows, _ = v.shape
    return dot(v.reshape(n * rows, 128), matrix).reshape(n, rows, 128)


def fine_to_level1(t_ref, r_ref, work, count, split):
    flat0 = t_ref[0, :count].reshape(count * NY, 128)
    flat1 = t_ref[1, :count].reshape(count * NY, 128)
    work[: count * NY, :] = dot(flat0, fine_to_half(0)) + dot(flat1, fine_to_half(1))
    r_ref[...] = jnp.zeros_like(r_ref)
    for p in range(count):
        even = work[pl.ds(p * NY, NY // 2, stride=2), :]
        odd = work[pl.ds(p * NY + 1, NY // 2, stride=2), :]
        r_ref[split + p, 0 : NY // 2, :] = even + odd


def down(r_ref, c0, c1, s1, s2, t_ref, work, s2_out, s21_out, r1_out):
    def first(j):
        for case in range(2):
            s1[case, j] = c0[4, j] * r_ref[case, j]

    planes(1, WINDOW - 1, first)

    def second(j):
        for case in range(2):
            s2[case, j] = s1[case, j] + c0[4, j] * (r_ref[case, j] - apply_plane(s1, case, j, c0))

    planes(2, WINDOW - 2, second)

    def third(q):
        for case in range(2):
            a, b = 2 * q + 3, 2 * q + 4
            t_ref[case, q] = (r_ref[case, a] - apply_plane(s2, case, a, c0)) + (
                r_ref[case, b] - apply_plane(s2, case, b, c0)
            )

    planes(0, 8, third, 1)
    for case in range(2):
        s2_out[case] = s2[case, 5:17]
    fine_to_level1(t_ref, r1_out, work, 8, 1)

    c = tuple(c1[k] for k in range(5))
    forcing = r1_out[1:9]
    smoothed = c[4][1:9] * forcing
    leftover = forcing - apply(smoothed, cut(c, 1, 9), z_prev, z_next)
    relaxed = (smoothed + c[4][1:9] * leftover)[1:7]
    s21_out[...] = relaxed[1:5]
    rest = (forcing[1:7] - apply(relaxed, cut(c, 2, 8), z_prev, z_next))[1:5]
    low, high = rest[0] + rest[1], rest[2] + rest[3]
    mixed = dot(low, half_to_quarter(0)) + dot(high, half_to_quarter(1))
    summed = pairs_of_rows(mixed[None], work)[0]
    return jnp.concatenate([summed, jnp.zeros((4, 128), F32)], axis=0)


def spread(out_ref, tile):
    out_ref[...] = jnp.broadcast_to(tile[None], out_ref.shape)


def count_kernel(me, index, out, acc):
    base = (me[0] * BLOCK - HALO) * NY
    rows = WINDOW * NY
    chunk = 512
    total = index.shape[1]
    for case in range(2):
        acc[...] = jnp.zeros_like(acc)

        def step(i, carry):
            ids = index[pl.ds(case, 1), pl.ds(pl.multiple_of(i * chunk, chunk), chunk)]
            row = (ids >> 7) - base
            col = ids & 127
            hit_row = jnp.where(iota((rows, chunk), 0) == row, 1.0, 0.0).astype(jnp.bfloat16)
            hit_col = jnp.where(iota((128, chunk), 0) == col, 1.0, 0.0).astype(jnp.bfloat16)
            acc[...] += lax.dot_general(
                hit_row, hit_col, (((1,), (1,)), ((), ())), preferred_element_type=F32
            )
            return carry

        lax.fori_loop(0, total // chunk, step, 0)
        out[case] = acc[...].reshape(WINDOW, NY, 128)


def neighbours_x(p):
    lane = iota(p.shape, 1)
    return jnp.where(lane > 0, roll(p, 1, 1), 0.0) + jnp.where(lane < NX - 1, roll(p, -1, 1), 0.0)


def neighbours_y(p):
    row = iota(p.shape, 0)
    return jnp.where(row > 0, roll(p, 1, 0), 0.0) + jnp.where(row < NY - 1, roll(p, -1, 0), 0.0)


def filter_parts(p):
    sides_y = neighbours_y(p)
    cross = neighbours_x(p) + sides_y
    return cross, 1.5 * p + 0.5 * cross + EDGE_WEIGHT * neighbours_x(sides_y)


def weight_of(me, members, z):
    at = me * BLOCK + z
    lane, row = iota((NY, NX), 1), iota((NY, NX), 0)
    nx = (lane > 0).astype(F32) + (lane < NX - 1).astype(F32)
    ny = (row > 0).astype(F32) + (row < NY - 1).astype(F32)
    nz = jnp.where(at > 0, 1.0, 0.0) + jnp.where(at < members * BLOCK - 1, 1.0, 0.0)
    return 1.5 + 0.5 * (nx + ny + nz) + EDGE_WEIGHT * (nx * ny + nx * nz + ny * nz)


def setup_kernel(
    members, me_ref, own, before, after, counts,
    c0, c1, force, s2_out, s21_out, r1_out, talk, mod, free, scale,
    raw, cross, base, s1, s2, t_ref, work, small,
):
    me = me_ref[0]

    def fill(k):
        raw[k] = before[0, k]
        raw[8 + k] = own[0, k]
        raw[16 + k] = after[0, k]

    planes(0, 8, fill, 1)

    def parts(k):
        a, b = filter_parts(raw[k])
        cross[k] = a
        base[k] = b

    planes(0, 24, parts)

    def material(j, passive, fixed):
        z = j - HALO
        at = me * BLOCK + z
        inside = jnp.where((at >= 0) & (at < members * BLOCK), 1.0, 0.0)
        filtered = base[j + 1] + 0.5 * (raw[j] + raw[j + 2]) + EDGE_WEIGHT * (cross[j] + cross[j + 2])
        weight = weight_of(me, members, z)
        density = jnp.where(passive == 1.0, 1.0, jnp.where(passive == 2.0, 0.0, filtered / weight))
        modulus = E_MIN + (1.0 - E_MIN) * density * density * density
        mod[j] = inside * modulus
        freedom = inside * (1.0 - fixed)
        free[j] = freedom
        for case in range(2):
            force[case, j] = freedom * (HEAT_SOURCE + counts[case, j])
        gradient = (-1.5 * (1.0 - E_MIN)) * density * density / (modulus * weight)
        return jnp.where(passive == 0.0, inside * gradient, 0.0)

    def below(j):
        material(j, before[1, j + 1], before[2, j + 1])

    def above(k):
        material(15 + k, after[1, k], after[2, k])

    planes(0, 6, below)
    scale[0] = material(6, before[1, 7], before[2, 7])

    def middle(k):
        scale[1 + k] = material(HALO + k, own[1, k], own[2, k])

    planes(0, 8, middle)
    scale[9] = material(15, after[1, 0], after[2, 0])
    planes(1, 7, above)

    lane, row = iota((NY, NX), 1), iota((NY, NX), 0)
    zero = jnp.zeros((NY, NX), F32)
    c0[2, 0] = zero

    def coefficients(j):
        m, f = mod[j], free[j]
        total, held = zero, zero
        for dim, mask, slot in ((1, lane > 0, 0), (0, row > 0, 1)):
            k = jnp.where(mask, jnp.sqrt(m * roll(m, 1, dim)), 0.0)
            ka = roll(k, -1, dim)
            fp = roll(f, 1, dim)
            total = total + k + ka
            held = held + k * (1.0 - fp) + ka * (1.0 - roll(f, -1, dim))
            c0[slot, j] = k * f * fp
        k, ka = jnp.sqrt(m * mod[j - 1]), jnp.sqrt(m * mod[j + 1])
        total = total + k + ka
        held = held + k * (1.0 - free[j - 1]) + ka * (1.0 - free[j + 1])
        c0[2, j] = k * f * free[j - 1]
        c0[3, j] = f * held + (1.0 - f)
        c0[4, j] = OMEGA / (f * total + (1.0 - f))

    planes(1, WINDOW - 1, coefficients)
    last = WINDOW - 1
    c0[2, last] = jnp.sqrt(mod[last] * mod[last - 1]) * free[last] * free[last - 1]
    for slot in (0, 1, 3, 4):
        c0[slot, 0] = zero
        c0[slot, last] = zero

    def add_up(q):
        t_ref[0, q] = mod[2 * q + 1] + mod[2 * q + 2]
        t_ref[1, q] = free[2 * q + 1] + free[2 * q + 2]

    planes(0, Q1, add_up)
    fine_to_level1(t_ref, small, work, Q1, 0)
    both = small[...]
    second = iota(both.shape, 2) >= 64
    both = jnp.where(second, (both > 0.0).astype(F32), 0.125 * both)
    turned = roll(both, 64, 2)
    m1 = jnp.where(second, turned, both)
    f1 = jnp.where(second, both, turned)
    for k, value in enumerate(couple(m1, f1, 2.0, 64, z_prev, z_next)):
        c1[k] = value

    low, high = both[3] + both[4], both[5] + both[6]
    mixed = dot(low, half_to_quarter(0)) + dot(high, half_to_quarter(1))
    coarse = pairs_of_rows(mixed[None], work)[0]
    is_free = (iota(coarse.shape, 1) & 32) > 0
    coarse = jnp.where(is_free, (coarse > 0.0).astype(F32), 0.125 * coarse)

    tile = down(force, c0, c1, s1, s2, t_ref, work, s2_out, s21_out, r1_out)
    small[0, 0:16, :] = tile
    small[0, 10:22, :] = coarse
    spread(talk, small[0])


def coarse_window(me, members, gathered, rows):
    lo, hi = rows
    tiles = []
    for d in range(ND):
        at = me + d - REACH
        inside = jnp.where((at >= 0) & (at < members), 1.0, 0.0)
        tiles.append(inside * gathered[jnp.clip(at, 0, members - 1), lo:hi, :])
    return jnp.stack(tiles, axis=0)


def coarse_setup(me, members, gathered, c2, c3, work, wide):
    wide[...] = jnp.zeros_like(wide)
    wide[:, 0:10, :] = coarse_window(me, members, gathered, (10, 20))
    both = wide[...]
    is_free = (iota(both.shape, 2) & 32) > 0
    m = jnp.where(is_free, roll(both, 32, 2), both)
    f = jnp.where(is_free, both, roll(both, -32, 2))
    for k, value in enumerate(couple(m, f, 4.0, 32, z_prev2, z_next2)):
        c2[k] = value
    eighth = quarter_to_eighth()
    m3 = 0.125 * pairs_of_rows(flat_dot(m, eighth), work)
    f3 = (pairs_of_rows(flat_dot(f, eighth), work) > 0.0).astype(F32)
    for k, value in enumerate(couple(m3, f3, 8.0, 16, z_prev, z_next)):
        c3[k] = value


def coarse_solve(r2, c2, c3, work):
    c = tuple(c2[k] for k in range(5))
    smoothed = c[4] * r2
    relaxed = smoothed + c[4] * (r2 - apply(smoothed, c, z_prev2, z_next2))
    leftover = (r2 - apply(relaxed, c, z_prev2, z_next2))[2 : ND - 2]
    forcing = pairs_of_rows(flat_dot(leftover, quarter_to_eighth()), work)
    lo, hi = 2, ND - 2
    v = c3[4, lo:hi] * forcing
    for _ in range(7):
        ck = tuple(c3[k, lo:hi] for k in range(5))
        v = v + ck[4] * (forcing - apply(v, ck, z_prev, z_next))
        v, forcing = v[1:-1], forcing[1:-1]
        lo, hi = lo + 1, hi - 1
    up = rows_twice(flat_dot(v, eighth_to_quarter()), work)
    lo, hi = REACH - 2, REACH + 3
    v = relaxed[lo:hi] + up
    ck = cut(c, lo, hi)
    for _ in range(2):
        v = v + ck[4] * (r2[lo:hi] - apply(v, ck, z_prev2, z_next2))
    return v[1:4]


def up_kernel(
    members, first, me_ref, gathered, r_ref, s2_ref, s21, s21_before, s21_after, r1_ref, c0, c1, *rest
):
    if first:
        out, c2, c3, va, vb, work, wide = rest
    else:
        c2, c3, out, dots, va, vb, work, wide = rest
    me = me_ref[0]
    if first:
        coarse_setup(me, members, gathered, c2, c3, work, wide)
    else:
        total = gathered[0, 8:16, :]
        for d in range(1, members):
            total = total + gathered[d, 8:16, :]
        dots[...] = total
    r2 = coarse_window(me, members, gathered, (0, 16))
    r2 = jnp.where(iota(r2.shape, 1) < 10, r2, 0.0)
    e2 = coarse_solve(r2, c2, c3, work)

    parts = []
    for low in range(2):
        spread_out = flat_dot(e2, quarter_to_half(low))
        parts.append(rows_twice(spread_out, work)[:, :R1])
    lifted = [parts[(z + 2) & 1][(z + 2) >> 1] for z in range(-2, 4)]
    correction = jnp.stack([lifted[(q - 3) // 2 + 2] for q in range(Q1)], axis=0)
    relaxed = jnp.concatenate([s21_before[1:4], s21[...], s21_after[0:3]], axis=0)
    c = tuple(c1[k] for k in range(5))
    v = relaxed + correction
    v = (v + c[4] * (r1_ref[...] - apply(v, c, z_prev, z_next)))[1:9]
    v = (v + c[4][1:9] * (r1_ref[1:9] - apply(v, cut(c, 1, 9), z_prev, z_next)))[1:7]

    for case in range(2):
        work[0 : 12 * R1, :] = rows_twice(flat_dot(v, half_to_fine(case)), work).reshape(12 * R1, 128)
        for p in range(6):
            fine = work[p * 2 * R1 : p * 2 * R1 + NY, :]
            va[case, 5 + 2 * p] = s2_ref[case, 2 * p] + fine
            va[case, 6 + 2 * p] = s2_ref[case, 2 * p + 1] + fine

    def once(j):
        for case in range(2):
            vb[case, j] = va[case, j] + c0[4, j] * (r_ref[case, j] - apply_plane(va, case, j, c0))

    planes(6, 16, once)

    def twice(j):
        for case in range(2):
            out[case, j - HALO] = vb[case, j] + c0[4, j] * (r_ref[case, j] - apply_plane(vb, case, j, c0))

    planes(7, 15, twice)


def lay_out(win, own, before, after, width):
    for case in range(2):
        for k in range(width):
            win[case, HALO - 1 - k] = before[case, before.shape[1] - 1 - k]
            win[case, HALO + BLOCK + k] = after[case, k]

    def inner(k):
        for case in range(2):
            win[case, HALO + k] = own[case, k]

    planes(0, BLOCK, inner)


def dot_rows(values):
    lane = iota((1, 128), 1)
    rows = []
    for a, b in values:
        rows.append(jnp.where(lane < 64, jnp.sum(a, keepdims=True), jnp.sum(b, keepdims=True)))
    return rows


def accumulate(count, term):
    def step(k, carry):
        return tuple(
            tuple(s + t for s, t in zip(carry[case], term(case, k))) for case in range(2)
        )

    zero = jnp.zeros((NY, NX), F32)
    start = tuple(tuple(zero for _ in range(count)) for _ in range(2))
    sums = lax.fori_loop(0, BLOCK, step, start)
    return dot_rows([(sums[0][i], sums[1][i]) for i in range(count)])


def finish_talk(talk, tile, rows, small):
    small[0, 0:16, :] = tile
    for i, row in enumerate(rows):
        small[0, 10 + i : 11 + i, :] = row
    spread(talk, small[0, 0:16])


def first_kernel(
    own, before, after, force, c0, c1,
    u_win, w_win, s2_out, s21_out, r1_out, talk,
    s1, s2, t_ref, work, small,
):
    lay_out(u_win, own, before, after, HALO)

    def image(j):
        for case in range(2):
            w_win[case, j] = apply_plane(u_win, case, j, c0)

    planes(1, WINDOW - 1, image)

    def term(case, k):
        u = own[case, k]
        return (force[case, HALO + k] * u, w_win[case, HALO + k] * u)

    rows = accumulate(2, term)
    tile = down(w_win, c0, c1, s1, s2, t_ref, work, s2_out, s21_out, r1_out)
    finish_talk(talk, tile, rows, small)


def of_case(row, case):
    return row[:, 64 * case : 64 * case + 1]


def second_kernel(
    own, before, after, dots0, force, u0, w0, c0, c1,
    m_win, u1, w1, n0, s2_out, s21_out, r1_out, talk,
    s1, s2, t_ref, work, small,
):
    lay_out(m_win, own, before, after, HALO)
    alpha = [of_case(dots0[2:3, :] / dots0[3:4, :], case) for case in range(2)]

    def update(j):
        for case in range(2):
            u1[case, j] = u0[case, j] - alpha[case] * m_win[case, j]

    planes(0, WINDOW, update)

    def image(j):
        for case in range(2):
            n = apply_plane(m_win, case, j, c0)
            s1[case, j] = n
            w1[case, j] = w0[case, j] - alpha[case] * n

    planes(1, WINDOW - 1, image)
    for case in range(2):
        n0[case] = s1[case, HALO : HALO + BLOCK]

    def term(case, k):
        j = HALO + k
        u, w = u1[case, j], w1[case, j]
        r = force[case, j] - alpha[case] * w0[case, j]
        return (r * u, w * u, u * w0[case, j] + u0[case, j] * w)

    rows = accumulate(3, term)
    tile = down(w1, c0, c1, s1, s2, t_ref, work, s2_out, s21_out, r1_out)
    finish_talk(talk, tile, rows, small)


def third_kernel(
    own, before, after, dots0, dots1, force, u0, w0, m0, n0, u1, w1, c0,
    u2, p1, x2, talk, m_win,
):
    lay_out(m_win, own, before, after, 2)
    gamma0, delta0 = dots0[2:3, :], dots0[3:4, :]
    gamma1 = dots1[2:3, :]
    beta = gamma1 / gamma0
    curve = dots1[3:4, :] + beta * dots1[4:5, :] + beta * beta * delta0
    a0 = [of_case(gamma0 / delta0, case) for case in range(2)]
    a1 = [of_case(gamma1 / curve, case) for case in range(2)]
    b1 = [of_case(beta, case) for case in range(2)]

    def update(i):
        j = i + 5
        for case in range(2):
            p = u1[case, j] + b1[case] * u0[case, j]
            p1[case, i] = p
            x2[case, i] = a0[case] * u0[case, j] + a1[case] * p
            u2[case, i] = u1[case, j] - a1[case] * (m_win[case, j] + b1[case] * m0[case, j])

    planes(0, 12, update)

    def term(case, k):
        j = HALO + k
        n1 = apply_plane(m_win, case, j, c0)
        s = w1[case, j] + b1[case] * w0[case, j]
        w = w1[case, j] - a1[case] * (n1 + b1[case] * n0[case, k])
        r = force[case, j] - a0[case] * w0[case, j] - a1[case] * s
        u, p = u2[case, k + 2], p1[case, k + 2]
        return (r * u, w * u, u * s + p * w)

    rows = accumulate(3, term)
    talk[...] = jnp.zeros_like(talk)
    for i, row in enumerate(rows):
        talk[:, i, :] = jnp.broadcast_to(row, (talk.shape[0], 128))


def last_kernel(gathered, dots0, dots1, u2, p1, x2, mod, free, state, energy, w_win):
    total = gathered[0]
    for d in range(1, gathered.shape[0]):
        total = total + gathered[d]
    gamma0, delta0 = dots0[2:3, :], dots0[3:4, :]
    gamma1 = dots1[2:3, :]
    beta1 = gamma1 / gamma0
    curve1 = dots1[3:4, :] + beta1 * dots1[4:5, :] + beta1 * beta1 * delta0
    gamma2 = total[0:1, :]
    beta2 = gamma2 / gamma1
    curve2 = total[1:2, :] + beta2 * total[2:3, :] + beta2 * beta2 * curve1
    a2 = [of_case(gamma2 / curve2, case) for case in range(2)]
    b2 = [of_case(beta2, case) for case in range(2)]

    def update(i):
        for case in range(2):
            x = x2[case, i] + a2[case] * (u2[case, i] + b2[case] * p1[case, i])
            w_win[case, i] = x

    planes(0, 12, update)
    for case in range(2):
        state[case] = w_win[case, 2:10]

    def hold(i):
        for case in range(2):
            w_win[case, i] = w_win[case, i] * free[i + 5]

    planes(0, 12, hold)
    lane, row = iota((NY, NX), 1), iota((NY, NX), 0)

    def power(i):
        m = mod[i + 6]
        out = jnp.zeros((NY, NX), F32)
        kx = jnp.where(lane > 0, jnp.sqrt(m * roll(m, 1, 1)), 0.0)
        ky = jnp.where(row > 0, jnp.sqrt(m * roll(m, 1, 0)), 0.0)
        kz, kn = jnp.sqrt(m * mod[i + 5]), jnp.sqrt(m * mod[i + 7])
        for case in range(2):
            v = w_win[case, i + 1]
            dx, dy = v - roll(v, 1, 1), v - roll(v, 1, 0)
            dz, dn = v - w_win[case, i], v - w_win[case, i + 2]
            px, py = kx * dx * dx, ky * dy * dy
            out = out + px + roll(px, -1, 1) + py + roll(py, -1, 0) + kz * dz * dz + kn * dn * dn
        energy[i] = out

    planes(0, 10, power)


def sensitivity_kernel(mine, other, scale, passive, out, g, cross, base):
    def gradient(i):
        value = scale[i] * (mine[i] + other[i])
        g[i] = value
        a, b = filter_parts(value)
        cross[i] = a
        base[i] = b

    planes(0, 10, gradient)

    def final(k):
        i = k + 1
        value = base[i] + 0.5 * (g[i - 1] + g[i + 1]) + EDGE_WEIGHT * (cross[i - 1] + cross[i + 1])
        out[k] = jnp.where(passive[k] == 0, value, 0.0)

    planes(0, 8, final)


def shape(*dims):
    return jax.ShapeDtypeStruct(dims, F32)


def call(body, outs, scratch, args, smem=0, name=None):
    vmem = pl.BlockSpec(memory_space=pltpu.VMEM)
    specs = [pl.BlockSpec(memory_space=pltpu.SMEM)] * smem + [vmem] * (len(args) - smem)
    return pl.pallas_call(
        body,
        out_shape=outs,
        in_specs=specs,
        out_specs=[vmem] * len(outs),
        scratch_shapes=[pltpu.VMEM(s, F32) for s in scratch],
        compiler_params=CPARAMS,
        name=name,
    )(*args)


def on_device(design, passive, fixed_mask, load_index):
    members = lax.axis_size("space")
    position = lax.axis_index("space")
    me = position.astype(jnp.int32).reshape(1)
    ahead = [(i, i + 1) for i in range(members - 1)]
    back = [(i + 1, i) for i in range(members - 1)]

    def both_ways(to_next, to_previous):
        return lax.ppermute(to_next, "space", ahead), lax.ppermute(to_previous, "space", back)

    def gather(tiles):
        return lax.all_to_all(tiles, "space", 0, 0)

    plane = (NY, NX)
    window = (2, WINDOW) + plane
    block = (2, BLOCK) + plane
    wide = (2, 12) + plane
    work = (800, 128)
    down_outs = [shape(*wide), shape(4, R1, 128), shape(Q1, R1, 128)]
    down_scratch = [window, window, (2, Q1) + plane, work, (Q1, R1, 128)]

    own = jnp.stack([design, passive.astype(F32), fixed_mask.astype(F32)])
    before, after = both_ways(own, own)
    counts = call(
        count_kernel, [shape(*window)], [(WINDOW * NY, 128)], (me, load_index), 1, "counts"
    )[0]
    c0, c1, force, s2, s21, r1, talk, mod, free, scale = call(
        functools.partial(setup_kernel, members),
        [shape(5, WINDOW, *plane), shape(5, Q1, R1, 128), shape(*window)]
        + down_outs
        + [shape(members, TALK, 128), shape(WINDOW, *plane), shape(WINDOW, *plane), shape(10, *plane)],
        [(24,) + plane] * 3 + down_scratch,
        (me, own, before, after, counts),
        1,
        "setup",
    )

    def up(first, r, talk, s2, s21, r1, coarse):
        s21_before, s21_after = both_ways(s21, s21)
        gathered = gather(talk)
        args = (me, gathered, r, s2, s21, s21_before, s21_after, r1, c0, c1) + tuple(coarse)
        outs = [shape(*block)]
        if first:
            outs += [shape(5, ND, R2, 128), shape(5, ND, R3, 128)]
        else:
            outs += [shape(8, 128)]
        scratch = [window, window, work, (ND, R2, 128)]
        return call(functools.partial(up_kernel, members, first), outs, scratch, args, 1, "up")

    u, c2, c3 = up(True, force, talk, s2, s21, r1, ())
    u_before, u_after = both_ways(u, u)
    u0, w0, s2, s21, r1, talk = call(
        first_kernel,
        [shape(*window), shape(*window)] + down_outs + [shape(members, R2, 128)],
        down_scratch,
        (u, u_before, u_after, force, c0, c1),
        name="first",
    )
    m, dots0 = up(False, w0, talk, s2, s21, r1, (c2, c3))
    m_before, m_after = both_ways(m, m)
    m0, u1, w1, n0, s2, s21, r1, talk = call(
        second_kernel,
        [shape(*window), shape(*window), shape(*window), shape(*block)] + down_outs + [shape(members, R2, 128)],
        down_scratch,
        (m, m_before, m_after, dots0, force, u0, w0, c0, c1),
        name="second",
    )
    m, dots1 = up(False, w1, talk, s2, s21, r1, (c2, c3))
    m_before, m_after = both_ways(m, m)
    u2, p1, x2, talk = call(
        third_kernel,
        [shape(*wide)] * 3 + [shape(members, 8, 128)],
        [window],
        (m, m_before, m_after, dots0, dots1, force, u0, w0, m0, n0, u1, w1, c0),
        name="third",
    )
    state, energy = call(
        last_kernel,
        [shape(*block), shape(10, *plane)],
        [wide],
        (gather(talk), dots0, dots1, u2, p1, x2, mod, free),
        name="last",
    )
    other = lax.ppermute(energy, "case", [(0, 1), (1, 0)])
    sensitivity = call(
        sensitivity_kernel,
        [shape(BLOCK, *plane)],
        [(10,) + plane] * 3,
        (energy, other, scale, passive),
        name="sensitivity",
    )[0]
    return state, sensitivity


def solution(mesh):
    placed = (
        P("space", None, None),
        P("space", None, None),
        P("space", None, None),
        P("case", None),
    )
    return jax.shard_map(
        on_device,
        mesh=mesh,
        in_specs=placed,
        out_specs=(P("case", "space", None, None), P("space", None, None)),
        check_vma=False,
    )
```

```python
import functools

import jax
import jax.numpy as jnp
from jax import lax
from jax.experimental import pallas as pl
from jax.experimental.pallas import tpu as pltpu
from jax.sharding import PartitionSpec as P

ITERS = 3
E_MIN = 0.01
OMEGA = 0.8
HEAT_SOURCE = 0.05
EDGE_WEIGHT = 1.5 - 2.0**0.5

F32 = jnp.float32
NY, NX = 40, 128
BLOCK = 8
HALO = 13
NEXT = HALO - BLOCK
WINDOW = BLOCK + 2 * HALO
Q1, R1 = 16, 24
QB = 6
REACH = 11
ND = 2 * REACH + 1
R2 = 16
R3 = 8
TALK = 24
CPARAMS = pltpu.CompilerParams(vmem_limit_bytes=32 * 1024 * 1024)


def iota(shape, dim):
    return lax.broadcasted_iota(jnp.int32, shape, dim)


def roll(v, by, dim):
    return pltpu.roll(v, by % v.shape[dim], dim)


def dot(a, b):
    return lax.dot_general(
        a, b, (((1,), (0,)), ((), ())), precision=lax.Precision.HIGHEST, preferred_element_type=F32
    )


def planes(lo, hi, body, group=8):
    def do(js):
        writes = [w for j in js for w in body(j)]
        for ref, index, value in writes:
            ref[index] = value

    count = (hi - lo) // group
    if count == 1:
        do([lo + k for k in range(group)])
    elif count > 1:

        def step(i, carry):
            do([lo + i * group + k for k in range(group)])
            return carry

        lax.fori_loop(0, count, step, 0)
    if lo + count * group < hi:
        do(list(range(lo + count * group, hi)))


def fine_to_half(case):
    i, j = iota((128, 128), 0), iota((128, 128), 1)
    return (j == 64 * case + (i >> 1)).astype(F32)


def half_to_fine(case):
    i, j = iota((128, 128), 0), iota((128, 128), 1)
    return (i == 64 * case + (j >> 1)).astype(F32)


def half_to_quarter(low):
    i, j = iota((128, 128), 0), iota((128, 128), 1)
    return (j == 64 * low + 32 * (i >> 6) + ((i & 63) >> 1)).astype(F32)


def quarter_to_half(low):
    i, j = iota((128, 128), 0), iota((128, 128), 1)
    return (i == 64 * low + 32 * (j >> 6) + ((j & 63) >> 1)).astype(F32)


def quarter_to_eighth():
    i, j = iota((128, 128), 0), iota((128, 128), 1)
    return (j == 16 * ((i >> 5) & 1) + ((i & 31) >> 1)).astype(F32)


def eighth_to_quarter():
    i, j = iota((128, 128), 0), iota((128, 128), 1)
    return (i == 16 * ((j >> 5) & 1) + ((j & 31) >> 1)).astype(F32)


def z_prev(v):
    return jnp.concatenate([jnp.zeros_like(v[:1]), v[:-1]], axis=0)


def z_next(v):
    return jnp.concatenate([v[1:], jnp.zeros_like(v[:1])], axis=0)


def z_prev2(v):
    turned = roll(v, 64, 2)
    return jnp.where(iota(v.shape, 2) >= 64, turned, z_prev(turned))


def z_next2(v):
    turned = roll(v, 64, 2)
    return jnp.where(iota(v.shape, 2) < 64, turned, z_next(turned))


def couple(m, f, factor, width, zp, zn):
    lead = (iota(m.shape, 2) & (width - 1)) > 0
    first = iota(m.shape, 1) > 0
    sides = (
        (lambda v: roll(v, 1, 2), lambda v: roll(v, -1, 2), lead),
        (lambda v: roll(v, 1, 1), lambda v: roll(v, -1, 1), first),
        (zp, zn, None),
    )
    total = jnp.zeros_like(m)
    held = jnp.zeros_like(m)
    coupling = []
    for prev, after, mask in sides:
        k = jnp.sqrt(m * prev(m))
        if mask is not None:
            k = jnp.where(mask, k, 0.0)
        ka = after(k)
        total = total + k + ka
        held = held + k * (1.0 - prev(f)) + ka * (1.0 - after(f))
        inner = factor * k * f * prev(f)
        coupling += [inner, after(inner)]
    rest = f * factor * held + (1.0 - f)
    weight = OMEGA / (f * factor * total + (1.0 - f))
    return tuple(coupling) + (rest, weight)


COUNT = 8
REST, WEIGHT = 6, 7


def apply(v, c, zp, zn):
    out = c[REST] * v + c[0] * (v - roll(v, 1, 2)) + c[1] * (v - roll(v, -1, 2))
    out = out + c[2] * (v - roll(v, 1, 1)) + c[3] * (v - roll(v, -1, 1))
    return out + c[4] * (v - zp(v)) + c[5] * (v - zn(v))


def cut(c, lo, hi):
    return tuple(x[lo:hi] for x in c)


COUNT0 = 7
Z0, REST0, WEIGHT0 = 4, 5, 6


def apply_plane(v_ref, case, i, c_ref, j):
    v = v_ref[case, i]
    out = c_ref[REST0, j] * v + c_ref[0, j] * (v - roll(v, 1, 1)) + c_ref[1, j] * (v - roll(v, -1, 1))
    out = out + c_ref[2, j] * (v - roll(v, 1, 0)) + c_ref[3, j] * (v - roll(v, -1, 0))
    return out + c_ref[Z0, j] * (v - v_ref[case, i - 1]) + c_ref[Z0, j + 1] * (v - v_ref[case, i + 1])


def copy_in(source, target, sem):
    copy = pltpu.make_async_copy(source, target, sem)
    copy.start()
    return copy


def pairs_of_rows(v, scratch):
    n, rows, _ = v.shape
    scratch[: n * rows, :] = v.reshape(n * rows, 128)
    half = n * rows // 2
    even = scratch[pl.ds(0, half, stride=2), :]
    odd = scratch[pl.ds(1, half, stride=2), :]
    return (even + odd).reshape(n, rows // 2, 128)


def put_rows_twice(v, scratch):
    n, rows, _ = v.shape
    flat = v.reshape(n * rows, 128)
    scratch[pl.ds(0, n * rows, stride=2), :] = flat
    scratch[pl.ds(1, n * rows, stride=2), :] = flat


def rows_twice(v, scratch):
    n, rows, _ = v.shape
    put_rows_twice(v, scratch)
    return scratch[: 2 * n * rows, :].reshape(n, 2 * rows, 128)


def flat_dot(v, matrix):
    n, rows, _ = v.shape
    return dot(v.reshape(n * rows, 128), matrix).reshape(n, rows, 128)


def fine_to_level1(t_ref, r_ref, work, count, split):
    flat0 = t_ref[0, :count].reshape(count * NY, 128)
    flat1 = t_ref[1, :count].reshape(count * NY, 128)
    work[: count * NY, :] = dot(flat0, fine_to_half(0)) + dot(flat1, fine_to_half(1))
    r_ref[...] = jnp.zeros_like(r_ref)
    for p in range(count):
        even = work[pl.ds(p * NY, NY // 2, stride=2), :]
        odd = work[pl.ds(p * NY + 1, NY // 2, stride=2), :]
        r_ref[split + p, 0 : NY // 2, :] = even + odd


def down(r_ref, c0, c1, s1, s2, t_ref, work, s2_hbm, sem, reach, rows, s21_out, r1_out, talk):
    trim = 4 - reach
    t = trim // 2

    def first(j):
        return [(s1, (case, j), c0[WEIGHT0, j] * r_ref[case, j]) for case in range(2)]

    planes(1 + trim, WINDOW - 1 - trim, first)

    def second(j):
        return [
            (s2, (case, j), s1[case, j] + c0[WEIGHT0, j] * (r_ref[case, j] - apply_plane(s1, case, j, c0, j)))
            for case in range(2)
        ]

    planes(2 + trim, WINDOW - 2 - trim, second)
    copy = copy_in(s2.at[:, HALO - reach : HALO + BLOCK + reach], s2_hbm, sem)
    count = Q1 - 2 - 2 * t

    def third(p):
        a = 2 * (p + 1 + t) + 1
        return [
            (
                t_ref,
                (case, p),
                (r_ref[case, a] - apply_plane(s2, case, a, c0, a))
                + (r_ref[case, a + 1] - apply_plane(s2, case, a + 1, c0, a + 1)),
            )
            for case in range(2)
        ]

    planes(0, count, third, 4)
    fine_to_level1(t_ref, r1_out, work, count, 1 + t)

    c = tuple(c1[k] for k in range(COUNT))
    lo, hi = 1 + t, Q1 - 1 - t
    forcing = r1_out[lo:hi]
    smoothed = c[WEIGHT][lo:hi] * forcing
    leftover = forcing - apply(smoothed, cut(c, lo, hi), z_prev, z_next)
    relaxed = (smoothed + c[WEIGHT][lo:hi] * leftover)[1:-1]
    s21_out[...] = relaxed
    lo, hi = QB - 1, QB + 5
    inner = relaxed[lo - 2 - t : hi - 2 - t]
    rest = (r1_out[lo:hi] - apply(inner, cut(c, lo, hi), z_prev, z_next))[1:5]
    low, high = rest[0] + rest[1], rest[2] + rest[3]
    mixed = dot(low, half_to_quarter(0)) + dot(high, half_to_quarter(1))
    summed = pairs_of_rows(mixed[None], work)[0]
    work[0:12, :] = summed
    at = 10
    for row in rows:
        work[at : at + row.shape[0], :] = row
        at += row.shape[0]
    tile = work[0 : talk.shape[1], :]
    talk[...] = jnp.broadcast_to(tile[None], talk.shape)
    return copy


def count_kernel(me, index, out, acc):
    base = (me[0] * BLOCK - HALO) * NY
    rows = WINDOW * NY
    chunk = 512
    total = index.shape[1]
    for case in range(2):
        acc[...] = jnp.zeros_like(acc)

        def step(i, carry):
            ids = index[pl.ds(case, 1), pl.ds(pl.multiple_of(i * chunk, chunk), chunk)]
            row = (ids >> 7) - base
            col = ids & 127
            hit_row = jnp.where(iota((rows, chunk), 0) == row, 1.0, 0.0).astype(jnp.bfloat16)
            hit_col = jnp.where(iota((128, chunk), 0) == col, 1.0, 0.0).astype(jnp.bfloat16)
            acc[...] += lax.dot_general(
                hit_row, hit_col, (((1,), (1,)), ((), ())), preferred_element_type=F32
            )
            return carry

        lax.fori_loop(0, total // chunk, step, 0)
        out[case] = acc[...].reshape(WINDOW, NY, 128)


def neighbours_x(p):
    lane = iota(p.shape, 1)
    return jnp.where(lane > 0, roll(p, 1, 1), 0.0) + jnp.where(lane < NX - 1, roll(p, -1, 1), 0.0)


def neighbours_y(p):
    row = iota(p.shape, 0)
    return jnp.where(row > 0, roll(p, 1, 0), 0.0) + jnp.where(row < NY - 1, roll(p, -1, 0), 0.0)


def filter_parts(p):
    sides_y = neighbours_y(p)
    cross = neighbours_x(p) + sides_y
    return cross, 1.5 * p + 0.5 * cross + EDGE_WEIGHT * neighbours_x(sides_y)


def weight_of(me, members, z):
    at = me * BLOCK + z
    lane, row = iota((NY, NX), 1), iota((NY, NX), 0)
    nx = (lane > 0).astype(F32) + (lane < NX - 1).astype(F32)
    ny = (row > 0).astype(F32) + (row < NY - 1).astype(F32)
    nz = jnp.where(at > 0, 1.0, 0.0) + jnp.where(at < members * BLOCK - 1, 1.0, 0.0)
    return 1.5 + 0.5 * (nx + ny + nz) + EDGE_WEIGHT * (nx * ny + nx * nz + ny * nz)


NEAR, AWAY = 3 * BLOCK, 3 * NEXT + 1


def collect_kernel(case_ref, design, passive, fixed, own, near, head, tail, all_head, all_tail):
    at = 0
    for k, source in enumerate((design, passive, fixed)):
        value = source[...].astype(F32)
        own[k * BLOCK : (k + 1) * BLOCK] = value
        count = NEXT + 1 if k == 0 else NEXT
        all_head[at : at + count] = value[0:count]
        all_tail[at : at + count] = value[BLOCK - count : BLOCK]
        at += count
    case = case_ref[0]
    near[...] = own[pl.ds(case * (NEAR // 2), NEAR // 2)]
    head[...] = all_head[pl.ds(case * (AWAY // 2), AWAY // 2)]
    tail[...] = all_tail[pl.ds(case * (AWAY // 2), AWAY // 2)]


def setup_kernel(
    members, me_ref, case_ref, own, before, after, before2, after2, o_before, o_after, o_before2, o_after2, counts,
    c0_hbm, c1_hbm, force_hbm, s2_hbm, s21, r1_out, talk, mod_hbm, free_hbm, scale_hbm,
    near_b, near_a, away_b, away_a,
    raw, cross, base, c0, c1, force, mod, free, scale, s1, s2, t_ref, work, small, sems,
):
    me, case = me_ref[0], case_ref[0]
    halves = (
        (near_b, before, o_before),
        (near_a, after, o_after),
        (away_b, before2, o_before2),
        (away_a, after2, o_after2),
    )
    for target, mine, other in halves:
        half = mine.shape[0]
        target[pl.ds(case * half, half)] = mine[...]
        target[pl.ds((1 - case) * half, half)] = other[...]
    start = 0
    for source, count in ((away_b, NEXT + 1), (near_b, BLOCK), (own, BLOCK), (near_a, BLOCK), (away_a, NEXT + 1)):
        raw[start : start + count] = source[0:count]
        start += count

    def parts(k):
        a, b = filter_parts(raw[k])
        return [(cross, (k,), a), (base, (k,), b)]

    planes(0, WINDOW + 2, parts, 6)

    def material(j, passive, fixed, near):
        z = j - HALO
        at = me * BLOCK + z
        inside = jnp.where((at >= 0) & (at < members * BLOCK), 1.0, 0.0)
        filtered = base[j + 1] + 0.5 * (raw[j] + raw[j + 2]) + EDGE_WEIGHT * (cross[j] + cross[j + 2])
        weight = weight_of(me, members, z)
        density = jnp.where(passive == 1.0, 1.0, jnp.where(passive == 2.0, 0.0, filtered / weight))
        modulus = E_MIN + (1.0 - E_MIN) * density * density * density
        freedom = inside * (1.0 - fixed)
        writes = [(mod, (j,), inside * modulus), (free, (j,), freedom)]
        writes += [(force, (case, j), freedom * (HEAT_SOURCE + counts[case, j])) for case in range(2)]
        if near:
            gradient = (-1.5 * (1.0 - E_MIN)) * density * density / (modulus * weight)
            gradient = jnp.where(passive == 0.0, inside * gradient, 0.0)
            writes.append((scale, (j - HALO + 1,), gradient))
        return writes

    def stretch(source, first, second, j0, lo, hi, near=False):
        planes(lo, hi, lambda j: material(j, source[first + j - j0], source[second + j - j0], near), 5)

    stretch(away_b, NEXT + 1, 2 * NEXT + 1, 0, 0, NEXT)
    stretch(near_b, BLOCK, 2 * BLOCK, NEXT, NEXT, HALO - 1)
    stretch(near_b, BLOCK, 2 * BLOCK, NEXT, HALO - 1, HALO, True)
    stretch(own, BLOCK, 2 * BLOCK, HALO, HALO, HALO + BLOCK, True)
    stretch(near_a, BLOCK, 2 * BLOCK, HALO + BLOCK, HALO + BLOCK, HALO + BLOCK + 1, True)
    stretch(near_a, BLOCK, 2 * BLOCK, HALO + BLOCK, HALO + BLOCK + 1, HALO + 2 * BLOCK)
    stretch(away_a, NEXT + 1, 2 * NEXT + 1, HALO + 2 * BLOCK, HALO + 2 * BLOCK, WINDOW)
    near = slice(HALO - 2, HALO + BLOCK + 2)
    copies = [
        copy_in(force, force_hbm, sems.at[0]),
        copy_in(mod.at[near], mod_hbm, sems.at[1]),
        copy_in(free.at[near], free_hbm, sems.at[2]),
        copy_in(scale, scale_hbm, sems.at[3]),
    ]

    lane, row = iota((NY, NX), 1), iota((NY, NX), 0)
    zero = jnp.zeros((NY, NX), F32)

    def coefficients(j):
        m, f = mod[j], free[j]
        total, held = zero, zero
        writes = []
        for dim, mask, slot in ((1, lane > 0, 0), (0, row > 0, 2)):
            k = jnp.where(mask, jnp.sqrt(m * roll(m, 1, dim)), 0.0)
            ka = roll(k, -1, dim)
            fp = roll(f, 1, dim)
            total = total + k + ka
            held = held + k * (1.0 - fp) + ka * (1.0 - roll(f, -1, dim))
            inner = k * f * fp
            writes += [(c0, (slot, j), inner), (c0, (slot + 1, j), roll(inner, -1, dim))]
        k, ka = jnp.sqrt(m * mod[j - 1]), jnp.sqrt(m * mod[j + 1])
        total = total + k + ka
        held = held + k * (1.0 - free[j - 1]) + ka * (1.0 - free[j + 1])
        writes.append((c0, (Z0, j), k * f * free[j - 1]))
        writes.append((c0, (REST0, j), f * held + (1.0 - f)))
        writes.append((c0, (WEIGHT0, j), OMEGA / (f * total + (1.0 - f))))
        return writes

    planes(1, WINDOW - 1, coefficients, 4)
    last = WINDOW - 1
    for slot in range(COUNT0):
        c0[slot, 0] = zero
        c0[slot, last] = zero
    c0[Z0, last] = jnp.sqrt(mod[last] * mod[last - 1]) * free[last] * free[last - 1]
    copies.append(copy_in(c0, c0_hbm, sems.at[4]))

    def join(q):
        return [(t_ref, (k, q), x[2 * q + 1] + x[2 * q + 2]) for k, x in enumerate((mod, free))]

    planes(0, Q1, join)
    fine_to_level1(t_ref, small, work, Q1, 0)
    both = small[...]
    second = iota(both.shape, 2) >= 64
    both = jnp.where(second, (both > 0.0).astype(F32), 0.125 * both)
    turned = roll(both, 64, 2)
    m1 = jnp.where(second, turned, both)
    f1 = jnp.where(second, both, turned)
    for k, value in enumerate(couple(m1, f1, 2.0, 64, z_prev, z_next)):
        c1[k] = value
    copies.append(copy_in(c1, c1_hbm, sems.at[5]))

    low, high = both[QB] + both[QB + 1], both[QB + 2] + both[QB + 3]
    mixed = dot(low, half_to_quarter(0)) + dot(high, half_to_quarter(1))
    coarse = pairs_of_rows(mixed[None], work)[0]
    is_free = (iota(coarse.shape, 1) & 32) > 0
    coarse = jnp.where(is_free, (coarse > 0.0).astype(F32), 0.125 * coarse)

    rows = (coarse, jnp.zeros((2, 128), F32))
    copies.append(down(force, c0, c1, s1, s2, t_ref, work, s2_hbm, sems.at[6], 2, rows, s21, r1_out, talk))
    for copy in copies:
        copy.wait()


def coarse_window(me, gathered, lo, hi):
    members = gathered.shape[0]
    tiles = []
    for d in range(ND):
        at = me + d - REACH
        inside = jnp.where((at >= 0) & (at < members), 1.0, 0.0)
        tiles.append(inside * gathered[jnp.clip(at, 0, members - 1), lo:hi, :])
    return jnp.stack(tiles, axis=0)


def coarse_setup(me, gathered, c2, c3, work, wide):
    wide[...] = jnp.zeros_like(wide)
    wide[:, 0:10, :] = coarse_window(me, gathered, 10, 20)
    both = wide[...]
    is_free = (iota(both.shape, 2) & 32) > 0
    m = jnp.where(is_free, roll(both, 32, 2), both)
    f = jnp.where(is_free, both, roll(both, -32, 2))
    for k, value in enumerate(couple(m, f, 4.0, 32, z_prev2, z_next2)):
        c2[k] = value
    eighth = quarter_to_eighth()
    m3 = 0.125 * pairs_of_rows(flat_dot(m, eighth), work)
    f3 = (pairs_of_rows(flat_dot(f, eighth), work) > 0.0).astype(F32)
    for k, value in enumerate(couple(m3, f3, 8.0, 16, z_prev, z_next)):
        c3[k] = value


def coarse_solve(r2, c2, c3, work):
    c = tuple(c2[k] for k in range(COUNT))
    smoothed = c[WEIGHT] * r2
    relaxed = smoothed + c[WEIGHT] * (r2 - apply(smoothed, c, z_prev2, z_next2))
    leftover = (r2 - apply(relaxed, c, z_prev2, z_next2))[2 : ND - 2]
    forcing = pairs_of_rows(flat_dot(leftover, quarter_to_eighth()), work)
    lo, hi = 2, ND - 2
    v = c3[WEIGHT, lo:hi] * forcing
    for _ in range(7):
        ck = tuple(c3[k, lo:hi] for k in range(COUNT))
        v = v + ck[WEIGHT] * (forcing - apply(v, ck, z_prev, z_next))
        v, forcing = v[1:-1], forcing[1:-1]
        lo, hi = lo + 1, hi - 1
    up = rows_twice(flat_dot(v, eighth_to_quarter()), work)
    lo, hi = REACH - 2, REACH + 3
    v = relaxed[lo:hi] + up
    ck = cut(c, lo, hi)
    for _ in range(2):
        v = v + ck[WEIGHT] * (r2[lo:hi] - apply(v, ck, z_prev2, z_next2))
    return v[1:4]


def level1_up(e2, relaxed, forcing, c, work):
    parts = []
    for low in range(2):
        lanes = flat_dot(e2, quarter_to_half(low))
        parts.append(rows_twice(lanes, work)[:, :R1])
    lifted = [parts[z & 1][z >> 1] for z in range(6)]
    n = relaxed.shape[0]
    lead = (12 - n) // 2
    v = relaxed + jnp.stack([lifted[(q + lead) // 2] for q in range(n)], axis=0)
    for _ in range(2):
        v = (v + c[WEIGHT] * (forcing - apply(v, c, z_prev, z_next)))[1:-1]
        forcing, c = forcing[1:-1], cut(c, 1, -1)
    return v


def level0_up(v1, s2, r, vb, c0, out, work):
    count = v1.shape[0]
    for case in range(2):
        lanes = flat_dot(v1, half_to_fine(case))
        put_rows_twice(lanes, work)
        for p in range(count):
            fine = work[p * 2 * R1 : p * 2 * R1 + NY, :]
            s2[case, 2 * p] = s2[case, 2 * p] + fine
            s2[case, 2 * p + 1] = s2[case, 2 * p + 1] + fine
    total = s2.shape[1]

    def sweep(v, case, i):
        return v[case, i] + c0[WEIGHT0, i] * (r[case, i - 1] - apply_plane(v, case, i, c0, i))

    def once(i):
        return [(vb, (case, i), sweep(s2, case, i)) for case in range(2)]

    planes(1, total - 1, once, 7 if total == 16 else 5)

    def twice(i):
        return [(out, (case, i - 2), sweep(vb, case, i)) for case in range(2)]

    planes(2, total - 2, twice, 6 if total == 16 else 8)


def add_up(parts):
    while len(parts) > 1:
        parts = [sum(parts[i : i + 2][1:], parts[i]) for i in range(0, len(parts), 2)]
    return parts[0]


def sum_of_rows(gathered, lo, hi):
    return add_up([gathered[d, lo:hi, :] for d in range(gathered.shape[0])])


def residual_window(me, gathered):
    r2 = coarse_window(me, gathered, 0, 16)
    return jnp.where(iota(r2.shape, 1) < 10, r2, 0.0)


def around(reach):
    return slice(HALO - reach, HALO + BLOCK + reach)


def up_kernel(first, me_ref, gathered, r_hbm, s2_hbm, s21, r1_ref, c0_hbm, c1_hbm, *rest):
    if first:
        out, head, tail, c2, c3, s2, r, c0, c1, vb, work, wide, sems = rest
    else:
        c2, c3, out, head, tail, dots, s2, r, c0, c1, vb, work, wide, sems = rest
    sources = (
        (s2_hbm, s2),
        (r_hbm.at[:, around(1)], r),
        (c0_hbm.at[:, around(2)], c0),
        (c1_hbm.at[:, 3:13], c1),
    )
    copies = [copy_in(a, b, sems.at[i]) for i, (a, b) in enumerate(sources)]
    me = me_ref[0]
    if first:
        coarse_setup(me, gathered, c2, c3, work, wide)
    else:
        dots[...] = sum_of_rows(gathered, 8, 16)
    e2 = coarse_solve(residual_window(me, gathered), c2, c3, work)
    for copy in copies:
        copy.wait()
    v1 = level1_up(e2, s21[...], r1_ref[3:13], tuple(c1[k] for k in range(COUNT)), work)

    level0_up(v1, s2, r, vb, c0, out, work)
    for case in range(2):
        head[case] = out[case, 0:NEXT]
        tail[case] = out[case, BLOCK - NEXT : BLOCK]


def lay_out(win, own, before, after, before2, after2):
    start = 0
    for source in (before2, before, own, after, after2):
        count = source.shape[1]
        for case in range(2):
            win[case, start : start + count] = source[case]
        start += count


def dot_rows(values):
    lane = iota((1, 128), 1)
    rows = []
    for a, b in values:
        rows.append(jnp.where(lane < 64, jnp.sum(a, keepdims=True), jnp.sum(b, keepdims=True)))
    return rows


def accumulate(count, term):
    sums = []
    for case in range(2):
        terms = [term(case, k) for k in range(BLOCK)]
        sums.append([add_up([t[i] for t in terms]) for i in range(count)])
    return dot_rows([(sums[0][i], sums[1][i]) for i in range(count)])


def first_kernel(
    own, before, after, before2, after2, force_hbm, c0, c1,
    u_hbm, w_hbm, s2_hbm, s21, r1_out, talk,
    u_win, w_win, force, s1, s2, t_ref, work, sems,
):
    copy_f = copy_in(force_hbm.at[:, around(0)], force, sems.at[0])
    lay_out(u_win, own, before, after, before2, after2)
    copies = [copy_in(u_win.at[:, around(2)], u_hbm, sems.at[1])]

    def image(j):
        return [(w_win, (case, j), apply_plane(u_win, case, j, c0, j)) for case in range(2)]

    planes(1, WINDOW - 1, image)
    copies.append(copy_in(w_win, w_hbm, sems.at[2]))
    copy_f.wait()

    def term(case, k):
        u = own[case, k]
        return (force[case, k] * u, w_win[case, HALO + k] * u)

    rows = accumulate(2, term) + [jnp.zeros((4, 128), F32)]
    copies.append(down(w_win, c0, c1, s1, s2, t_ref, work, s2_hbm, sems.at[3], 2, rows, s21, r1_out, talk))
    for copy in copies:
        copy.wait()


def of_case(row, case):
    return row[:, 64 * case : 64 * case + 1]


def second_kernel(
    own, before, after, before2, after2, dots0, force_hbm, u0_hbm, w0_hbm, c0, c1,
    m_hbm, u1_hbm, w1_hbm, n0_hbm, s2_hbm, s21, r1_out, talk,
    m_win, u0, w0, n0, u1, w1, force, s1, s2, t_ref, work, sems,
):
    copy_w = copy_in(w0_hbm, w0, sems.at[0])
    copy_u = copy_in(u0_hbm, u0, sems.at[1])
    copy_f = copy_in(force_hbm.at[:, around(0)], force, sems.at[2])
    lay_out(m_win, own, before, after, before2, after2)
    copies = [copy_in(m_win.at[:, around(2)], m_hbm, sems.at[3])]
    alpha = [of_case(dots0[2:3, :] / dots0[3:4, :], case) for case in range(2)]
    copy_w.wait()

    def image(j, block=False):
        writes = []
        for case in range(2):
            n = apply_plane(m_win, case, j, c0, j)
            writes.append((w1, (case, j), w0[case, j] - alpha[case] * n))
            if block:
                writes.append((n0, (case, j - HALO), n))
        return writes

    planes(1, HALO, image, 6)
    planes(HALO, HALO + BLOCK, functools.partial(image, block=True))
    planes(HALO + BLOCK, WINDOW - 1, image, 6)
    copies.append(copy_in(n0, n0_hbm, sems.at[4]))
    copies.append(copy_in(w1, w1_hbm, sems.at[5]))
    copy_u.wait()

    def update(i):
        return [(u1, (case, i), u0[case, i] - alpha[case] * m_win[case, i + HALO - 2]) for case in range(2)]

    planes(0, BLOCK + 4, update)
    copies.append(copy_in(u1, u1_hbm, sems.at[6]))
    copy_f.wait()

    def term(case, k):
        j = HALO + k
        u, w, ww = u1[case, k + 2], w1[case, j], w0[case, j]
        r = force[case, k] - alpha[case] * ww
        return (r * u, w * u, u * ww + u0[case, k + 2] * w)

    rows = accumulate(3, term) + [jnp.zeros((3, 128), F32)]
    copies.append(down(w1, c0, c1, s1, s2, t_ref, work, s2_hbm, sems.at[7], 4, rows, s21, r1_out, talk))
    for copy in copies:
        copy.wait()


def third_kernel(
    me_ref, gathered, dots0, s21, r1_ref, c0_hbm, c1_hbm, c2, c3,
    w1_hbm, s2_hbm, force_hbm, u0_hbm, w0_hbm, m0_hbm, n0_hbm, u1_hbm,
    u2, p1, x2, talk, dots1,
    s2, w1, vb, m_win, force, u0, w0, m0, n0, u1, c0, c1, work, sems,
):
    sources = (
        (c1_hbm.at[:, 2:14], c1),
        (s2_hbm, s2),
        (c0_hbm.at[:, around(4)], c0),
        (w1_hbm.at[:, around(3)], w1),
        (force_hbm.at[:, around(0)], force),
        (u0_hbm, u0),
        (w0_hbm.at[:, around(0)], w0),
        (m0_hbm, m0),
        (n0_hbm, n0),
        (u1_hbm, u1),
    )
    copies = [copy_in(a, b, sems.at[i]) for i, (a, b) in enumerate(sources)]
    dots1[...] = sum_of_rows(gathered, 8, 16)
    e2 = coarse_solve(residual_window(me_ref[0], gathered), c2, c3, work)
    copies[0].wait()
    v1 = level1_up(e2, s21[...], r1_ref[2:14], tuple(c1[k] for k in range(COUNT)), work)

    for copy in copies[1:]:
        copy.wait()
    level0_up(v1, s2, w1, vb, c0, m_win, work)

    gamma0, delta0 = dots0[2:3, :], dots0[3:4, :]
    gamma1 = dots1[2:3, :]
    beta = gamma1 / gamma0
    curve = dots1[3:4, :] + beta * dots1[4:5, :] + beta * beta * delta0
    a0 = [of_case(gamma0 / delta0, case) for case in range(2)]
    a1 = [of_case(gamma1 / curve, case) for case in range(2)]
    b1 = [of_case(beta, case) for case in range(2)]

    def update(i):
        writes = []
        for case in range(2):
            p = u1[case, i] + b1[case] * u0[case, i]
            writes.append((p1, (case, i), p))
            writes.append((x2, (case, i), a0[case] * u0[case, i] + a1[case] * p))
            u = u1[case, i] - a1[case] * (m_win[case, i] + b1[case] * m0[case, i])
            writes.append((u2, (case, i), u))
        return writes

    planes(0, 12, update)

    def term(case, k):
        n1 = apply_plane(m_win, case, k + 2, c0, k + 4)
        ww, wv = w0[case, k], w1[case, k + 3]
        s = wv + b1[case] * ww
        w = wv - a1[case] * (n1 + b1[case] * n0[case, k])
        r = force[case, k] - a0[case] * ww - a1[case] * s
        u, p = u2[case, k + 2], p1[case, k + 2]
        return (r * u, w * u, u * s + p * w)

    rows = accumulate(3, term) + [jnp.zeros((5, 128), F32)]
    tile = jnp.concatenate(rows, axis=0)
    talk[...] = jnp.broadcast_to(tile[None], talk.shape)


def last_kernel(gathered, dots0, dots1, u2, p1, x2, mod, free, state, energy, w_win):
    total = add_up([gathered[d] for d in range(gathered.shape[0])])
    gamma0, delta0 = dots0[2:3, :], dots0[3:4, :]
    gamma1 = dots1[2:3, :]
    beta1 = gamma1 / gamma0
    curve1 = dots1[3:4, :] + beta1 * dots1[4:5, :] + beta1 * beta1 * delta0
    gamma2 = total[0:1, :]
    beta2 = gamma2 / gamma1
    curve2 = total[1:2, :] + beta2 * total[2:3, :] + beta2 * beta2 * curve1
    a2 = [of_case(gamma2 / curve2, case) for case in range(2)]
    b2 = [of_case(beta2, case) for case in range(2)]

    def update(i):
        return [
            (w_win, (case, i), x2[case, i] + a2[case] * (u2[case, i] + b2[case] * p1[case, i])) for case in range(2)
        ]

    planes(0, 12, update, 4)
    state[...] = w_win[:, 2:10]

    def hold(i):
        return [(w_win, (case, i), w_win[case, i] * free[i]) for case in range(2)]

    planes(0, 12, hold, 4)
    lane, row = iota((NY, NX), 1), iota((NY, NX), 0)

    def power(i):
        m = mod[i + 1]
        out = jnp.zeros((NY, NX), F32)
        kx = jnp.where(lane > 0, jnp.sqrt(m * roll(m, 1, 1)), 0.0)
        ky = jnp.where(row > 0, jnp.sqrt(m * roll(m, 1, 0)), 0.0)
        kz, kn = jnp.sqrt(m * mod[i]), jnp.sqrt(m * mod[i + 2])
        for case in range(2):
            v = w_win[case, i + 1]
            dx, dy = v - roll(v, 1, 1), v - roll(v, 1, 0)
            dz, dn = v - w_win[case, i], v - w_win[case, i + 2]
            px, py = kx * dx * dx, ky * dy * dy
            out = out + px + roll(px, -1, 1) + py + roll(py, -1, 0) + kz * dz * dz + kn * dn * dn
        return [(energy, (i,), out)]

    planes(0, 10, power, 5)


def sensitivity_kernel(mine, other, scale, passive, out, g, cross, base):
    def gradient(i):
        value = scale[i] * (mine[i] + other[i])
        a, b = filter_parts(value)
        return [(g, (i,), value), (cross, (i,), a), (base, (i,), b)]

    planes(0, 10, gradient, 5)

    def final(k):
        i = k + 1
        value = base[i] + 0.5 * (g[i - 1] + g[i + 1]) + EDGE_WEIGHT * (cross[i - 1] + cross[i + 1])
        return [(out, (k,), jnp.where(passive[k] == 0, value, 0.0))]

    planes(0, 8, final)


def shape(*dims):
    return jax.ShapeDtypeStruct(dims, F32)


def hbm(*dims):
    return pltpu.HBM(dims, F32), pltpu.HBM


def vmem(*dims):
    return shape(*dims), pltpu.VMEM


def call(body, outs, scratch, args, name, sems=0, cost=None):
    pairs = [a if isinstance(a, tuple) else (a, pltpu.VMEM) for a in args]
    scratches = [pltpu.VMEM(s, F32) for s in scratch]
    if sems:
        scratches.append(pltpu.SemaphoreType.DMA((sems,)))
    given = [pltpu.with_memory_space_constraint(a, m) if m is pltpu.HBM else a for a, m in pairs]
    return pl.pallas_call(
        body,
        out_shape=[o for o, _ in outs],
        in_specs=[pl.BlockSpec(memory_space=m) for _, m in pairs],
        out_specs=[pl.BlockSpec(memory_space=m) for _, m in outs],
        scratch_shapes=scratches,
        compiler_params=CPARAMS,
        cost_estimate=cost,
        name=name,
    )(*given)


def on_device(design, passive, fixed_mask, load_index):
    members = lax.axis_size("space")
    position = lax.axis_index("space")
    me = position.astype(jnp.int32).reshape(1)
    ahead = [(i, i + 1) for i in range(members - 1)]
    back = [(i + 1, i) for i in range(members - 1)]

    def two_either_side(own, head, tail):
        skip = [(i, i + 2) for i in range(members - 2)]
        skip_back = [(i + 2, i) for i in range(members - 2)]
        return (
            lax.ppermute(own, "space", ahead),
            lax.ppermute(own, "space", back),
            lax.ppermute(tail, "space", skip),
            lax.ppermute(head, "space", skip_back),
        )

    def gather(tiles):
        return lax.all_to_all(tiles, "space", 0, 0)

    plane = (NY, NX)
    window = (2, WINDOW) + plane
    block = (2, BLOCK) + plane
    wide = (2, BLOCK + 4) + plane
    wider = (2, BLOCK + 8) + plane
    work = (800, 128)
    t_shape = (2, Q1) + plane
    position_ref = (me, pltpu.SMEM)

    def down_outs(reach, count):
        near = 2 + reach // 2
        return [
            hbm(2, BLOCK + 2 * reach, *plane),
            vmem(4 + 2 * near, R1, 128),
            vmem(Q1, R1, 128),
            vmem(members, count, 128),
        ]

    def far(x):
        return (x, pltpu.HBM)

    case_ref = (lax.axis_index("case").astype(jnp.int32).reshape(1), pltpu.SMEM)
    own, near, head, tail = call(
        collect_kernel,
        [vmem(NEAR, *plane), vmem(NEAR // 2, *plane), vmem(AWAY // 2, *plane), vmem(AWAY // 2, *plane)],
        [(AWAY,) + plane] * 2,
        (case_ref, design, passive, fixed_mask),
        "collect",
    )
    listened = two_either_side(near, head, tail)
    listened += tuple(lax.ppermute(x, "case", [(0, 1), (1, 0)]) for x in listened)
    counts = call(
        count_kernel,
        [vmem(*window)],
        [(WINDOW * NY, 128)],
        (position_ref, load_index),
        "counts",
        cost=pl.CostEstimate(flops=3 * 10**10, bytes_accessed=10**7, transcendentals=0),
    )[0]
    c0, c1, force, s2, s21, r1, talk, mod, free, scale = call(
        functools.partial(setup_kernel, members),
        [hbm(COUNT0, WINDOW, *plane), hbm(COUNT, Q1, R1, 128), hbm(*window)]
        + down_outs(2, TALK)
        + [hbm(12, *plane), hbm(12, *plane), hbm(10, *plane)],
        [(NEAR,) + plane] * 2
        + [(AWAY,) + plane] * 2
        + [(WINDOW + 2,) + plane] * 3
        + [(COUNT0, WINDOW) + plane, (COUNT, Q1, R1, 128)]
        + [window, (WINDOW,) + plane, (WINDOW,) + plane, (10,) + plane, window, window, t_shape, work]
        + [(Q1, R1, 128)],
        (position_ref, case_ref, own) + listened + (counts,),
        "setup",
        7,
    )

    def up(first, r, s2, s21, r1, talk, more):
        args = (position_ref, gather(talk), far(r), far(s2), s21, r1, far(c0), far(c1)) + tuple(more)
        outs = [vmem(*block), vmem(2, NEXT, *plane), vmem(2, NEXT, *plane)]
        if first:
            outs += [vmem(COUNT, ND, R2, 128), vmem(COUNT, ND, R3, 128)]
        else:
            outs += [vmem(8, 128)]
        scratch = [wide, (2, 10) + plane, (COUNT0, 12) + plane, (COUNT, 10, R1, 128), wide, work, (ND, R2, 128)]
        return call(functools.partial(up_kernel, first), outs, scratch, args, "up", 4)

    u, head, tail, c2, c3 = up(True, force, s2, s21, r1, talk, ())
    u0, w0, s2, s21, r1, talk = call(
        first_kernel,
        [hbm(*wide), hbm(*window)] + down_outs(2, R2),
        [window, window, block, window, window, t_shape, work],
        (u,) + two_either_side(u, head, tail) + (far(force), c0, c1),
        "first",
        4,
    )
    m, head, tail, dots0 = up(False, w0, s2, s21, r1, talk, (c2, c3))
    m0, u1, w1, n0, s2, s21, r1, talk = call(
        second_kernel,
        [hbm(*wide), hbm(*wide), hbm(*window), hbm(*block)] + down_outs(4, R2),
        [window, wide, window, block, wide, window, block, window, window, t_shape, work],
        (m,) + two_either_side(m, head, tail) + (dots0, far(force), far(u0), far(w0), c0, c1),
        "second",
        8,
    )
    u2, p1, x2, talk, dots1 = call(
        third_kernel,
        [vmem(*wide)] * 3 + [vmem(members, 8, 128), vmem(8, 128)],
        [wider, (2, 14) + plane, wider, wide, block, wide, block, wide, block, wide]
        + [(COUNT0, 16) + plane, (COUNT, 12, R1, 128), work],
        (position_ref, gather(talk), dots0, s21, r1, far(c0), far(c1), c2, c3)
        + tuple(far(x) for x in (w1, s2, force, u0, w0, m0, n0, u1)),
        "third",
        10,
    )
    state, energy = call(
        last_kernel,
        [vmem(*block), vmem(10, *plane)],
        [wide],
        (gather(talk), dots0, dots1, u2, p1, x2, mod, free),
        "last",
    )
    other = lax.ppermute(energy, "case", [(0, 1), (1, 0)])
    sensitivity = call(
        sensitivity_kernel,
        [vmem(BLOCK, *plane)],
        [(10,) + plane] * 3,
        (energy, other, scale, passive),
        "sensitivity",
    )[0]
    return state, sensitivity


def solution(mesh):
    placed = (
        P("space", None, None),
        P("space", None, None),
        P("space", None, None),
        P("case", None),
    )
    return jax.shard_map(
        on_device,
        mesh=mesh,
        in_specs=placed,
        out_specs=(P("case", "space", None, None), P("space", None, None)),
        check_vma=False,
    )
```

```python
import functools

import jax
import jax.numpy as jnp
from jax import lax
from jax.experimental import pallas as pl
from jax.experimental.pallas import tpu as pltpu
from jax.sharding import PartitionSpec as P

ITERS = 3
E_MIN = 0.01
OMEGA = 0.8
HEAT_SOURCE = 0.05
EDGE_WEIGHT = 1.5 - 2.0**0.5

F32 = jnp.float32
NY, NX = 40, 128
BLOCK = 8
HALO = 13
NEXT = HALO - BLOCK
WINDOW = BLOCK + 2 * HALO
Q1, R1 = 16, 24
QB = 6
REACH = 11
ND = 2 * REACH + 1
R2 = 16
R3 = 8
TALK = 24
CPARAMS = pltpu.CompilerParams(vmem_limit_bytes=32 * 1024 * 1024)


def iota(shape, dim):
    return lax.broadcasted_iota(jnp.int32, shape, dim)


def roll(v, by, dim):
    return pltpu.roll(v, by % v.shape[dim], dim)


def dot(a, b):
    return lax.dot_general(
        a, b, (((1,), (0,)), ((), ())), precision=lax.Precision.HIGHEST, preferred_element_type=F32
    )


def planes(lo, hi, body, group=8):
    def do(js):
        writes = [w for j in js for w in body(j)]
        for ref, index, value in writes:
            ref[index] = value

    count = (hi - lo) // group
    if count == 1:
        do([lo + k for k in range(group)])
    elif count > 1:

        def step(i, carry):
            do([lo + i * group + k for k in range(group)])
            return carry

        lax.fori_loop(0, count, step, 0)
    if lo + count * group < hi:
        do(list(range(lo + count * group, hi)))


def fine_to_half(case):
    i, j = iota((128, 128), 0), iota((128, 128), 1)
    return (j == 64 * case + (i >> 1)).astype(F32)


def half_to_fine(case):
    i, j = iota((128, 128), 0), iota((128, 128), 1)
    return (i == 64 * case + (j >> 1)).astype(F32)


def half_to_quarter(low):
    i, j = iota((128, 128), 0), iota((128, 128), 1)
    return (j == 64 * low + 32 * (i >> 6) + ((i & 63) >> 1)).astype(F32)


def quarter_to_half(low):
    i, j = iota((128, 128), 0), iota((128, 128), 1)
    return (i == 64 * low + 32 * (j >> 6) + ((j & 63) >> 1)).astype(F32)


def quarter_to_eighth():
    i, j = iota((128, 128), 0), iota((128, 128), 1)
    return (j == 16 * ((i >> 5) & 1) + ((i & 31) >> 1)).astype(F32)


def eighth_to_quarter():
    i, j = iota((128, 128), 0), iota((128, 128), 1)
    return (i == 16 * ((j >> 5) & 1) + ((j & 31) >> 1)).astype(F32)


def z_prev(v):
    return jnp.concatenate([jnp.zeros_like(v[:1]), v[:-1]], axis=0)


def z_next(v):
    return jnp.concatenate([v[1:], jnp.zeros_like(v[:1])], axis=0)


def z_prev2(v):
    turned = roll(v, 64, 2)
    return jnp.where(iota(v.shape, 2) >= 64, turned, z_prev(turned))


def z_next2(v):
    turned = roll(v, 64, 2)
    return jnp.where(iota(v.shape, 2) < 64, turned, z_next(turned))


def couple(m, f, factor, width, zp, zn):
    lead = (iota(m.shape, 2) & (width - 1)) > 0
    first = iota(m.shape, 1) > 0
    sides = (
        (lambda v: roll(v, 1, 2), lambda v: roll(v, -1, 2), lead),
        (lambda v: roll(v, 1, 1), lambda v: roll(v, -1, 1), first),
        (zp, zn, None),
    )
    total = jnp.zeros_like(m)
    held = jnp.zeros_like(m)
    coupling = []
    for prev, after, mask in sides:
        k = jnp.sqrt(m * prev(m))
        if mask is not None:
            k = jnp.where(mask, k, 0.0)
        ka = after(k)
        total = total + k + ka
        held = held + k * (1.0 - prev(f)) + ka * (1.0 - after(f))
        inner = factor * k * f * prev(f)
        coupling += [inner, after(inner)]
    rest = f * factor * held + (1.0 - f)
    weight = OMEGA / (f * factor * total + (1.0 - f))
    return tuple(coupling) + (rest, weight)


COUNT = 8
REST, WEIGHT = 6, 7


def apply(v, c, zp, zn):
    out = c[REST] * v + c[0] * (v - roll(v, 1, 2)) + c[1] * (v - roll(v, -1, 2))
    out = out + c[2] * (v - roll(v, 1, 1)) + c[3] * (v - roll(v, -1, 1))
    return out + c[4] * (v - zp(v)) + c[5] * (v - zn(v))


def cut(c, lo, hi):
    return tuple(x[lo:hi] for x in c)


COUNT0 = 7
Z0, REST0, WEIGHT0 = 4, 5, 6


def apply_plane(v_ref, case, i, c_ref, j):
    v = v_ref[case, i]
    out = c_ref[REST0, j] * v + c_ref[0, j] * (v - roll(v, 1, 1)) + c_ref[1, j] * (v - roll(v, -1, 1))
    out = out + c_ref[2, j] * (v - roll(v, 1, 0)) + c_ref[3, j] * (v - roll(v, -1, 0))
    return out + c_ref[Z0, j] * (v - v_ref[case, i - 1]) + c_ref[Z0, j + 1] * (v - v_ref[case, i + 1])


def copy_in(source, target, sem):
    copy = pltpu.make_async_copy(source, target, sem)
    copy.start()
    return copy


def pairs_of_rows(v, scratch):
    n, rows, _ = v.shape
    scratch[: n * rows, :] = v.reshape(n * rows, 128)
    half = n * rows // 2
    even = scratch[pl.ds(0, half, stride=2), :]
    odd = scratch[pl.ds(1, half, stride=2), :]
    return (even + odd).reshape(n, rows // 2, 128)


def put_rows_twice(v, scratch):
    n, rows, _ = v.shape
    flat = v.reshape(n * rows, 128)
    scratch[pl.ds(0, n * rows, stride=2), :] = flat
    scratch[pl.ds(1, n * rows, stride=2), :] = flat


def rows_twice(v, scratch):
    n, rows, _ = v.shape
    put_rows_twice(v, scratch)
    return scratch[: 2 * n * rows, :].reshape(n, 2 * rows, 128)


def flat_dot(v, matrix):
    n, rows, _ = v.shape
    return dot(v.reshape(n * rows, 128), matrix).reshape(n, rows, 128)


def fine_to_level1(t_ref, r_ref, work, count, split):
    flat0 = t_ref[0, :count].reshape(count * NY, 128)
    flat1 = t_ref[1, :count].reshape(count * NY, 128)
    work[: count * NY, :] = dot(flat0, fine_to_half(0)) + dot(flat1, fine_to_half(1))
    r_ref[...] = jnp.zeros_like(r_ref)
    for p in range(count):
        even = work[pl.ds(p * NY, NY // 2, stride=2), :]
        odd = work[pl.ds(p * NY + 1, NY // 2, stride=2), :]
        r_ref[split + p, 0 : NY // 2, :] = even + odd


def down(r_ref, c0, c1, s1, s2, t_ref, work, s2_hbm, sem, reach, rows, s21_out, r1_out, talk):
    trim = 4 - reach
    t = trim // 2

    def first(j):
        return [(s1, (case, j), c0[WEIGHT0, j] * r_ref[case, j]) for case in range(2)]

    planes(1 + trim, WINDOW - 1 - trim, first)

    def second(j):
        return [
            (s2, (case, j), s1[case, j] + c0[WEIGHT0, j] * (r_ref[case, j] - apply_plane(s1, case, j, c0, j)))
            for case in range(2)
        ]

    planes(2 + trim, WINDOW - 2 - trim, second)
    copy = copy_in(s2.at[:, HALO - reach : HALO + BLOCK + reach], s2_hbm, sem)
    count = Q1 - 2 - 2 * t

    def third(p):
        a = 2 * (p + 1 + t) + 1
        return [
            (
                t_ref,
                (case, p),
                (r_ref[case, a] - apply_plane(s2, case, a, c0, a))
                + (r_ref[case, a + 1] - apply_plane(s2, case, a + 1, c0, a + 1)),
            )
            for case in range(2)
        ]

    planes(0, count, third, 4)
    fine_to_level1(t_ref, r1_out, work, count, 1 + t)

    c = tuple(c1[k] for k in range(COUNT))
    lo, hi = 1 + t, Q1 - 1 - t
    forcing = r1_out[lo:hi]
    smoothed = c[WEIGHT][lo:hi] * forcing
    leftover = forcing - apply(smoothed, cut(c, lo, hi), z_prev, z_next)
    relaxed = (smoothed + c[WEIGHT][lo:hi] * leftover)[1:-1]
    s21_out[...] = relaxed
    lo, hi = QB - 1, QB + 5
    inner = relaxed[lo - 2 - t : hi - 2 - t]
    rest = (r1_out[lo:hi] - apply(inner, cut(c, lo, hi), z_prev, z_next))[1:5]
    low, high = rest[0] + rest[1], rest[2] + rest[3]
    mixed = dot(low, half_to_quarter(0)) + dot(high, half_to_quarter(1))
    summed = pairs_of_rows(mixed[None], work)[0]
    work[0:12, :] = summed
    at = 10
    for row in rows:
        work[at : at + row.shape[0], :] = row
        at += row.shape[0]
    tile = work[0 : talk.shape[1], :]
    talk[...] = jnp.broadcast_to(tile[None], talk.shape)
    return copy


def count_kernel(me, index, out, acc):
    base = (me[0] * BLOCK - HALO) * NY
    rows = WINDOW * NY
    chunk = 512
    total = index.shape[1]
    for case in range(2):
        acc[...] = jnp.zeros_like(acc)

        def step(i, carry):
            ids = index[pl.ds(case, 1), pl.ds(pl.multiple_of(i * chunk, chunk), chunk)]
            row = (ids >> 7) - base
            col = ids & 127
            hit_row = jnp.where(iota((rows, chunk), 0) == row, 1.0, 0.0).astype(jnp.bfloat16)
            hit_col = jnp.where(iota((128, chunk), 0) == col, 1.0, 0.0).astype(jnp.bfloat16)
            acc[...] += lax.dot_general(
                hit_row, hit_col, (((1,), (1,)), ((), ())), preferred_element_type=F32
            )
            return carry

        lax.fori_loop(0, total // chunk, step, 0)
        out[case] = acc[...].reshape(WINDOW, NY, 128)


def neighbours_x(p):
    lane = iota(p.shape, 1)
    return jnp.where(lane > 0, roll(p, 1, 1), 0.0) + jnp.where(lane < NX - 1, roll(p, -1, 1), 0.0)


def neighbours_y(p):
    row = iota(p.shape, 0)
    return jnp.where(row > 0, roll(p, 1, 0), 0.0) + jnp.where(row < NY - 1, roll(p, -1, 0), 0.0)


def filter_parts(p):
    sides_y = neighbours_y(p)
    cross = neighbours_x(p) + sides_y
    return cross, 1.5 * p + 0.5 * cross + EDGE_WEIGHT * neighbours_x(sides_y)


def weight_of(me, members, z):
    at = me * BLOCK + z
    lane, row = iota((NY, NX), 1), iota((NY, NX), 0)
    nx = (lane > 0).astype(F32) + (lane < NX - 1).astype(F32)
    ny = (row > 0).astype(F32) + (row < NY - 1).astype(F32)
    nz = jnp.where(at > 0, 1.0, 0.0) + jnp.where(at < members * BLOCK - 1, 1.0, 0.0)
    return 1.5 + 0.5 * (nx + ny + nz) + EDGE_WEIGHT * (nx * ny + nx * nz + ny * nz)


NEAR, AWAY = 3 * BLOCK, 3 * NEXT + 1


def collect_kernel(
    case_ref, design_hbm, passive_hbm, fixed_hbm, own, near, head, tail, all_head, all_tail, design, passive, fixed, sems
):
    pairs = ((design_hbm, design), (passive_hbm, passive), (fixed_hbm, fixed))
    copies = [copy_in(a, b, sems.at[i]) for i, (a, b) in enumerate(pairs)]
    for copy in copies:
        copy.wait()
    at = 0
    for k, source in enumerate((design, passive, fixed)):
        value = source[...].astype(F32)
        own[k * BLOCK : (k + 1) * BLOCK] = value
        count = NEXT + 1 if k == 0 else NEXT
        all_head[at : at + count] = value[0:count]
        all_tail[at : at + count] = value[BLOCK - count : BLOCK]
        at += count
    case = case_ref[0]
    near[...] = own[pl.ds(case * (NEAR // 2), NEAR // 2)]
    head[...] = all_head[pl.ds(case * (AWAY // 2), AWAY // 2)]
    tail[...] = all_tail[pl.ds(case * (AWAY // 2), AWAY // 2)]


def setup_kernel(
    members, me_ref, case_ref, own, before, after, before2, after2, o_before, o_after, o_before2, o_after2, counts,
    c0_hbm, c1_hbm, force_hbm, s2_hbm, s21, r1_out, talk, mod_hbm, free_hbm, scale_hbm,
    near_b, near_a, away_b, away_a,
    raw, cross, base, c0, c1, force, mod, free, scale, s1, s2, t_ref, work, small, sems,
):
    me, case = me_ref[0], case_ref[0]
    halves = (
        (near_b, before, o_before),
        (near_a, after, o_after),
        (away_b, before2, o_before2),
        (away_a, after2, o_after2),
    )
    for target, mine, other in halves:
        half = mine.shape[0]
        target[pl.ds(case * half, half)] = mine[...]
        target[pl.ds((1 - case) * half, half)] = other[...]
    start = 0
    for source, count in ((away_b, NEXT + 1), (near_b, BLOCK), (own, BLOCK), (near_a, BLOCK), (away_a, NEXT + 1)):
        raw[start : start + count] = source[0:count]
        start += count

    def parts(k):
        a, b = filter_parts(raw[k])
        return [(cross, (k,), a), (base, (k,), b)]

    planes(0, WINDOW + 2, parts, 6)

    def material(j, passive, fixed, near):
        z = j - HALO
        at = me * BLOCK + z
        inside = jnp.where((at >= 0) & (at < members * BLOCK), 1.0, 0.0)
        filtered = base[j + 1] + 0.5 * (raw[j] + raw[j + 2]) + EDGE_WEIGHT * (cross[j] + cross[j + 2])
        weight = weight_of(me, members, z)
        density = jnp.where(passive == 1.0, 1.0, jnp.where(passive == 2.0, 0.0, filtered / weight))
        modulus = E_MIN + (1.0 - E_MIN) * density * density * density
        freedom = inside * (1.0 - fixed)
        writes = [(mod, (j,), inside * modulus), (free, (j,), freedom)]
        writes += [(force, (case, j), freedom * (HEAT_SOURCE + counts[case, j])) for case in range(2)]
        if near:
            gradient = (-1.5 * (1.0 - E_MIN)) * density * density / (modulus * weight)
            gradient = jnp.where(passive == 0.0, inside * gradient, 0.0)
            writes.append((scale, (j - HALO + 1,), gradient))
        return writes

    def stretch(source, first, second, j0, lo, hi, near=False):
        planes(lo, hi, lambda j: material(j, source[first + j - j0], source[second + j - j0], near), 5)

    stretch(away_b, NEXT + 1, 2 * NEXT + 1, 0, 0, NEXT)
    stretch(near_b, BLOCK, 2 * BLOCK, NEXT, NEXT, HALO - 1)
    stretch(near_b, BLOCK, 2 * BLOCK, NEXT, HALO - 1, HALO, True)
    stretch(own, BLOCK, 2 * BLOCK, HALO, HALO, HALO + BLOCK, True)
    stretch(near_a, BLOCK, 2 * BLOCK, HALO + BLOCK, HALO + BLOCK, HALO + BLOCK + 1, True)
    stretch(near_a, BLOCK, 2 * BLOCK, HALO + BLOCK, HALO + BLOCK + 1, HALO + 2 * BLOCK)
    stretch(away_a, NEXT + 1, 2 * NEXT + 1, HALO + 2 * BLOCK, HALO + 2 * BLOCK, WINDOW)
    near = slice(HALO - 2, HALO + BLOCK + 2)
    copies = [
        copy_in(force, force_hbm, sems.at[0]),
        copy_in(mod.at[near], mod_hbm, sems.at[1]),
        copy_in(free.at[near], free_hbm, sems.at[2]),
        copy_in(scale, scale_hbm, sems.at[3]),
    ]

    lane, row = iota((NY, NX), 1), iota((NY, NX), 0)
    zero = jnp.zeros((NY, NX), F32)

    def coefficients(j):
        m, f = mod[j], free[j]
        total, held = zero, zero
        writes = []
        for dim, mask, slot in ((1, lane > 0, 0), (0, row > 0, 2)):
            k = jnp.where(mask, jnp.sqrt(m * roll(m, 1, dim)), 0.0)
            ka = roll(k, -1, dim)
            fp = roll(f, 1, dim)
            total = total + k + ka
            held = held + k * (1.0 - fp) + ka * (1.0 - roll(f, -1, dim))
            inner = k * f * fp
            writes += [(c0, (slot, j), inner), (c0, (slot + 1, j), roll(inner, -1, dim))]
        k, ka = jnp.sqrt(m * mod[j - 1]), jnp.sqrt(m * mod[j + 1])
        total = total + k + ka
        held = held + k * (1.0 - free[j - 1]) + ka * (1.0 - free[j + 1])
        writes.append((c0, (Z0, j), k * f * free[j - 1]))
        writes.append((c0, (REST0, j), f * held + (1.0 - f)))
        writes.append((c0, (WEIGHT0, j), OMEGA / (f * total + (1.0 - f))))
        return writes

    planes(1, WINDOW - 1, coefficients, 4)
    last = WINDOW - 1
    for slot in range(COUNT0):
        c0[slot, 0] = zero
        c0[slot, last] = zero
    c0[Z0, last] = jnp.sqrt(mod[last] * mod[last - 1]) * free[last] * free[last - 1]
    copies.append(copy_in(c0, c0_hbm, sems.at[4]))

    def join(q):
        return [(t_ref, (k, q), x[2 * q + 1] + x[2 * q + 2]) for k, x in enumerate((mod, free))]

    planes(0, Q1, join)
    fine_to_level1(t_ref, small, work, Q1, 0)
    both = small[...]
    second = iota(both.shape, 2) >= 64
    both = jnp.where(second, (both > 0.0).astype(F32), 0.125 * both)
    turned = roll(both, 64, 2)
    m1 = jnp.where(second, turned, both)
    f1 = jnp.where(second, both, turned)
    for k, value in enumerate(couple(m1, f1, 2.0, 64, z_prev, z_next)):
        c1[k] = value
    copies.append(copy_in(c1, c1_hbm, sems.at[5]))

    low, high = both[QB] + both[QB + 1], both[QB + 2] + both[QB + 3]
    mixed = dot(low, half_to_quarter(0)) + dot(high, half_to_quarter(1))
    coarse = pairs_of_rows(mixed[None], work)[0]
    is_free = (iota(coarse.shape, 1) & 32) > 0
    coarse = jnp.where(is_free, (coarse > 0.0).astype(F32), 0.125 * coarse)

    rows = (coarse, jnp.zeros((2, 128), F32))
    copies.append(down(force, c0, c1, s1, s2, t_ref, work, s2_hbm, sems.at[6], 2, rows, s21, r1_out, talk))
    for copy in copies:
        copy.wait()


def coarse_window(me, gathered, lo, hi):
    members = gathered.shape[0]
    tiles = []
    for d in range(ND):
        at = me + d - REACH
        inside = jnp.where((at >= 0) & (at < members), 1.0, 0.0)
        tiles.append(inside * gathered[jnp.clip(at, 0, members - 1), lo:hi, :])
    return jnp.stack(tiles, axis=0)


def coarse_setup(me, gathered, c2, c3, work, wide):
    wide[...] = jnp.zeros_like(wide)
    wide[:, 0:10, :] = coarse_window(me, gathered, 10, 20)
    both = wide[...]
    is_free = (iota(both.shape, 2) & 32) > 0
    m = jnp.where(is_free, roll(both, 32, 2), both)
    f = jnp.where(is_free, both, roll(both, -32, 2))
    for k, value in enumerate(couple(m, f, 4.0, 32, z_prev2, z_next2)):
        c2[k] = value
    eighth = quarter_to_eighth()
    m3 = 0.125 * pairs_of_rows(flat_dot(m, eighth), work)
    f3 = (pairs_of_rows(flat_dot(f, eighth), work) > 0.0).astype(F32)
    for k, value in enumerate(couple(m3, f3, 8.0, 16, z_prev, z_next)):
        c3[k] = value


def coarse_solve(r2, c2, c3, work):
    c = tuple(c2[k] for k in range(COUNT))
    smoothed = c[WEIGHT] * r2
    relaxed = smoothed + c[WEIGHT] * (r2 - apply(smoothed, c, z_prev2, z_next2))
    leftover = (r2 - apply(relaxed, c, z_prev2, z_next2))[2 : ND - 2]
    forcing = pairs_of_rows(flat_dot(leftover, quarter_to_eighth()), work)
    lo, hi = 2, ND - 2
    v = c3[WEIGHT, lo:hi] * forcing
    for _ in range(7):
        ck = tuple(c3[k, lo:hi] for k in range(COUNT))
        v = v + ck[WEIGHT] * (forcing - apply(v, ck, z_prev, z_next))
        v, forcing = v[1:-1], forcing[1:-1]
        lo, hi = lo + 1, hi - 1
    up = rows_twice(flat_dot(v, eighth_to_quarter()), work)
    lo, hi = REACH - 2, REACH + 3
    v = relaxed[lo:hi] + up
    ck = cut(c, lo, hi)
    for _ in range(2):
        v = v + ck[WEIGHT] * (r2[lo:hi] - apply(v, ck, z_prev2, z_next2))
    return v[1:4]


def level1_up(e2, relaxed, forcing, c, work):
    parts = []
    for low in range(2):
        lanes = flat_dot(e2, quarter_to_half(low))
        parts.append(rows_twice(lanes, work)[:, :R1])
    lifted = [parts[z & 1][z >> 1] for z in range(6)]
    n = relaxed.shape[0]
    lead = (12 - n) // 2
    v = relaxed + jnp.stack([lifted[(q + lead) // 2] for q in range(n)], axis=0)
    for _ in range(2):
        v = (v + c[WEIGHT] * (forcing - apply(v, c, z_prev, z_next)))[1:-1]
        forcing, c = forcing[1:-1], cut(c, 1, -1)
    return v


def level0_up(v1, s2, r, vb, c0, out, work):
    count = v1.shape[0]
    for case in range(2):
        lanes = flat_dot(v1, half_to_fine(case))
        put_rows_twice(lanes, work)
        for p in range(count):
            fine = work[p * 2 * R1 : p * 2 * R1 + NY, :]
            s2[case, 2 * p] = s2[case, 2 * p] + fine
            s2[case, 2 * p + 1] = s2[case, 2 * p + 1] + fine
    total = s2.shape[1]

    def sweep(v, case, i):
        return v[case, i] + c0[WEIGHT0, i] * (r[case, i - 1] - apply_plane(v, case, i, c0, i))

    def once(i):
        return [(vb, (case, i), sweep(s2, case, i)) for case in range(2)]

    planes(1, total - 1, once, 7 if total == 16 else 5)

    def twice(i):
        return [(out, (case, i - 2), sweep(vb, case, i)) for case in range(2)]

    planes(2, total - 2, twice, 6 if total == 16 else 8)


def add_up(parts):
    while len(parts) > 1:
        parts = [sum(parts[i : i + 2][1:], parts[i]) for i in range(0, len(parts), 2)]
    return parts[0]


def sum_of_rows(gathered, lo, hi):
    return add_up([gathered[d, lo:hi, :] for d in range(gathered.shape[0])])


def residual_window(me, gathered):
    r2 = coarse_window(me, gathered, 0, 16)
    return jnp.where(iota(r2.shape, 1) < 10, r2, 0.0)


def around(reach):
    return slice(HALO - reach, HALO + BLOCK + reach)


def up_kernel(first, me_ref, gathered, r_hbm, s2_hbm, s21, r1_ref, c0_hbm, c1_hbm, *rest):
    if first:
        out, head, tail, c2, c3, s2, r, c0, c1, vb, work, wide, sems = rest
    else:
        c2, c3, out, head, tail, dots, s2, r, c0, c1, vb, work, wide, sems = rest
    sources = (
        (s2_hbm, s2),
        (r_hbm.at[:, around(1)], r),
        (c0_hbm.at[:, around(2)], c0),
        (c1_hbm.at[:, 3:13], c1),
    )
    copies = [copy_in(a, b, sems.at[i]) for i, (a, b) in enumerate(sources)]
    me = me_ref[0]
    if first:
        coarse_setup(me, gathered, c2, c3, work, wide)
    else:
        dots[...] = sum_of_rows(gathered, 8, 16)
    e2 = coarse_solve(residual_window(me, gathered), c2, c3, work)
    for copy in copies:
        copy.wait()
    v1 = level1_up(e2, s21[...], r1_ref[3:13], tuple(c1[k] for k in range(COUNT)), work)

    level0_up(v1, s2, r, vb, c0, out, work)
    for case in range(2):
        head[case] = out[case, 0:NEXT]
        tail[case] = out[case, BLOCK - NEXT : BLOCK]


def lay_out(win, own, before, after, before2, after2):
    start = 0
    for source in (before2, before, own, after, after2):
        count = source.shape[1]
        for case in range(2):
            win[case, start : start + count] = source[case]
        start += count


def dot_rows(values):
    lane = iota((1, 128), 1)
    rows = []
    for a, b in values:
        rows.append(jnp.where(lane < 64, jnp.sum(a, keepdims=True), jnp.sum(b, keepdims=True)))
    return rows


def accumulate(count, term):
    sums = []
    for case in range(2):
        terms = [term(case, k) for k in range(BLOCK)]
        sums.append([add_up([t[i] for t in terms]) for i in range(count)])
    return dot_rows([(sums[0][i], sums[1][i]) for i in range(count)])


def first_kernel(
    own, before, after, before2, after2, force_hbm, c0, c1,
    u_hbm, w_hbm, s2_hbm, s21, r1_out, talk,
    u_win, w_win, force, s1, s2, t_ref, work, sems,
):
    copy_f = copy_in(force_hbm.at[:, around(0)], force, sems.at[0])
    lay_out(u_win, own, before, after, before2, after2)
    copies = [copy_in(u_win.at[:, around(2)], u_hbm, sems.at[1])]

    def image(j):
        return [(w_win, (case, j), apply_plane(u_win, case, j, c0, j)) for case in range(2)]

    planes(1, WINDOW - 1, image)
    copies.append(copy_in(w_win, w_hbm, sems.at[2]))
    copy_f.wait()

    def term(case, k):
        u = own[case, k]
        return (force[case, k] * u, w_win[case, HALO + k] * u)

    rows = accumulate(2, term) + [jnp.zeros((4, 128), F32)]
    copies.append(down(w_win, c0, c1, s1, s2, t_ref, work, s2_hbm, sems.at[3], 2, rows, s21, r1_out, talk))
    for copy in copies:
        copy.wait()


def of_case(row, case):
    return row[:, 64 * case : 64 * case + 1]


def second_kernel(
    own, before, after, before2, after2, dots0, force_hbm, u0_hbm, w0_hbm, c0, c1,
    m_hbm, u1_hbm, w1_hbm, n0_hbm, s2_hbm, s21, r1_out, talk,
    m_win, u0, w0, n0, u1, w1, force, s1, s2, t_ref, work, sems,
):
    copy_w = copy_in(w0_hbm, w0, sems.at[0])
    copy_u = copy_in(u0_hbm, u0, sems.at[1])
    copy_f = copy_in(force_hbm.at[:, around(0)], force, sems.at[2])
    lay_out(m_win, own, before, after, before2, after2)
    copies = [copy_in(m_win.at[:, around(2)], m_hbm, sems.at[3])]
    alpha = [of_case(dots0[2:3, :] / dots0[3:4, :], case) for case in range(2)]
    copy_w.wait()

    def image(j, block=False):
        writes = []
        for case in range(2):
            n = apply_plane(m_win, case, j, c0, j)
            writes.append((w1, (case, j), w0[case, j] - alpha[case] * n))
            if block:
                writes.append((n0, (case, j - HALO), n))
        return writes

    planes(1, HALO, image, 6)
    planes(HALO, HALO + BLOCK, functools.partial(image, block=True))
    planes(HALO + BLOCK, WINDOW - 1, image, 6)
    copies.append(copy_in(n0, n0_hbm, sems.at[4]))
    copies.append(copy_in(w1, w1_hbm, sems.at[5]))
    copy_u.wait()

    def update(i):
        return [(u1, (case, i), u0[case, i] - alpha[case] * m_win[case, i + HALO - 2]) for case in range(2)]

    planes(0, BLOCK + 4, update)
    copies.append(copy_in(u1, u1_hbm, sems.at[6]))
    copy_f.wait()

    def term(case, k):
        j = HALO + k
        u, w, ww = u1[case, k + 2], w1[case, j], w0[case, j]
        r = force[case, k] - alpha[case] * ww
        return (r * u, w * u, u * ww + u0[case, k + 2] * w)

    rows = accumulate(3, term) + [jnp.zeros((3, 128), F32)]
    copies.append(down(w1, c0, c1, s1, s2, t_ref, work, s2_hbm, sems.at[7], 4, rows, s21, r1_out, talk))
    for copy in copies:
        copy.wait()


def third_kernel(
    me_ref, gathered, dots0, s21, r1_ref, c0_hbm, c1_hbm, c2, c3,
    w1_hbm, s2_hbm, force_hbm, u0_hbm, w0_hbm, m0_hbm, n0_hbm, u1_hbm,
    u2, p1, x2, talk, dots1,
    s2, w1, vb, m_win, force, u0, w0, m0, n0, u1, c0, c1, work, sems,
):
    sources = (
        (c1_hbm.at[:, 2:14], c1),
        (s2_hbm, s2),
        (c0_hbm.at[:, around(4)], c0),
        (w1_hbm.at[:, around(3)], w1),
        (force_hbm.at[:, around(0)], force),
        (u0_hbm, u0),
        (w0_hbm.at[:, around(0)], w0),
        (m0_hbm, m0),
        (n0_hbm, n0),
        (u1_hbm, u1),
    )
    copies = [copy_in(a, b, sems.at[i]) for i, (a, b) in enumerate(sources)]
    dots1[...] = sum_of_rows(gathered, 8, 16)
    e2 = coarse_solve(residual_window(me_ref[0], gathered), c2, c3, work)
    copies[0].wait()
    v1 = level1_up(e2, s21[...], r1_ref[2:14], tuple(c1[k] for k in range(COUNT)), work)

    for copy in copies[1:]:
        copy.wait()
    level0_up(v1, s2, w1, vb, c0, m_win, work)

    gamma0, delta0 = dots0[2:3, :], dots0[3:4, :]
    gamma1 = dots1[2:3, :]
    beta = gamma1 / gamma0
    curve = dots1[3:4, :] + beta * dots1[4:5, :] + beta * beta * delta0
    a0 = [of_case(gamma0 / delta0, case) for case in range(2)]
    a1 = [of_case(gamma1 / curve, case) for case in range(2)]
    b1 = [of_case(beta, case) for case in range(2)]

    def update(i):
        writes = []
        for case in range(2):
            p = u1[case, i] + b1[case] * u0[case, i]
            writes.append((p1, (case, i), p))
            writes.append((x2, (case, i), a0[case] * u0[case, i] + a1[case] * p))
            u = u1[case, i] - a1[case] * (m_win[case, i] + b1[case] * m0[case, i])
            writes.append((u2, (case, i), u))
        return writes

    planes(0, 12, update)

    def term(case, k):
        n1 = apply_plane(m_win, case, k + 2, c0, k + 4)
        ww, wv = w0[case, k], w1[case, k + 3]
        s = wv + b1[case] * ww
        w = wv - a1[case] * (n1 + b1[case] * n0[case, k])
        r = force[case, k] - a0[case] * ww - a1[case] * s
        u, p = u2[case, k + 2], p1[case, k + 2]
        return (r * u, w * u, u * s + p * w)

    rows = accumulate(3, term) + [jnp.zeros((5, 128), F32)]
    tile = jnp.concatenate(rows, axis=0)
    talk[...] = jnp.broadcast_to(tile[None], talk.shape)


def last_kernel(gathered, dots0, dots1, u2, p1, x2, mod, free, state, energy, w_win):
    total = add_up([gathered[d] for d in range(gathered.shape[0])])
    gamma0, delta0 = dots0[2:3, :], dots0[3:4, :]
    gamma1 = dots1[2:3, :]
    beta1 = gamma1 / gamma0
    curve1 = dots1[3:4, :] + beta1 * dots1[4:5, :] + beta1 * beta1 * delta0
    gamma2 = total[0:1, :]
    beta2 = gamma2 / gamma1
    curve2 = total[1:2, :] + beta2 * total[2:3, :] + beta2 * beta2 * curve1
    a2 = [of_case(gamma2 / curve2, case) for case in range(2)]
    b2 = [of_case(beta2, case) for case in range(2)]

    def update(i):
        return [
            (w_win, (case, i), x2[case, i] + a2[case] * (u2[case, i] + b2[case] * p1[case, i])) for case in range(2)
        ]

    planes(0, 12, update, 4)
    state[...] = w_win[:, 2:10]

    def hold(i):
        return [(w_win, (case, i), w_win[case, i] * free[i]) for case in range(2)]

    planes(0, 12, hold, 4)
    lane, row = iota((NY, NX), 1), iota((NY, NX), 0)

    def power(i):
        m = mod[i + 1]
        out = jnp.zeros((NY, NX), F32)
        kx = jnp.where(lane > 0, jnp.sqrt(m * roll(m, 1, 1)), 0.0)
        ky = jnp.where(row > 0, jnp.sqrt(m * roll(m, 1, 0)), 0.0)
        kz, kn = jnp.sqrt(m * mod[i]), jnp.sqrt(m * mod[i + 2])
        for case in range(2):
            v = w_win[case, i + 1]
            dx, dy = v - roll(v, 1, 1), v - roll(v, 1, 0)
            dz, dn = v - w_win[case, i], v - w_win[case, i + 2]
            px, py = kx * dx * dx, ky * dy * dy
            out = out + px + roll(px, -1, 1) + py + roll(py, -1, 0) + kz * dz * dz + kn * dn * dn
        return [(energy, (i,), out)]

    planes(0, 10, power, 5)


def sensitivity_kernel(mine, other, scale, passive, out, g, cross, base):
    def gradient(i):
        value = scale[i] * (mine[i] + other[i])
        a, b = filter_parts(value)
        return [(g, (i,), value), (cross, (i,), a), (base, (i,), b)]

    planes(0, 10, gradient, 5)

    def final(k):
        i = k + 1
        value = base[i] + 0.5 * (g[i - 1] + g[i + 1]) + EDGE_WEIGHT * (cross[i - 1] + cross[i + 1])
        return [(out, (k,), jnp.where(passive[k] == 0, value, 0.0))]

    planes(0, 8, final)


def shape(*dims):
    return jax.ShapeDtypeStruct(dims, F32)


def hbm(*dims):
    return pltpu.HBM(dims, F32), pltpu.HBM


def vmem(*dims):
    return shape(*dims), pltpu.VMEM


def call(body, outs, scratch, args, name, sems=0, cost=None):
    pairs = [a if isinstance(a, tuple) else (a, pltpu.VMEM) for a in args]
    scratches = [pltpu.VMEM(s, F32) if isinstance(s, tuple) else s for s in scratch]
    if sems:
        scratches.append(pltpu.SemaphoreType.DMA((sems,)))
    given = [pltpu.with_memory_space_constraint(a, m) if m is pltpu.HBM else a for a, m in pairs]
    return pl.pallas_call(
        body,
        out_shape=[o for o, _ in outs],
        in_specs=[pl.BlockSpec(memory_space=m) for _, m in pairs],
        out_specs=[pl.BlockSpec(memory_space=m) for _, m in outs],
        scratch_shapes=scratches,
        compiler_params=CPARAMS,
        cost_estimate=cost,
        name=name,
    )(*given)


def on_device(design, passive, fixed_mask, load_index):
    members = lax.axis_size("space")
    position = lax.axis_index("space")
    me = position.astype(jnp.int32).reshape(1)
    ahead = [(i, i + 1) for i in range(members - 1)]
    back = [(i + 1, i) for i in range(members - 1)]

    def two_either_side(own, head, tail):
        skip = [(i, i + 2) for i in range(members - 2)]
        skip_back = [(i + 2, i) for i in range(members - 2)]
        away = lax.ppermute(tail, "space", skip), lax.ppermute(head, "space", skip_back)
        return (lax.ppermute(own, "space", ahead), lax.ppermute(own, "space", back)) + away

    def gather(tiles):
        return lax.all_to_all(tiles, "space", 0, 0)

    plane = (NY, NX)
    window = (2, WINDOW) + plane
    block = (2, BLOCK) + plane
    wide = (2, BLOCK + 4) + plane
    wider = (2, BLOCK + 8) + plane
    work = (800, 128)
    t_shape = (2, Q1) + plane
    position_ref = (me, pltpu.SMEM)

    def down_outs(reach, count):
        near = 2 + reach // 2
        return [
            hbm(2, BLOCK + 2 * reach, *plane),
            vmem(4 + 2 * near, R1, 128),
            vmem(Q1, R1, 128),
            vmem(members, count, 128),
        ]

    def far(x):
        return (x, pltpu.HBM)

    case_ref = (lax.axis_index("case").astype(jnp.int32).reshape(1), pltpu.SMEM)
    own, near, head, tail = call(
        collect_kernel,
        [vmem(NEAR, *plane), vmem(NEAR // 2, *plane), vmem(AWAY // 2, *plane), vmem(AWAY // 2, *plane)],
        [(AWAY,) + plane] * 2 + [pltpu.VMEM((BLOCK,) + plane, x.dtype) for x in (design, passive, fixed_mask)],
        (case_ref, far(design), far(passive), far(fixed_mask)),
        "collect",
        3,
    )
    listened = two_either_side(near, head, tail)
    counts = call(
        count_kernel,
        [vmem(*window)],
        [(WINDOW * NY, 128)],
        (position_ref, load_index),
        "counts",
        cost=pl.CostEstimate(flops=3 * 10**10, bytes_accessed=10**7, transcendentals=0),
    )[0]
    listened, counts = lax.optimization_barrier((listened, counts))
    listened += tuple(lax.ppermute(x, "case", [(0, 1), (1, 0)]) for x in listened)
    c0, c1, force, s2, s21, r1, talk, mod, free, scale = call(
        functools.partial(setup_kernel, members),
        [hbm(COUNT0, WINDOW, *plane), hbm(COUNT, Q1, R1, 128), hbm(*window)]
        + down_outs(2, TALK)
        + [hbm(12, *plane), hbm(12, *plane), hbm(10, *plane)],
        [(NEAR,) + plane] * 2
        + [(AWAY,) + plane] * 2
        + [(WINDOW + 2,) + plane] * 3
        + [(COUNT0, WINDOW) + plane, (COUNT, Q1, R1, 128)]
        + [window, (WINDOW,) + plane, (WINDOW,) + plane, (10,) + plane, window, window, t_shape, work]
        + [(Q1, R1, 128)],
        (position_ref, case_ref, own) + listened + (counts,),
        "setup",
        7,
    )

    def up(first, r, s2, s21, r1, talk, more):
        args = (position_ref, gather(talk), far(r), far(s2), s21, r1, far(c0), far(c1)) + tuple(more)
        outs = [vmem(*block), vmem(2, NEXT, *plane), vmem(2, NEXT, *plane)]
        if first:
            outs += [vmem(COUNT, ND, R2, 128), vmem(COUNT, ND, R3, 128)]
        else:
            outs += [vmem(8, 128)]
        scratch = [wide, (2, 10) + plane, (COUNT0, 12) + plane, (COUNT, 10, R1, 128), wide, work, (ND, R2, 128)]
        return call(functools.partial(up_kernel, first), outs, scratch, args, "up", 4)

    u, head, tail, c2, c3 = up(True, force, s2, s21, r1, talk, ())
    u0, w0, s2, s21, r1, talk = call(
        first_kernel,
        [hbm(*wide), hbm(*window)] + down_outs(2, R2),
        [window, window, block, window, window, t_shape, work],
        (u,) + two_either_side(u, head, tail) + (far(force), c0, c1),
        "first",
        4,
    )
    m, head, tail, dots0 = up(False, w0, s2, s21, r1, talk, (c2, c3))
    m0, u1, w1, n0, s2, s21, r1, talk = call(
        second_kernel,
        [hbm(*wide), hbm(*wide), hbm(*window), hbm(*block)] + down_outs(4, R2),
        [window, wide, window, block, wide, window, block, window, window, t_shape, work],
        (m,) + two_either_side(m, head, tail) + (dots0, far(force), far(u0), far(w0), c0, c1),
        "second",
        8,
    )
    u2, p1, x2, talk, dots1 = call(
        third_kernel,
        [vmem(*wide)] * 3 + [vmem(members, 8, 128), vmem(8, 128)],
        [wider, (2, 14) + plane, wider, wide, block, wide, block, wide, block, wide]
        + [(COUNT0, 16) + plane, (COUNT, 12, R1, 128), work],
        (position_ref, gather(talk), dots0, s21, r1, far(c0), far(c1), c2, c3)
        + tuple(far(x) for x in (w1, s2, force, u0, w0, m0, n0, u1)),
        "third",
        10,
    )
    state, energy = call(
        last_kernel,
        [vmem(*block), vmem(10, *plane)],
        [wide],
        (gather(talk), dots0, dots1, u2, p1, x2, mod, free),
        "last",
    )
    other = lax.ppermute(energy, "case", [(0, 1), (1, 0)])
    sensitivity = call(
        sensitivity_kernel,
        [vmem(BLOCK, *plane)],
        [(10,) + plane] * 3,
        (energy, other, scale, passive),
        "sensitivity",
    )[0]
    return state, sensitivity


def solution(mesh):
    placed = (
        P("space", None, None),
        P("space", None, None),
        P("space", None, None),
        P("case", None),
    )
    return jax.shard_map(
        on_device,
        mesh=mesh,
        in_specs=placed,
        out_specs=(P("case", "space", None, None), P("space", None, None)),
        check_vma=False,
    )
```

```python
import functools

import jax
import jax.numpy as jnp
from jax import lax
from jax.experimental import pallas as pl
from jax.experimental.pallas import tpu as pltpu
from jax.sharding import PartitionSpec as P

ITERS = 3
E_MIN = 0.01
OMEGA = 0.8
HEAT_SOURCE = 0.05
EDGE_WEIGHT = 1.5 - 2.0**0.5

F32 = jnp.float32
NY, NX = 40, 128
BLOCK = 8
HALO = 13
NEXT = HALO - BLOCK
WINDOW = BLOCK + 2 * HALO
Q1, R1 = 16, 24
QB = 6
REACH = 11
ND = 2 * REACH + 1
R2 = 16
R3 = 8
TALK = 24
CPARAMS = pltpu.CompilerParams(vmem_limit_bytes=32 * 1024 * 1024)


def iota(shape, dim):
    return lax.broadcasted_iota(jnp.int32, shape, dim)


def roll(v, by, dim):
    return pltpu.roll(v, by % v.shape[dim], dim)


def dot(a, b):
    b = b.astype(jnp.bfloat16)
    out = None
    for _ in range(3):
        part = a.astype(jnp.bfloat16)
        a = a - part.astype(F32)
        product = lax.dot_general(part, b, (((1,), (0,)), ((), ())), preferred_element_type=F32)
        out = product if out is None else out + product
    return out


def planes(lo, hi, body, group=8):
    def do(js):
        writes = [w for j in js for w in body(j)]
        for ref, index, value in writes:
            ref[index] = value

    count = (hi - lo) // group
    if count == 1:
        do([lo + k for k in range(group)])
    elif count > 1:

        def step(i, carry):
            do([lo + i * group + k for k in range(group)])
            return carry

        lax.fori_loop(0, count, step, 0)
    if lo + count * group < hi:
        do(list(range(lo + count * group, hi)))


def fine_to_half(case):
    i, j = iota((128, 128), 0), iota((128, 128), 1)
    return (j == 64 * case + (i >> 1)).astype(F32)


def half_to_fine(case):
    i, j = iota((128, 128), 0), iota((128, 128), 1)
    return (i == 64 * case + (j >> 1)).astype(F32)


def half_to_quarter(low):
    i, j = iota((128, 128), 0), iota((128, 128), 1)
    return (j == 64 * low + 32 * (i >> 6) + ((i & 63) >> 1)).astype(F32)


def quarter_to_half(low):
    i, j = iota((128, 128), 0), iota((128, 128), 1)
    return (i == 64 * low + 32 * (j >> 6) + ((j & 63) >> 1)).astype(F32)


def quarter_to_eighth():
    i, j = iota((128, 128), 0), iota((128, 128), 1)
    return (j == 16 * ((i >> 5) & 1) + ((i & 31) >> 1)).astype(F32)


def eighth_to_quarter():
    i, j = iota((128, 128), 0), iota((128, 128), 1)
    return (i == 16 * ((j >> 5) & 1) + ((j & 31) >> 1)).astype(F32)


def z_prev(v):
    return jnp.concatenate([jnp.zeros_like(v[:1]), v[:-1]], axis=0)


def z_next(v):
    return jnp.concatenate([v[1:], jnp.zeros_like(v[:1])], axis=0)


def z_prev2(v):
    turned = roll(v, 64, 2)
    return jnp.where(iota(v.shape, 2) >= 64, turned, z_prev(turned))


def z_next2(v):
    turned = roll(v, 64, 2)
    return jnp.where(iota(v.shape, 2) < 64, turned, z_next(turned))


def couple(m, f, factor, width, zp, zn):
    lead = (iota(m.shape, 2) & (width - 1)) > 0
    first = iota(m.shape, 1) > 0
    sides = (
        (lambda v: roll(v, 1, 2), lambda v: roll(v, -1, 2), lead),
        (lambda v: roll(v, 1, 1), lambda v: roll(v, -1, 1), first),
        (zp, zn, None),
    )
    total = jnp.zeros_like(m)
    held = jnp.zeros_like(m)
    coupling = []
    for prev, after, mask in sides:
        k = jnp.sqrt(m * prev(m))
        if mask is not None:
            k = jnp.where(mask, k, 0.0)
        ka = after(k)
        total = total + k + ka
        held = held + k * (1.0 - prev(f)) + ka * (1.0 - after(f))
        inner = factor * k * f * prev(f)
        coupling += [inner, after(inner)]
    rest = f * factor * held + (1.0 - f)
    weight = OMEGA / (f * factor * total + (1.0 - f))
    return tuple(coupling) + (rest, weight)


COUNT = 8
REST, WEIGHT = 6, 7


def apply(v, c, zp, zn):
    out = c[REST] * v + c[0] * (v - roll(v, 1, 2)) + c[1] * (v - roll(v, -1, 2))
    out = out + c[2] * (v - roll(v, 1, 1)) + c[3] * (v - roll(v, -1, 1))
    return out + c[4] * (v - zp(v)) + c[5] * (v - zn(v))


def cut(c, lo, hi):
    return tuple(x[lo:hi] for x in c)


COUNT0 = 7
Z0, REST0, WEIGHT0 = 4, 5, 6


def apply_plane(v_ref, case, i, c_ref, j):
    v = v_ref[case, i]
    out = c_ref[REST0, j] * v + c_ref[0, j] * (v - roll(v, 1, 1)) + c_ref[1, j] * (v - roll(v, -1, 1))
    out = out + c_ref[2, j] * (v - roll(v, 1, 0)) + c_ref[3, j] * (v - roll(v, -1, 0))
    return out + c_ref[Z0, j] * (v - v_ref[case, i - 1]) + c_ref[Z0, j + 1] * (v - v_ref[case, i + 1])


def copy_in(source, target, sem):
    copy = pltpu.make_async_copy(source, target, sem)
    copy.start()
    return copy


def pairs_of_rows(v, scratch):
    n, rows, _ = v.shape
    scratch[: n * rows, :] = v.reshape(n * rows, 128)
    half = n * rows // 2
    even = scratch[pl.ds(0, half, stride=2), :]
    odd = scratch[pl.ds(1, half, stride=2), :]
    return (even + odd).reshape(n, rows // 2, 128)


def put_rows_twice(v, scratch):
    n, rows, _ = v.shape
    flat = v.reshape(n * rows, 128)
    scratch[pl.ds(0, n * rows, stride=2), :] = flat
    scratch[pl.ds(1, n * rows, stride=2), :] = flat


def rows_twice(v, scratch):
    n, rows, _ = v.shape
    put_rows_twice(v, scratch)
    return scratch[: 2 * n * rows, :].reshape(n, 2 * rows, 128)


def flat_dot(v, matrix):
    n, rows, _ = v.shape
    return dot(v.reshape(n * rows, 128), matrix).reshape(n, rows, 128)


def fine_to_level1(t_ref, r_ref, work, count, split):
    flat0 = t_ref[0, :count].reshape(count * NY, 128)
    flat1 = t_ref[1, :count].reshape(count * NY, 128)
    work[: count * NY, :] = dot(flat0, fine_to_half(0)) + dot(flat1, fine_to_half(1))
    r_ref[...] = jnp.zeros_like(r_ref)
    for p in range(count):
        even = work[pl.ds(p * NY, NY // 2, stride=2), :]
        odd = work[pl.ds(p * NY + 1, NY // 2, stride=2), :]
        r_ref[split + p, 0 : NY // 2, :] = even + odd


def down(r_ref, c0, c1, s1, s2, t_ref, work, s2_hbm, sem, reach, rows, s21_out, r1_out, talk):
    trim = 4 - reach
    t = trim // 2

    def first(j):
        return [(s1, (case, j), c0[WEIGHT0, j] * r_ref[case, j]) for case in range(2)]

    planes(1 + trim, WINDOW - 1 - trim, first)

    def second(j):
        return [
            (s2, (case, j), s1[case, j] + c0[WEIGHT0, j] * (r_ref[case, j] - apply_plane(s1, case, j, c0, j)))
            for case in range(2)
        ]

    planes(2 + trim, WINDOW - 2 - trim, second)
    copy = copy_in(s2.at[:, HALO - reach : HALO + BLOCK + reach], s2_hbm, sem)
    count = Q1 - 2 - 2 * t

    def third(p):
        a = 2 * (p + 1 + t) + 1
        return [
            (
                t_ref,
                (case, p),
                (r_ref[case, a] - apply_plane(s2, case, a, c0, a))
                + (r_ref[case, a + 1] - apply_plane(s2, case, a + 1, c0, a + 1)),
            )
            for case in range(2)
        ]

    planes(0, count, third, 4)
    fine_to_level1(t_ref, r1_out, work, count, 1 + t)

    c = tuple(c1[k] for k in range(COUNT))
    lo, hi = 1 + t, Q1 - 1 - t
    forcing = r1_out[lo:hi]
    smoothed = c[WEIGHT][lo:hi] * forcing
    leftover = forcing - apply(smoothed, cut(c, lo, hi), z_prev, z_next)
    relaxed = (smoothed + c[WEIGHT][lo:hi] * leftover)[1:-1]
    s21_out[...] = relaxed
    lo, hi = QB - 1, QB + 5
    inner = relaxed[lo - 2 - t : hi - 2 - t]
    rest = (r1_out[lo:hi] - apply(inner, cut(c, lo, hi), z_prev, z_next))[1:5]
    low, high = rest[0] + rest[1], rest[2] + rest[3]
    mixed = dot(low, half_to_quarter(0)) + dot(high, half_to_quarter(1))
    summed = pairs_of_rows(mixed[None], work)[0]
    work[0:12, :] = summed
    at = 10
    for row in rows:
        work[at : at + row.shape[0], :] = row
        at += row.shape[0]
    tile = work[0 : talk.shape[1], :]
    talk[...] = jnp.broadcast_to(tile[None], talk.shape)
    return copy


COUNT_ROWS = 8 * -(-WINDOW * NY // 32)


def count_kernel(me, index, out, acc, flat):
    base = (me[0] * BLOCK - HALO) * NY
    chunk = 512
    total = index.shape[1]
    for case in range(2):
        acc[...] = jnp.zeros_like(acc)

        def step(i, carry):
            ids = index[pl.ds(case, 1), pl.ds(pl.multiple_of(i * chunk, chunk), chunk)]
            row = (ids >> 7) - base
            col = (ids & 127) + 128 * (row & 3)
            hit_row = jnp.where(iota((COUNT_ROWS, chunk), 0) == (row >> 2), 1.0, 0.0).astype(jnp.bfloat16)
            hit_col = jnp.where(iota((512, chunk), 0) == col, 1.0, 0.0).astype(jnp.bfloat16)
            acc[...] += lax.dot_general(
                hit_row, hit_col, (((1,), (1,)), ((), ())), preferred_element_type=F32
            )
            return carry

        lax.fori_loop(0, total // chunk, step, 0)
        for low in range(4):
            flat[pl.ds(low, COUNT_ROWS, stride=4), :] = acc[:, 128 * low : 128 * (low + 1)]
        out[case] = flat[0 : WINDOW * NY, :].reshape(WINDOW, NY, 128)


def neighbours_x(p):
    lane = iota(p.shape, 1)
    return jnp.where(lane > 0, roll(p, 1, 1), 0.0) + jnp.where(lane < NX - 1, roll(p, -1, 1), 0.0)


def neighbours_y(p):
    row = iota(p.shape, 0)
    return jnp.where(row > 0, roll(p, 1, 0), 0.0) + jnp.where(row < NY - 1, roll(p, -1, 0), 0.0)


def filter_parts(p):
    sides_y = neighbours_y(p)
    cross = neighbours_x(p) + sides_y
    return cross, 1.5 * p + 0.5 * cross + EDGE_WEIGHT * neighbours_x(sides_y)


def weight_of(me, members, z):
    at = me * BLOCK + z
    lane, row = iota((NY, NX), 1), iota((NY, NX), 0)
    nx = (lane > 0).astype(F32) + (lane < NX - 1).astype(F32)
    ny = (row > 0).astype(F32) + (row < NY - 1).astype(F32)
    nz = jnp.where(at > 0, 1.0, 0.0) + jnp.where(at < members * BLOCK - 1, 1.0, 0.0)
    return 1.5 + 0.5 * (nx + ny + nz) + EDGE_WEIGHT * (nx * ny + nx * nz + ny * nz)


NEAR, AWAY = 3 * BLOCK, 3 * NEXT + 1


def collect_kernel(
    case_ref, design_hbm, passive_hbm, fixed_hbm, own, near, head, tail, all_head, all_tail, design, passive, fixed, sems
):
    pairs = ((design_hbm, design), (passive_hbm, passive), (fixed_hbm, fixed))
    copies = [copy_in(a, b, sems.at[i]) for i, (a, b) in enumerate(pairs)]
    for copy in copies:
        copy.wait()
    at = 0
    for k, source in enumerate((design, passive, fixed)):
        value = source[...].astype(F32)
        own[k * BLOCK : (k + 1) * BLOCK] = value
        count = NEXT + 1 if k == 0 else NEXT
        all_head[at : at + count] = value[0:count]
        all_tail[at : at + count] = value[BLOCK - count : BLOCK]
        at += count
    case = case_ref[0]
    near[...] = own[pl.ds(case * (NEAR // 2), NEAR // 2)]
    head[...] = all_head[pl.ds(case * (AWAY // 2), AWAY // 2)]
    tail[...] = all_tail[pl.ds(case * (AWAY // 2), AWAY // 2)]


def setup_kernel(
    members, me_ref, case_ref, own, before, after, before2, after2, o_before, o_after, o_before2, o_after2, counts,
    c0_hbm, c1_hbm, force_hbm, s2_hbm, s21, r1_out, talk, mod_hbm, free_hbm, scale_hbm,
    near_b, near_a, away_b, away_a,
    raw, cross, base, c0, c1, force, mod, free, scale, s1, s2, t_ref, work, small, sems,
):
    me, case = me_ref[0], case_ref[0]
    halves = (
        (near_b, before, o_before),
        (near_a, after, o_after),
        (away_b, before2, o_before2),
        (away_a, after2, o_after2),
    )
    for target, mine, other in halves:
        half = mine.shape[0]
        target[pl.ds(case * half, half)] = mine[...]
        target[pl.ds((1 - case) * half, half)] = other[...]
    start = 0
    for source, count in ((away_b, NEXT + 1), (near_b, BLOCK), (own, BLOCK), (near_a, BLOCK), (away_a, NEXT + 1)):
        raw[start : start + count] = source[0:count]
        start += count

    def parts(k):
        a, b = filter_parts(raw[k])
        return [(cross, (k,), a), (base, (k,), b)]

    planes(0, WINDOW + 2, parts, 6)

    def material(j, passive, fixed, near):
        z = j - HALO
        at = me * BLOCK + z
        inside = jnp.where((at >= 0) & (at < members * BLOCK), 1.0, 0.0)
        filtered = base[j + 1] + 0.5 * (raw[j] + raw[j + 2]) + EDGE_WEIGHT * (cross[j] + cross[j + 2])
        weight = weight_of(me, members, z)
        density = jnp.where(passive == 1.0, 1.0, jnp.where(passive == 2.0, 0.0, filtered / weight))
        modulus = E_MIN + (1.0 - E_MIN) * density * density * density
        freedom = inside * (1.0 - fixed)
        writes = [(mod, (j,), inside * modulus), (free, (j,), freedom)]
        writes += [(force, (case, j), freedom * (HEAT_SOURCE + counts[case, j])) for case in range(2)]
        if near:
            gradient = (-1.5 * (1.0 - E_MIN)) * density * density / (modulus * weight)
            gradient = jnp.where(passive == 0.0, inside * gradient, 0.0)
            writes.append((scale, (j - HALO + 1,), gradient))
        return writes

    def stretch(source, first, second, j0, lo, hi, near=False):
        planes(lo, hi, lambda j: material(j, source[first + j - j0], source[second + j - j0], near), 5)

    stretch(away_b, NEXT + 1, 2 * NEXT + 1, 0, 0, NEXT)
    stretch(near_b, BLOCK, 2 * BLOCK, NEXT, NEXT, HALO - 1)
    stretch(near_b, BLOCK, 2 * BLOCK, NEXT, HALO - 1, HALO, True)
    stretch(own, BLOCK, 2 * BLOCK, HALO, HALO, HALO + BLOCK, True)
    stretch(near_a, BLOCK, 2 * BLOCK, HALO + BLOCK, HALO + BLOCK, HALO + BLOCK + 1, True)
    stretch(near_a, BLOCK, 2 * BLOCK, HALO + BLOCK, HALO + BLOCK + 1, HALO + 2 * BLOCK)
    stretch(away_a, NEXT + 1, 2 * NEXT + 1, HALO + 2 * BLOCK, HALO + 2 * BLOCK, WINDOW)
    near = slice(HALO - 2, HALO + BLOCK + 2)
    copies = [
        copy_in(force, force_hbm, sems.at[0]),
        copy_in(mod.at[near], mod_hbm, sems.at[1]),
        copy_in(free.at[near], free_hbm, sems.at[2]),
        copy_in(scale, scale_hbm, sems.at[3]),
    ]

    lane, row = iota((NY, NX), 1), iota((NY, NX), 0)
    zero = jnp.zeros((NY, NX), F32)

    def coefficients(j):
        m, f = mod[j], free[j]
        total, held = zero, zero
        writes = []
        for dim, mask, slot in ((1, lane > 0, 0), (0, row > 0, 2)):
            k = jnp.where(mask, jnp.sqrt(m * roll(m, 1, dim)), 0.0)
            ka = roll(k, -1, dim)
            fp = roll(f, 1, dim)
            total = total + k + ka
            held = held + k * (1.0 - fp) + ka * (1.0 - roll(f, -1, dim))
            inner = k * f * fp
            writes += [(c0, (slot, j), inner), (c0, (slot + 1, j), roll(inner, -1, dim))]
        k, ka = jnp.sqrt(m * mod[j - 1]), jnp.sqrt(m * mod[j + 1])
        total = total + k + ka
        held = held + k * (1.0 - free[j - 1]) + ka * (1.0 - free[j + 1])
        writes.append((c0, (Z0, j), k * f * free[j - 1]))
        writes.append((c0, (REST0, j), f * held + (1.0 - f)))
        writes.append((c0, (WEIGHT0, j), OMEGA / (f * total + (1.0 - f))))
        return writes

    planes(1, WINDOW - 1, coefficients, 4)
    last = WINDOW - 1
    for slot in range(COUNT0):
        c0[slot, 0] = zero
        c0[slot, last] = zero
    c0[Z0, last] = jnp.sqrt(mod[last] * mod[last - 1]) * free[last] * free[last - 1]
    copies.append(copy_in(c0, c0_hbm, sems.at[4]))

    def join(q):
        return [(t_ref, (k, q), x[2 * q + 1] + x[2 * q + 2]) for k, x in enumerate((mod, free))]

    planes(0, Q1, join)
    fine_to_level1(t_ref, small, work, Q1, 0)
    both = small[...]
    second = iota(both.shape, 2) >= 64
    both = jnp.where(second, (both > 0.0).astype(F32), 0.125 * both)
    turned = roll(both, 64, 2)
    m1 = jnp.where(second, turned, both)
    f1 = jnp.where(second, both, turned)
    for k, value in enumerate(couple(m1, f1, 2.0, 64, z_prev, z_next)):
        c1[k] = value
    copies.append(copy_in(c1, c1_hbm, sems.at[5]))

    low, high = both[QB] + both[QB + 1], both[QB + 2] + both[QB + 3]
    mixed = dot(low, half_to_quarter(0)) + dot(high, half_to_quarter(1))
    coarse = pairs_of_rows(mixed[None], work)[0]
    is_free = (iota(coarse.shape, 1) & 32) > 0
    coarse = jnp.where(is_free, (coarse > 0.0).astype(F32), 0.125 * coarse)

    rows = (coarse, jnp.zeros((2, 128), F32))
    copies.append(down(force, c0, c1, s1, s2, t_ref, work, s2_hbm, sems.at[6], 2, rows, s21, r1_out, talk))
    for copy in copies:
        copy.wait()


def coarse_window(me, gathered, lo, hi):
    members = gathered.shape[0]
    tiles = []
    for d in range(ND):
        at = me + d - REACH
        inside = jnp.where((at >= 0) & (at < members), 1.0, 0.0)
        tiles.append(inside * gathered[jnp.clip(at, 0, members - 1), lo:hi, :])
    return jnp.stack(tiles, axis=0)


def coarse_setup(me, gathered, c2, c3, work, wide):
    wide[...] = jnp.zeros_like(wide)
    wide[:, 0:10, :] = coarse_window(me, gathered, 10, 20)
    both = wide[...]
    is_free = (iota(both.shape, 2) & 32) > 0
    m = jnp.where(is_free, roll(both, 32, 2), both)
    f = jnp.where(is_free, both, roll(both, -32, 2))
    for k, value in enumerate(couple(m, f, 4.0, 32, z_prev2, z_next2)):
        c2[k] = value
    eighth = quarter_to_eighth()
    m3 = 0.125 * pairs_of_rows(flat_dot(m, eighth), work)
    f3 = (pairs_of_rows(flat_dot(f, eighth), work) > 0.0).astype(F32)
    for k, value in enumerate(couple(m3, f3, 8.0, 16, z_prev, z_next)):
        c3[k] = value


def coarse_solve(r2, c2, c3, work):
    c = tuple(c2[k] for k in range(COUNT))
    smoothed = c[WEIGHT] * r2
    relaxed = smoothed + c[WEIGHT] * (r2 - apply(smoothed, c, z_prev2, z_next2))
    leftover = (r2 - apply(relaxed, c, z_prev2, z_next2))[2 : ND - 2]
    forcing = pairs_of_rows(flat_dot(leftover, quarter_to_eighth()), work)
    lo, hi = 2, ND - 2
    v = c3[WEIGHT, lo:hi] * forcing
    for _ in range(7):
        ck = tuple(c3[k, lo:hi] for k in range(COUNT))
        v = v + ck[WEIGHT] * (forcing - apply(v, ck, z_prev, z_next))
        v, forcing = v[1:-1], forcing[1:-1]
        lo, hi = lo + 1, hi - 1
    up = rows_twice(flat_dot(v, eighth_to_quarter()), work)
    lo, hi = REACH - 2, REACH + 3
    v = relaxed[lo:hi] + up
    ck = cut(c, lo, hi)
    for _ in range(2):
        v = v + ck[WEIGHT] * (r2[lo:hi] - apply(v, ck, z_prev2, z_next2))
    return v[1:4]


def level1_up(e2, relaxed, forcing, c, work):
    parts = []
    for low in range(2):
        lanes = flat_dot(e2, quarter_to_half(low))
        parts.append(rows_twice(lanes, work)[:, :R1])
    lifted = [parts[z & 1][z >> 1] for z in range(6)]
    n = relaxed.shape[0]
    lead = (12 - n) // 2
    v = relaxed + jnp.stack([lifted[(q + lead) // 2] for q in range(n)], axis=0)
    for _ in range(2):
        v = (v + c[WEIGHT] * (forcing - apply(v, c, z_prev, z_next)))[1:-1]
        forcing, c = forcing[1:-1], cut(c, 1, -1)
    return v


def level0_up(v1, s2, r, vb, c0, out, work):
    count = v1.shape[0]
    for case in range(2):
        lanes = flat_dot(v1, half_to_fine(case))
        put_rows_twice(lanes, work)
        for p in range(count):
            fine = work[p * 2 * R1 : p * 2 * R1 + NY, :]
            s2[case, 2 * p] = s2[case, 2 * p] + fine
            s2[case, 2 * p + 1] = s2[case, 2 * p + 1] + fine
    total = s2.shape[1]

    def sweep(v, case, i):
        return v[case, i] + c0[WEIGHT0, i] * (r[case, i - 1] - apply_plane(v, case, i, c0, i))

    def once(i):
        return [(vb, (case, i), sweep(s2, case, i)) for case in range(2)]

    planes(1, total - 1, once, 7 if total == 16 else 5)

    def twice(i):
        return [(out, (case, i - 2), sweep(vb, case, i)) for case in range(2)]

    planes(2, total - 2, twice, 6 if total == 16 else 8)


def add_up(parts):
    while len(parts) > 1:
        parts = [sum(parts[i : i + 2][1:], parts[i]) for i in range(0, len(parts), 2)]
    return parts[0]


def sum_of_rows(gathered, lo, hi):
    return add_up([gathered[d, lo:hi, :] for d in range(gathered.shape[0])])


def residual_window(me, gathered):
    r2 = coarse_window(me, gathered, 0, 16)
    return jnp.where(iota(r2.shape, 1) < 10, r2, 0.0)


def around(reach):
    return slice(HALO - reach, HALO + BLOCK + reach)


def up_kernel(first, me_ref, gathered, r_hbm, s2_hbm, s21, r1_ref, c0_hbm, c1_hbm, *rest):
    if first:
        out, head, tail, c2, c3, s2, r, c0, c1, vb, work, wide, sems = rest
    else:
        c2, c3, out, head, tail, dots, s2, r, c0, c1, vb, work, wide, sems = rest
    sources = (
        (s2_hbm, s2),
        (r_hbm.at[:, around(1)], r),
        (c0_hbm.at[:, around(2)], c0),
        (c1_hbm.at[:, 3:13], c1),
    )
    copies = [copy_in(a, b, sems.at[i]) for i, (a, b) in enumerate(sources)]
    me = me_ref[0]
    if first:
        coarse_setup(me, gathered, c2, c3, work, wide)
    else:
        dots[...] = sum_of_rows(gathered, 8, 16)
    e2 = coarse_solve(residual_window(me, gathered), c2, c3, work)
    for copy in copies:
        copy.wait()
    v1 = level1_up(e2, s21[...], r1_ref[3:13], tuple(c1[k] for k in range(COUNT)), work)

    level0_up(v1, s2, r, vb, c0, out, work)
    for case in range(2):
        head[case] = out[case, 0:NEXT]
        tail[case] = out[case, BLOCK - NEXT : BLOCK]


def lay_out(win, own, before, after, before2, after2):
    start = 0
    for source in (before2, before, own, after, after2):
        count = source.shape[1]
        for case in range(2):
            win[case, start : start + count] = source[case]
        start += count


def dot_rows(values):
    lane = iota((1, 128), 1)
    rows = []
    for a, b in values:
        rows.append(jnp.where(lane < 64, jnp.sum(a, keepdims=True), jnp.sum(b, keepdims=True)))
    return rows


def accumulate(count, term):
    sums = []
    for case in range(2):
        terms = [term(case, k) for k in range(BLOCK)]
        sums.append([add_up([t[i] for t in terms]) for i in range(count)])
    return dot_rows([(sums[0][i], sums[1][i]) for i in range(count)])


def first_kernel(
    own, before, after, before2, after2, force_hbm, c0, c1,
    u_hbm, w_hbm, s2_hbm, s21, r1_out, talk,
    u_win, w_win, force, s1, s2, t_ref, work, sems,
):
    copy_f = copy_in(force_hbm.at[:, around(0)], force, sems.at[0])
    lay_out(u_win, own, before, after, before2, after2)
    copies = [copy_in(u_win.at[:, around(2)], u_hbm, sems.at[1])]

    def image(j):
        return [(w_win, (case, j), apply_plane(u_win, case, j, c0, j)) for case in range(2)]

    planes(1, WINDOW - 1, image)
    copies.append(copy_in(w_win, w_hbm, sems.at[2]))
    copy_f.wait()

    def term(case, k):
        u = own[case, k]
        return (force[case, k] * u, w_win[case, HALO + k] * u)

    rows = accumulate(2, term) + [jnp.zeros((4, 128), F32)]
    copies.append(down(w_win, c0, c1, s1, s2, t_ref, work, s2_hbm, sems.at[3], 2, rows, s21, r1_out, talk))
    for copy in copies:
        copy.wait()


def of_case(row, case):
    return row[:, 64 * case : 64 * case + 1]


def second_kernel(
    own, before, after, before2, after2, dots0, force_hbm, u0_hbm, w0_hbm, c0, c1,
    m_hbm, u1_hbm, w1_hbm, n0_hbm, s2_hbm, s21, r1_out, talk,
    m_win, u0, w0, n0, u1, w1, force, s1, s2, t_ref, work, sems,
):
    copy_w = copy_in(w0_hbm, w0, sems.at[0])
    copy_u = copy_in(u0_hbm, u0, sems.at[1])
    copy_f = copy_in(force_hbm.at[:, around(0)], force, sems.at[2])
    lay_out(m_win, own, before, after, before2, after2)
    copies = [copy_in(m_win.at[:, around(2)], m_hbm, sems.at[3])]
    alpha = [of_case(dots0[2:3, :] / dots0[3:4, :], case) for case in range(2)]
    copy_w.wait()

    def image(j, block=False):
        writes = []
        for case in range(2):
            n = apply_plane(m_win, case, j, c0, j)
            writes.append((w1, (case, j), w0[case, j] - alpha[case] * n))
            if block:
                writes.append((n0, (case, j - HALO), n))
        return writes

    planes(1, HALO, image, 6)
    planes(HALO, HALO + BLOCK, functools.partial(image, block=True))
    planes(HALO + BLOCK, WINDOW - 1, image, 6)
    copies.append(copy_in(n0, n0_hbm, sems.at[4]))
    copies.append(copy_in(w1, w1_hbm, sems.at[5]))
    copy_u.wait()

    def update(i):
        return [(u1, (case, i), u0[case, i] - alpha[case] * m_win[case, i + HALO - 2]) for case in range(2)]

    planes(0, BLOCK + 4, update)
    copies.append(copy_in(u1, u1_hbm, sems.at[6]))
    copy_f.wait()

    def term(case, k):
        j = HALO + k
        u, w, ww = u1[case, k + 2], w1[case, j], w0[case, j]
        r = force[case, k] - alpha[case] * ww
        return (r * u, w * u, u * ww + u0[case, k + 2] * w)

    rows = accumulate(3, term) + [jnp.zeros((3, 128), F32)]
    copies.append(down(w1, c0, c1, s1, s2, t_ref, work, s2_hbm, sems.at[7], 4, rows, s21, r1_out, talk))
    for copy in copies:
        copy.wait()


def third_kernel(
    me_ref, gathered, dots0, s21, r1_ref, c0_hbm, c1_hbm, c2, c3,
    w1_hbm, s2_hbm, force_hbm, u0_hbm, w0_hbm, m0_hbm, n0_hbm, u1_hbm,
    u2, p1, x2, talk, dots1,
    s2, w1, vb, m_win, force, u0, w0, m0, n0, u1, c0, c1, work, sems,
):
    sources = (
        (c1_hbm.at[:, 2:14], c1),
        (s2_hbm, s2),
        (c0_hbm.at[:, around(4)], c0),
        (w1_hbm.at[:, around(3)], w1),
        (force_hbm.at[:, around(0)], force),
        (u0_hbm, u0),
        (w0_hbm.at[:, around(0)], w0),
        (m0_hbm, m0),
        (n0_hbm, n0),
        (u1_hbm, u1),
    )
    copies = [copy_in(a, b, sems.at[i]) for i, (a, b) in enumerate(sources)]
    dots1[...] = sum_of_rows(gathered, 8, 16)
    e2 = coarse_solve(residual_window(me_ref[0], gathered), c2, c3, work)
    copies[0].wait()
    v1 = level1_up(e2, s21[...], r1_ref[2:14], tuple(c1[k] for k in range(COUNT)), work)

    for copy in copies[1:]:
        copy.wait()
    level0_up(v1, s2, w1, vb, c0, m_win, work)

    gamma0, delta0 = dots0[2:3, :], dots0[3:4, :]
    gamma1 = dots1[2:3, :]
    beta = gamma1 / gamma0
    curve = dots1[3:4, :] + beta * dots1[4:5, :] + beta * beta * delta0
    a0 = [of_case(gamma0 / delta0, case) for case in range(2)]
    a1 = [of_case(gamma1 / curve, case) for case in range(2)]
    b1 = [of_case(beta, case) for case in range(2)]

    def update(i):
        writes = []
        for case in range(2):
            p = u1[case, i] + b1[case] * u0[case, i]
            writes.append((p1, (case, i), p))
            writes.append((x2, (case, i), a0[case] * u0[case, i] + a1[case] * p))
            u = u1[case, i] - a1[case] * (m_win[case, i] + b1[case] * m0[case, i])
            writes.append((u2, (case, i), u))
        return writes

    planes(0, 12, update)

    def term(case, k):
        n1 = apply_plane(m_win, case, k + 2, c0, k + 4)
        ww, wv = w0[case, k], w1[case, k + 3]
        s = wv + b1[case] * ww
        w = wv - a1[case] * (n1 + b1[case] * n0[case, k])
        r = force[case, k] - a0[case] * ww - a1[case] * s
        u, p = u2[case, k + 2], p1[case, k + 2]
        return (r * u, w * u, u * s + p * w)

    rows = accumulate(3, term) + [jnp.zeros((5, 128), F32)]
    tile = jnp.concatenate(rows, axis=0)
    talk[...] = jnp.broadcast_to(tile[None], talk.shape)


def last_kernel(gathered, dots0, dots1, u2, p1, x2, mod, free, state, energy, w_win):
    total = add_up([gathered[d] for d in range(gathered.shape[0])])
    gamma0, delta0 = dots0[2:3, :], dots0[3:4, :]
    gamma1 = dots1[2:3, :]
    beta1 = gamma1 / gamma0
    curve1 = dots1[3:4, :] + beta1 * dots1[4:5, :] + beta1 * beta1 * delta0
    gamma2 = total[0:1, :]
    beta2 = gamma2 / gamma1
    curve2 = total[1:2, :] + beta2 * total[2:3, :] + beta2 * beta2 * curve1
    a2 = [of_case(gamma2 / curve2, case) for case in range(2)]
    b2 = [of_case(beta2, case) for case in range(2)]

    def update(i):
        return [
            (w_win, (case, i), x2[case, i] + a2[case] * (u2[case, i] + b2[case] * p1[case, i])) for case in range(2)
        ]

    planes(0, 12, update, 4)
    state[...] = w_win[:, 2:10]

    def hold(i):
        return [(w_win, (case, i), w_win[case, i] * free[i]) for case in range(2)]

    planes(0, 12, hold, 4)
    lane, row = iota((NY, NX), 1), iota((NY, NX), 0)

    def power(i):
        m = mod[i + 1]
        out = jnp.zeros((NY, NX), F32)
        kx = jnp.where(lane > 0, jnp.sqrt(m * roll(m, 1, 1)), 0.0)
        ky = jnp.where(row > 0, jnp.sqrt(m * roll(m, 1, 0)), 0.0)
        kz, kn = jnp.sqrt(m * mod[i]), jnp.sqrt(m * mod[i + 2])
        for case in range(2):
            v = w_win[case, i + 1]
            dx, dy = v - roll(v, 1, 1), v - roll(v, 1, 0)
            dz, dn = v - w_win[case, i], v - w_win[case, i + 2]
            px, py = kx * dx * dx, ky * dy * dy
            out = out + px + roll(px, -1, 1) + py + roll(py, -1, 0) + kz * dz * dz + kn * dn * dn
        return [(energy, (i,), out)]

    planes(0, 10, power, 5)


def sensitivity_kernel(mine, other, scale, passive, out, g, cross, base):
    def gradient(i):
        value = scale[i] * (mine[i] + other[i])
        a, b = filter_parts(value)
        return [(g, (i,), value), (cross, (i,), a), (base, (i,), b)]

    planes(0, 10, gradient, 5)

    def final(k):
        i = k + 1
        value = base[i] + 0.5 * (g[i - 1] + g[i + 1]) + EDGE_WEIGHT * (cross[i - 1] + cross[i + 1])
        return [(out, (k,), jnp.where(passive[k] == 0, value, 0.0))]

    planes(0, 8, final)


def shape(*dims):
    return jax.ShapeDtypeStruct(dims, F32)


def hbm(*dims):
    return pltpu.HBM(dims, F32), pltpu.HBM


def vmem(*dims):
    return shape(*dims), pltpu.VMEM


def call(body, outs, scratch, args, name, sems=0, cost=None):
    pairs = [a if isinstance(a, tuple) else (a, pltpu.VMEM) for a in args]
    scratches = [pltpu.VMEM(s, F32) if isinstance(s, tuple) else s for s in scratch]
    if sems:
        scratches.append(pltpu.SemaphoreType.DMA((sems,)))
    given = [pltpu.with_memory_space_constraint(a, m) if m is pltpu.HBM else a for a, m in pairs]
    return pl.pallas_call(
        body,
        out_shape=[o for o, _ in outs],
        in_specs=[pl.BlockSpec(memory_space=m) for _, m in pairs],
        out_specs=[pl.BlockSpec(memory_space=m) for _, m in outs],
        scratch_shapes=scratches,
        compiler_params=CPARAMS,
        cost_estimate=cost,
        name=name,
    )(*given)


def on_device(design, passive, fixed_mask, load_index):
    members = lax.axis_size("space")
    position = lax.axis_index("space")
    me = position.astype(jnp.int32).reshape(1)
    ahead = [(i, i + 1) for i in range(members - 1)]
    back = [(i + 1, i) for i in range(members - 1)]

    def two_either_side(own, head, tail):
        skip = [(i, i + 2) for i in range(members - 2)]
        skip_back = [(i + 2, i) for i in range(members - 2)]
        away = lax.ppermute(tail, "space", skip), lax.ppermute(head, "space", skip_back)
        return (lax.ppermute(own, "space", ahead), lax.ppermute(own, "space", back)) + away

    def gather(tiles):
        return lax.all_to_all(tiles, "space", 0, 0)

    plane = (NY, NX)
    window = (2, WINDOW) + plane
    block = (2, BLOCK) + plane
    wide = (2, BLOCK + 4) + plane
    wider = (2, BLOCK + 8) + plane
    work = (800, 128)
    t_shape = (2, Q1) + plane
    position_ref = (me, pltpu.SMEM)

    def down_outs(reach, count):
        near = 2 + reach // 2
        return [
            hbm(2, BLOCK + 2 * reach, *plane),
            vmem(4 + 2 * near, R1, 128),
            vmem(Q1, R1, 128),
            vmem(members, count, 128),
        ]

    def far(x):
        return (x, pltpu.HBM)

    case_ref = (lax.axis_index("case").astype(jnp.int32).reshape(1), pltpu.SMEM)
    own, near, head, tail = call(
        collect_kernel,
        [vmem(NEAR, *plane), vmem(NEAR // 2, *plane), vmem(AWAY // 2, *plane), vmem(AWAY // 2, *plane)],
        [(AWAY,) + plane] * 2 + [pltpu.VMEM((BLOCK,) + plane, x.dtype) for x in (design, passive, fixed_mask)],
        (case_ref, far(design), far(passive), far(fixed_mask)),
        "collect",
        3,
    )
    listened = two_either_side(near, head, tail)
    counts = call(
        count_kernel,
        [vmem(*window)],
        [(COUNT_ROWS, 512), (4 * COUNT_ROWS, 128)],
        (position_ref, load_index),
        "counts",
        cost=pl.CostEstimate(flops=3 * 10**10, bytes_accessed=10**7, transcendentals=0),
    )[0]
    listened, counts = lax.optimization_barrier((listened, counts))
    listened += tuple(lax.ppermute(x, "case", [(0, 1), (1, 0)]) for x in listened)
    c0, c1, force, s2, s21, r1, talk, mod, free, scale = call(
        functools.partial(setup_kernel, members),
        [hbm(COUNT0, WINDOW, *plane), hbm(COUNT, Q1, R1, 128), hbm(*window)]
        + down_outs(2, TALK)
        + [hbm(12, *plane), hbm(12, *plane), hbm(10, *plane)],
        [(NEAR,) + plane] * 2
        + [(AWAY,) + plane] * 2
        + [(WINDOW + 2,) + plane] * 3
        + [(COUNT0, WINDOW) + plane, (COUNT, Q1, R1, 128)]
        + [window, (WINDOW,) + plane, (WINDOW,) + plane, (10,) + plane, window, window, t_shape, work]
        + [(Q1, R1, 128)],
        (position_ref, case_ref, own) + listened + (counts,),
        "setup",
        7,
    )

    def up(first, r, s2, s21, r1, talk, more):
        args = (position_ref, gather(talk), far(r), far(s2), s21, r1, far(c0), far(c1)) + tuple(more)
        outs = [vmem(*block), vmem(2, NEXT, *plane), vmem(2, NEXT, *plane)]
        if first:
            outs += [vmem(COUNT, ND, R2, 128), vmem(COUNT, ND, R3, 128)]
        else:
            outs += [vmem(8, 128)]
        scratch = [wide, (2, 10) + plane, (COUNT0, 12) + plane, (COUNT, 10, R1, 128), wide, work, (ND, R2, 128)]
        return call(functools.partial(up_kernel, first), outs, scratch, args, "up", 4)

    u, head, tail, c2, c3 = up(True, force, s2, s21, r1, talk, ())
    u0, w0, s2, s21, r1, talk = call(
        first_kernel,
        [hbm(*wide), hbm(*window)] + down_outs(2, R2),
        [window, window, block, window, window, t_shape, work],
        (u,) + two_either_side(u, head, tail) + (far(force), c0, c1),
        "first",
        4,
    )
    m, head, tail, dots0 = up(False, w0, s2, s21, r1, talk, (c2, c3))
    m0, u1, w1, n0, s2, s21, r1, talk = call(
        second_kernel,
        [hbm(*wide), hbm(*wide), hbm(*window), hbm(*block)] + down_outs(4, R2),
        [window, wide, window, block, wide, window, block, window, window, t_shape, work],
        (m,) + two_either_side(m, head, tail) + (dots0, far(force), far(u0), far(w0), c0, c1),
        "second",
        8,
    )
    u2, p1, x2, talk, dots1 = call(
        third_kernel,
        [vmem(*wide)] * 3 + [vmem(members, 8, 128), vmem(8, 128)],
        [wider, (2, 14) + plane, wider, wide, block, wide, block, wide, block, wide]
        + [(COUNT0, 16) + plane, (COUNT, 12, R1, 128), work],
        (position_ref, gather(talk), dots0, s21, r1, far(c0), far(c1), c2, c3)
        + tuple(far(x) for x in (w1, s2, force, u0, w0, m0, n0, u1)),
        "third",
        10,
    )
    state, energy = call(
        last_kernel,
        [vmem(*block), vmem(10, *plane)],
        [wide],
        (gather(talk), dots0, dots1, u2, p1, x2, mod, free),
        "last",
    )
    other = lax.ppermute(energy, "case", [(0, 1), (1, 0)])
    sensitivity = call(
        sensitivity_kernel,
        [vmem(BLOCK, *plane)],
        [(10,) + plane] * 3,
        (energy, other, scale, passive),
        "sensitivity",
    )[0]
    return state, sensitivity


def solution(mesh):
    placed = (
        P("space", None, None),
        P("space", None, None),
        P("space", None, None),
        P("case", None),
    )
    return jax.shard_map(
        on_device,
        mesh=mesh,
        in_specs=placed,
        out_specs=(P("case", "space", None, None), P("space", None, None)),
        check_vma=False,
    )
```

```python
import functools

import jax
import jax.numpy as jnp
from jax import lax
from jax.experimental import pallas as pl
from jax.experimental.pallas import tpu as pltpu
from jax.sharding import PartitionSpec as P

ITERS = 3
E_MIN = 0.01
OMEGA = 0.8
HEAT_SOURCE = 0.05
EDGE_WEIGHT = 1.5 - 2.0**0.5

F32 = jnp.float32
NY, NX = 40, 128
BLOCK = 8
HALO = 13
NEXT = HALO - BLOCK
WINDOW = BLOCK + 2 * HALO
Q1, R1 = 16, 24
QB = 6
REACH = 11
ND = 2 * REACH + 1
R2 = 16
R3 = 8
TALK = 24
LONG = pl.CostEstimate(flops=4 * 10**10, bytes_accessed=10**8, transcendentals=0)
CPARAMS = pltpu.CompilerParams(vmem_limit_bytes=32 * 1024 * 1024)


def iota(shape, dim):
    return lax.broadcasted_iota(jnp.int32, shape, dim)


def roll(v, by, dim):
    return pltpu.roll(v, by % v.shape[dim], dim)


def dot(a, b):
    b = b.astype(jnp.bfloat16)
    out = None
    for _ in range(3):
        part = a.astype(jnp.bfloat16)
        a = a - part.astype(F32)
        product = lax.dot_general(part, b, (((1,), (0,)), ((), ())), preferred_element_type=F32)
        out = product if out is None else out + product
    return out


def planes(lo, hi, body, group=8):
    def do(js):
        writes = [w for j in js for w in body(j)]
        for ref, index, value in writes:
            ref[index] = value

    count = (hi - lo) // group
    if count == 1:
        do([lo + k for k in range(group)])
    elif count > 1:

        def step(i, carry):
            do([lo + i * group + k for k in range(group)])
            return carry

        lax.fori_loop(0, count, step, 0)
    if lo + count * group < hi:
        do(list(range(lo + count * group, hi)))


def fine_to_half(case):
    i, j = iota((128, 128), 0), iota((128, 128), 1)
    return (j == 64 * case + (i >> 1)).astype(F32)


def half_to_fine(case):
    i, j = iota((128, 128), 0), iota((128, 128), 1)
    return (i == 64 * case + (j >> 1)).astype(F32)


def half_to_quarter(low):
    i, j = iota((128, 128), 0), iota((128, 128), 1)
    return (j == 64 * low + 32 * (i >> 6) + ((i & 63) >> 1)).astype(F32)


def quarter_to_half(low):
    i, j = iota((128, 128), 0), iota((128, 128), 1)
    return (i == 64 * low + 32 * (j >> 6) + ((j & 63) >> 1)).astype(F32)


def quarter_to_eighth():
    i, j = iota((128, 128), 0), iota((128, 128), 1)
    return (j == 16 * ((i >> 5) & 1) + ((i & 31) >> 1)).astype(F32)


def eighth_to_quarter():
    i, j = iota((128, 128), 0), iota((128, 128), 1)
    return (i == 16 * ((j >> 5) & 1) + ((j & 31) >> 1)).astype(F32)


def z_prev(v):
    return jnp.concatenate([jnp.zeros_like(v[:1]), v[:-1]], axis=0)


def z_next(v):
    return jnp.concatenate([v[1:], jnp.zeros_like(v[:1])], axis=0)


def z_prev2(v):
    turned = roll(v, 64, 2)
    return jnp.where(iota(v.shape, 2) >= 64, turned, z_prev(turned))


def z_next2(v):
    turned = roll(v, 64, 2)
    return jnp.where(iota(v.shape, 2) < 64, turned, z_next(turned))


def couple(m, f, factor, width, zp, zn):
    lead = (iota(m.shape, 2) & (width - 1)) > 0
    first = iota(m.shape, 1) > 0
    sides = (
        (lambda v: roll(v, 1, 2), lambda v: roll(v, -1, 2), lead),
        (lambda v: roll(v, 1, 1), lambda v: roll(v, -1, 1), first),
        (zp, zn, None),
    )
    total = jnp.zeros_like(m)
    held = jnp.zeros_like(m)
    coupling = []
    for prev, after, mask in sides:
        k = jnp.sqrt(m * prev(m))
        if mask is not None:
            k = jnp.where(mask, k, 0.0)
        ka = after(k)
        total = total + k + ka
        held = held + k * (1.0 - prev(f)) + ka * (1.0 - after(f))
        inner = factor * k * f * prev(f)
        coupling += [inner, after(inner)]
    rest = f * factor * held + (1.0 - f)
    weight = OMEGA / (f * factor * total + (1.0 - f))
    return tuple(coupling) + (rest, weight)


COUNT = 8
REST, WEIGHT = 6, 7


def apply(v, c, zp, zn):
    out = c[REST] * v + c[0] * (v - roll(v, 1, 2)) + c[1] * (v - roll(v, -1, 2))
    out = out + c[2] * (v - roll(v, 1, 1)) + c[3] * (v - roll(v, -1, 1))
    return out + c[4] * (v - zp(v)) + c[5] * (v - zn(v))


def cut(c, lo, hi):
    return tuple(x[lo:hi] for x in c)


COUNT0 = 7
Z0, REST0, WEIGHT0 = 4, 5, 6


def apply_plane(v_ref, case, i, c_ref, j):
    v = v_ref[case, i]
    out = c_ref[REST0, j] * v + c_ref[0, j] * (v - roll(v, 1, 1)) + c_ref[1, j] * (v - roll(v, -1, 1))
    out = out + c_ref[2, j] * (v - roll(v, 1, 0)) + c_ref[3, j] * (v - roll(v, -1, 0))
    return out + c_ref[Z0, j] * (v - v_ref[case, i - 1]) + c_ref[Z0, j + 1] * (v - v_ref[case, i + 1])


def copy_in(source, target, sem):
    copy = pltpu.make_async_copy(source, target, sem)
    copy.start()
    return copy


def pairs_of_rows(v, scratch):
    n, rows, _ = v.shape
    scratch[: n * rows, :] = v.reshape(n * rows, 128)
    half = n * rows // 2
    even = scratch[pl.ds(0, half, stride=2), :]
    odd = scratch[pl.ds(1, half, stride=2), :]
    return (even + odd).reshape(n, rows // 2, 128)


def put_rows_twice(v, scratch):
    n, rows, _ = v.shape
    flat = v.reshape(n * rows, 128)
    scratch[pl.ds(0, n * rows, stride=2), :] = flat
    scratch[pl.ds(1, n * rows, stride=2), :] = flat


def rows_twice(v, scratch):
    n, rows, _ = v.shape
    put_rows_twice(v, scratch)
    return scratch[: 2 * n * rows, :].reshape(n, 2 * rows, 128)


def flat_dot(v, matrix):
    n, rows, _ = v.shape
    return dot(v.reshape(n * rows, 128), matrix).reshape(n, rows, 128)


def fine_to_level1(t_ref, r_ref, work, count, split):
    flat0 = t_ref[0, :count].reshape(count * NY, 128)
    flat1 = t_ref[1, :count].reshape(count * NY, 128)
    work[: count * NY, :] = dot(flat0, fine_to_half(0)) + dot(flat1, fine_to_half(1))
    r_ref[...] = jnp.zeros_like(r_ref)
    for p in range(count):
        even = work[pl.ds(p * NY, NY // 2, stride=2), :]
        odd = work[pl.ds(p * NY + 1, NY // 2, stride=2), :]
        r_ref[split + p, 0 : NY // 2, :] = even + odd


def down(r_ref, c0, c1, s1, s2, t_ref, work, s2_hbm, sem, reach, rows, s21_out, r1_out, talk):
    trim = 4 - reach
    t = trim // 2

    def first(j):
        return [(s1, (case, j), c0[WEIGHT0, j] * r_ref[case, j]) for case in range(2)]

    planes(1 + trim, WINDOW - 1 - trim, first)

    def second(j):
        return [
            (s2, (case, j), s1[case, j] + c0[WEIGHT0, j] * (r_ref[case, j] - apply_plane(s1, case, j, c0, j)))
            for case in range(2)
        ]

    planes(2 + trim, WINDOW - 2 - trim, second)
    copy = copy_in(s2.at[:, HALO - reach : HALO + BLOCK + reach], s2_hbm, sem)
    count = Q1 - 2 - 2 * t

    def third(p):
        a = 2 * (p + 1 + t) + 1
        return [
            (
                t_ref,
                (case, p),
                (r_ref[case, a] - apply_plane(s2, case, a, c0, a))
                + (r_ref[case, a + 1] - apply_plane(s2, case, a + 1, c0, a + 1)),
            )
            for case in range(2)
        ]

    planes(0, count, third, 4)
    fine_to_level1(t_ref, r1_out, work, count, 1 + t)

    c = tuple(c1[k] for k in range(COUNT))
    lo, hi = 1 + t, Q1 - 1 - t
    forcing = r1_out[lo:hi]
    smoothed = c[WEIGHT][lo:hi] * forcing
    leftover = forcing - apply(smoothed, cut(c, lo, hi), z_prev, z_next)
    relaxed = (smoothed + c[WEIGHT][lo:hi] * leftover)[1:-1]
    s21_out[...] = relaxed
    lo, hi = QB - 1, QB + 5
    inner = relaxed[lo - 2 - t : hi - 2 - t]
    rest = (r1_out[lo:hi] - apply(inner, cut(c, lo, hi), z_prev, z_next))[1:5]
    low, high = rest[0] + rest[1], rest[2] + rest[3]
    mixed = dot(low, half_to_quarter(0)) + dot(high, half_to_quarter(1))
    summed = pairs_of_rows(mixed[None], work)[0]
    work[0:12, :] = summed
    at = 10
    for row in rows:
        work[at : at + row.shape[0], :] = row
        at += row.shape[0]
    tile = work[0 : talk.shape[1], :]
    talk[...] = jnp.broadcast_to(tile[None], talk.shape)
    return copy


COUNT_ROWS = 8 * -(-WINDOW * NY // 32)


def count_kernel(me, index, out, acc, flat):
    base = (me[0] * BLOCK - HALO) * NY
    chunk = 512
    total = index.shape[1]
    for case in range(2):
        acc[...] = jnp.zeros_like(acc)

        def step(i, carry):
            ids = index[pl.ds(case, 1), pl.ds(pl.multiple_of(i * chunk, chunk), chunk)]
            row = (ids >> 7) - base
            col = (ids & 127) + 128 * (row & 3)
            hit_row = jnp.where(iota((COUNT_ROWS, chunk), 0) == (row >> 2), 1.0, 0.0).astype(jnp.bfloat16)
            hit_col = jnp.where(iota((512, chunk), 0) == col, 1.0, 0.0).astype(jnp.bfloat16)
            acc[...] += lax.dot_general(
                hit_row, hit_col, (((1,), (1,)), ((), ())), preferred_element_type=F32
            )
            return carry

        lax.fori_loop(0, total // chunk, step, 0)
        for low in range(4):
            flat[pl.ds(low, COUNT_ROWS, stride=4), :] = acc[:, 128 * low : 128 * (low + 1)]
        out[case] = flat[0 : WINDOW * NY, :].reshape(WINDOW, NY, 128)


def neighbours_x(p):
    lane = iota(p.shape, 1)
    return jnp.where(lane > 0, roll(p, 1, 1), 0.0) + jnp.where(lane < NX - 1, roll(p, -1, 1), 0.0)


def neighbours_y(p):
    row = iota(p.shape, 0)
    return jnp.where(row > 0, roll(p, 1, 0), 0.0) + jnp.where(row < NY - 1, roll(p, -1, 0), 0.0)


def filter_parts(p):
    sides_y = neighbours_y(p)
    cross = neighbours_x(p) + sides_y
    return cross, 1.5 * p + 0.5 * cross + EDGE_WEIGHT * neighbours_x(sides_y)


def weight_of(me, members, z):
    at = me * BLOCK + z
    lane, row = iota((NY, NX), 1), iota((NY, NX), 0)
    nx = (lane > 0).astype(F32) + (lane < NX - 1).astype(F32)
    ny = (row > 0).astype(F32) + (row < NY - 1).astype(F32)
    nz = jnp.where(at > 0, 1.0, 0.0) + jnp.where(at < members * BLOCK - 1, 1.0, 0.0)
    return 1.5 + 0.5 * (nx + ny + nz) + EDGE_WEIGHT * (nx * ny + nx * nz + ny * nz)


NEAR, AWAY = 3 * BLOCK, 3 * NEXT + 1


def collect_kernel(
    case_ref, design_hbm, passive_hbm, fixed_hbm, own, near, head, tail, all_head, all_tail, design, passive, fixed, sems
):
    pairs = ((design_hbm, design), (passive_hbm, passive), (fixed_hbm, fixed))
    copies = [copy_in(a, b, sems.at[i]) for i, (a, b) in enumerate(pairs)]
    for copy in copies:
        copy.wait()
    at = 0
    for k, source in enumerate((design, passive, fixed)):
        value = source[...].astype(F32)
        own[k * BLOCK : (k + 1) * BLOCK] = value
        count = NEXT + 1 if k == 0 else NEXT
        all_head[at : at + count] = value[0:count]
        all_tail[at : at + count] = value[BLOCK - count : BLOCK]
        at += count
    case = case_ref[0]
    near[...] = own[pl.ds(case * (NEAR // 2), NEAR // 2)]
    head[...] = all_head[pl.ds(case * (AWAY // 2), AWAY // 2)]
    tail[...] = all_tail[pl.ds(case * (AWAY // 2), AWAY // 2)]


def setup_kernel(
    members, me_ref, case_ref, own, before, after, before2, after2, o_before, o_after, o_before2, o_after2, counts,
    c0_hbm, c1_hbm, force_hbm, s2_hbm, s21, r1_out, talk, mod_hbm, free_hbm, scale_hbm,
    near_b, near_a, away_b, away_a,
    raw, cross, base, c0, c1, force, mod, free, scale, s1, s2, t_ref, work, small, sems,
):
    me, case = me_ref[0], case_ref[0]
    halves = (
        (near_b, before, o_before),
        (near_a, after, o_after),
        (away_b, before2, o_before2),
        (away_a, after2, o_after2),
    )
    for target, mine, other in halves:
        half = mine.shape[0]
        target[pl.ds(case * half, half)] = mine[...]
        target[pl.ds((1 - case) * half, half)] = other[...]
    start = 0
    for source, count in ((away_b, NEXT + 1), (near_b, BLOCK), (own, BLOCK), (near_a, BLOCK), (away_a, NEXT + 1)):
        raw[start : start + count] = source[0:count]
        start += count

    def parts(k):
        a, b = filter_parts(raw[k])
        return [(cross, (k,), a), (base, (k,), b)]

    planes(0, WINDOW + 2, parts, 6)

    def material(j, passive, fixed, near):
        z = j - HALO
        at = me * BLOCK + z
        inside = jnp.where((at >= 0) & (at < members * BLOCK), 1.0, 0.0)
        filtered = base[j + 1] + 0.5 * (raw[j] + raw[j + 2]) + EDGE_WEIGHT * (cross[j] + cross[j + 2])
        weight = weight_of(me, members, z)
        density = jnp.where(passive == 1.0, 1.0, jnp.where(passive == 2.0, 0.0, filtered / weight))
        modulus = E_MIN + (1.0 - E_MIN) * density * density * density
        freedom = inside * (1.0 - fixed)
        writes = [(mod, (j,), inside * modulus), (free, (j,), freedom)]
        writes += [(force, (case, j), freedom * (HEAT_SOURCE + counts[case, j])) for case in range(2)]
        if near:
            gradient = (-1.5 * (1.0 - E_MIN)) * density * density / (modulus * weight)
            gradient = jnp.where(passive == 0.0, inside * gradient, 0.0)
            writes.append((scale, (j - HALO + 1,), gradient))
        return writes

    def stretch(source, first, second, j0, lo, hi, near=False):
        planes(lo, hi, lambda j: material(j, source[first + j - j0], source[second + j - j0], near), 5)

    stretch(away_b, NEXT + 1, 2 * NEXT + 1, 0, 0, NEXT)
    stretch(near_b, BLOCK, 2 * BLOCK, NEXT, NEXT, HALO - 1)
    stretch(near_b, BLOCK, 2 * BLOCK, NEXT, HALO - 1, HALO, True)
    stretch(own, BLOCK, 2 * BLOCK, HALO, HALO, HALO + BLOCK, True)
    stretch(near_a, BLOCK, 2 * BLOCK, HALO + BLOCK, HALO + BLOCK, HALO + BLOCK + 1, True)
    stretch(near_a, BLOCK, 2 * BLOCK, HALO + BLOCK, HALO + BLOCK + 1, HALO + 2 * BLOCK)
    stretch(away_a, NEXT + 1, 2 * NEXT + 1, HALO + 2 * BLOCK, HALO + 2 * BLOCK, WINDOW)
    near = slice(HALO - 2, HALO + BLOCK + 2)
    copies = [
        copy_in(force, force_hbm, sems.at[0]),
        copy_in(mod.at[near], mod_hbm, sems.at[1]),
        copy_in(free.at[near], free_hbm, sems.at[2]),
        copy_in(scale, scale_hbm, sems.at[3]),
    ]

    lane, row = iota((NY, NX), 1), iota((NY, NX), 0)
    zero = jnp.zeros((NY, NX), F32)

    def coefficients(j):
        m, f = mod[j], free[j]
        total, held = zero, zero
        writes = []
        for dim, mask, slot in ((1, lane > 0, 0), (0, row > 0, 2)):
            k = jnp.where(mask, jnp.sqrt(m * roll(m, 1, dim)), 0.0)
            ka = roll(k, -1, dim)
            fp = roll(f, 1, dim)
            total = total + k + ka
            held = held + k * (1.0 - fp) + ka * (1.0 - roll(f, -1, dim))
            inner = k * f * fp
            writes += [(c0, (slot, j), inner), (c0, (slot + 1, j), roll(inner, -1, dim))]
        k, ka = jnp.sqrt(m * mod[j - 1]), jnp.sqrt(m * mod[j + 1])
        total = total + k + ka
        held = held + k * (1.0 - free[j - 1]) + ka * (1.0 - free[j + 1])
        writes.append((c0, (Z0, j), k * f * free[j - 1]))
        writes.append((c0, (REST0, j), f * held + (1.0 - f)))
        writes.append((c0, (WEIGHT0, j), OMEGA / (f * total + (1.0 - f))))
        return writes

    planes(1, WINDOW - 1, coefficients, 4)
    last = WINDOW - 1
    for slot in range(COUNT0):
        c0[slot, 0] = zero
        c0[slot, last] = zero
    c0[Z0, last] = jnp.sqrt(mod[last] * mod[last - 1]) * free[last] * free[last - 1]
    copies.append(copy_in(c0, c0_hbm, sems.at[4]))

    def join(q):
        return [(t_ref, (k, q), x[2 * q + 1] + x[2 * q + 2]) for k, x in enumerate((mod, free))]

    planes(0, Q1, join)
    fine_to_level1(t_ref, small, work, Q1, 0)
    both = small[...]
    second = iota(both.shape, 2) >= 64
    both = jnp.where(second, (both > 0.0).astype(F32), 0.125 * both)
    turned = roll(both, 64, 2)
    m1 = jnp.where(second, turned, both)
    f1 = jnp.where(second, both, turned)
    for k, value in enumerate(couple(m1, f1, 2.0, 64, z_prev, z_next)):
        c1[k] = value
    copies.append(copy_in(c1, c1_hbm, sems.at[5]))

    low, high = both[QB] + both[QB + 1], both[QB + 2] + both[QB + 3]
    mixed = dot(low, half_to_quarter(0)) + dot(high, half_to_quarter(1))
    coarse = pairs_of_rows(mixed[None], work)[0]
    is_free = (iota(coarse.shape, 1) & 32) > 0
    coarse = jnp.where(is_free, (coarse > 0.0).astype(F32), 0.125 * coarse)

    rows = (coarse, jnp.zeros((2, 128), F32))
    copies.append(down(force, c0, c1, s1, s2, t_ref, work, s2_hbm, sems.at[6], 2, rows, s21, r1_out, talk))
    for copy in copies:
        copy.wait()


def coarse_window(me, gathered, lo, hi):
    members = gathered.shape[0]
    tiles = []
    for d in range(ND):
        at = me + d - REACH
        inside = jnp.where((at >= 0) & (at < members), 1.0, 0.0)
        tiles.append(inside * gathered[jnp.clip(at, 0, members - 1), lo:hi, :])
    return jnp.stack(tiles, axis=0)


def coarse_setup(me, gathered, c2, c3, work, wide):
    wide[...] = jnp.zeros_like(wide)
    wide[:, 0:10, :] = coarse_window(me, gathered, 10, 20)
    both = wide[...]
    is_free = (iota(both.shape, 2) & 32) > 0
    m = jnp.where(is_free, roll(both, 32, 2), both)
    f = jnp.where(is_free, both, roll(both, -32, 2))
    for k, value in enumerate(couple(m, f, 4.0, 32, z_prev2, z_next2)):
        c2[k] = value
    eighth = quarter_to_eighth()
    m3 = 0.125 * pairs_of_rows(flat_dot(m, eighth), work)
    f3 = (pairs_of_rows(flat_dot(f, eighth), work) > 0.0).astype(F32)
    for k, value in enumerate(couple(m3, f3, 8.0, 16, z_prev, z_next)):
        c3[k] = value


def coarse_solve(r2, c2, c3, work):
    c = tuple(c2[k] for k in range(COUNT))
    smoothed = c[WEIGHT] * r2
    relaxed = smoothed + c[WEIGHT] * (r2 - apply(smoothed, c, z_prev2, z_next2))
    leftover = (r2 - apply(relaxed, c, z_prev2, z_next2))[2 : ND - 2]
    forcing = pairs_of_rows(flat_dot(leftover, quarter_to_eighth()), work)
    lo, hi = 2, ND - 2
    v = c3[WEIGHT, lo:hi] * forcing
    for _ in range(7):
        ck = tuple(c3[k, lo:hi] for k in range(COUNT))
        v = v + ck[WEIGHT] * (forcing - apply(v, ck, z_prev, z_next))
        v, forcing = v[1:-1], forcing[1:-1]
        lo, hi = lo + 1, hi - 1
    up = rows_twice(flat_dot(v, eighth_to_quarter()), work)
    lo, hi = REACH - 2, REACH + 3
    v = relaxed[lo:hi] + up
    ck = cut(c, lo, hi)
    for _ in range(2):
        v = v + ck[WEIGHT] * (r2[lo:hi] - apply(v, ck, z_prev2, z_next2))
    return v[1:4]


def level1_up(e2, relaxed, forcing, c, work):
    parts = []
    for low in range(2):
        lanes = flat_dot(e2, quarter_to_half(low))
        parts.append(rows_twice(lanes, work)[:, :R1])
    lifted = [parts[z & 1][z >> 1] for z in range(6)]
    n = relaxed.shape[0]
    lead = (12 - n) // 2
    v = relaxed + jnp.stack([lifted[(q + lead) // 2] for q in range(n)], axis=0)
    for _ in range(2):
        v = (v + c[WEIGHT] * (forcing - apply(v, c, z_prev, z_next)))[1:-1]
        forcing, c = forcing[1:-1], cut(c, 1, -1)
    return v


def level0_up(v1, s2, r, vb, c0, out, work):
    count = v1.shape[0]
    for case in range(2):
        lanes = flat_dot(v1, half_to_fine(case))
        put_rows_twice(lanes, work)
        for p in range(count):
            fine = work[p * 2 * R1 : p * 2 * R1 + NY, :]
            s2[case, 2 * p] = s2[case, 2 * p] + fine
            s2[case, 2 * p + 1] = s2[case, 2 * p + 1] + fine
    total = s2.shape[1]

    def sweep(v, case, i):
        return v[case, i] + c0[WEIGHT0, i] * (r[case, i - 1] - apply_plane(v, case, i, c0, i))

    def once(i):
        return [(vb, (case, i), sweep(s2, case, i)) for case in range(2)]

    planes(1, total - 1, once, 7 if total == 16 else 5)

    def twice(i):
        return [(out, (case, i - 2), sweep(vb, case, i)) for case in range(2)]

    planes(2, total - 2, twice, 6 if total == 16 else 8)


def add_up(parts):
    while len(parts) > 1:
        parts = [sum(parts[i : i + 2][1:], parts[i]) for i in range(0, len(parts), 2)]
    return parts[0]


def sum_of_rows(gathered, lo, hi):
    return add_up([gathered[d, lo:hi, :] for d in range(gathered.shape[0])])


def residual_window(me, gathered):
    r2 = coarse_window(me, gathered, 0, 16)
    return jnp.where(iota(r2.shape, 1) < 10, r2, 0.0)


def around(reach):
    return slice(HALO - reach, HALO + BLOCK + reach)


def pass_kernel(source, target):
    target[...] = source[...]


def up_kernel(first, me_ref, gathered, r_hbm, s2_hbm, s21, r1_ref, c0_hbm, c1_hbm, *rest):
    if first:
        out, head, tail, c2, c3, s2, r, c0, c1, vb, work, wide, sems = rest
    else:
        c2, c3, out, head, tail, dots, s2, r, c0, c1, vb, work, wide, sems = rest
    sources = (
        (s2_hbm, s2),
        (r_hbm.at[:, around(1)], r),
        (c0_hbm.at[:, around(2)], c0),
        (c1_hbm.at[:, 3:13], c1),
    )
    copies = [copy_in(a, b, sems.at[i]) for i, (a, b) in enumerate(sources)]
    me = me_ref[0]
    if first:
        coarse_setup(me, gathered, c2, c3, work, wide)
    else:
        dots[...] = sum_of_rows(gathered, 8, 16)
    e2 = coarse_solve(residual_window(me, gathered), c2, c3, work)
    for copy in copies:
        copy.wait()
    v1 = level1_up(e2, s21[...], r1_ref[3:13], tuple(c1[k] for k in range(COUNT)), work)

    level0_up(v1, s2, r, vb, c0, out, work)
    for case in range(2):
        head[case] = out[case, 0:NEXT]
        tail[case] = out[case, BLOCK - NEXT : BLOCK]


def lay_out(win, own, before, after, before2, after2):
    start = 0
    for source in (before2, before, own, after, after2):
        count = source.shape[1]
        for case in range(2):
            win[case, start : start + count] = source[case]
        start += count


def dot_rows(values):
    lane = iota((1, 128), 1)
    rows = []
    for a, b in values:
        rows.append(jnp.where(lane < 64, jnp.sum(a, keepdims=True), jnp.sum(b, keepdims=True)))
    return rows


def accumulate(count, term):
    sums = []
    for case in range(2):
        terms = [term(case, k) for k in range(BLOCK)]
        sums.append([add_up([t[i] for t in terms]) for i in range(count)])
    return dot_rows([(sums[0][i], sums[1][i]) for i in range(count)])


def first_kernel(
    own, before, after, before2, after2, force_hbm, c0, c1,
    u_hbm, w_hbm, s2_hbm, s21, r1_out, talk,
    u_win, w_win, force, s1, s2, t_ref, work, sems,
):
    copy_f = copy_in(force_hbm.at[:, around(0)], force, sems.at[0])
    lay_out(u_win, own, before, after, before2, after2)
    copies = [copy_in(u_win.at[:, around(2)], u_hbm, sems.at[1])]

    def image(j):
        return [(w_win, (case, j), apply_plane(u_win, case, j, c0, j)) for case in range(2)]

    planes(1, WINDOW - 1, image)
    copies.append(copy_in(w_win, w_hbm, sems.at[2]))
    copy_f.wait()

    def term(case, k):
        u = own[case, k]
        return (force[case, k] * u, w_win[case, HALO + k] * u)

    rows = accumulate(2, term) + [jnp.zeros((4, 128), F32)]
    copies.append(down(w_win, c0, c1, s1, s2, t_ref, work, s2_hbm, sems.at[3], 2, rows, s21, r1_out, talk))
    for copy in copies:
        copy.wait()


def of_case(row, case):
    return row[:, 64 * case : 64 * case + 1]


def second_kernel(
    own, before, after, before2, after2, dots0, force_hbm, u0_hbm, w0_hbm, c0, c1,
    m_hbm, u1_hbm, w1_hbm, n0_hbm, s2_hbm, s21, r1_out, talk,
    m_win, u0, w0, n0, u1, w1, force, s1, s2, t_ref, work, sems,
):
    copy_w = copy_in(w0_hbm, w0, sems.at[0])
    copy_u = copy_in(u0_hbm, u0, sems.at[1])
    copy_f = copy_in(force_hbm.at[:, around(0)], force, sems.at[2])
    lay_out(m_win, own, before, after, before2, after2)
    copies = [copy_in(m_win.at[:, around(2)], m_hbm, sems.at[3])]
    alpha = [of_case(dots0[2:3, :] / dots0[3:4, :], case) for case in range(2)]
    copy_w.wait()

    def image(j, block=False):
        writes = []
        for case in range(2):
            n = apply_plane(m_win, case, j, c0, j)
            writes.append((w1, (case, j), w0[case, j] - alpha[case] * n))
            if block:
                writes.append((n0, (case, j - HALO), n))
        return writes

    planes(1, HALO, image, 6)
    planes(HALO, HALO + BLOCK, functools.partial(image, block=True))
    planes(HALO + BLOCK, WINDOW - 1, image, 6)
    copies.append(copy_in(n0, n0_hbm, sems.at[4]))
    copies.append(copy_in(w1, w1_hbm, sems.at[5]))
    copy_u.wait()

    def update(i):
        return [(u1, (case, i), u0[case, i] - alpha[case] * m_win[case, i + HALO - 2]) for case in range(2)]

    planes(0, BLOCK + 4, update)
    copies.append(copy_in(u1, u1_hbm, sems.at[6]))
    copy_f.wait()

    def term(case, k):
        j = HALO + k
        u, w, ww = u1[case, k + 2], w1[case, j], w0[case, j]
        r = force[case, k] - alpha[case] * ww
        return (r * u, w * u, u * ww + u0[case, k + 2] * w)

    rows = accumulate(3, term) + [jnp.zeros((3, 128), F32)]
    copies.append(down(w1, c0, c1, s1, s2, t_ref, work, s2_hbm, sems.at[7], 4, rows, s21, r1_out, talk))
    for copy in copies:
        copy.wait()


def third_kernel(
    me_ref, gathered, dots0, s21, r1_ref, c0_hbm, c1_hbm, c2, c3,
    w1_hbm, s2_hbm, force_hbm, u0_hbm, w0_hbm, m0_hbm, n0_hbm, u1_hbm,
    u2, p1, x2, talk, dots1,
    s2, w1, vb, m_win, force, u0, w0, m0, n0, u1, c0, c1, work, sems,
):
    sources = (
        (c1_hbm.at[:, 2:14], c1),
        (s2_hbm, s2),
        (c0_hbm.at[:, around(4)], c0),
        (w1_hbm.at[:, around(3)], w1),
        (force_hbm.at[:, around(0)], force),
        (u0_hbm, u0),
        (w0_hbm.at[:, around(0)], w0),
        (m0_hbm, m0),
        (n0_hbm, n0),
        (u1_hbm, u1),
    )
    copies = [copy_in(a, b, sems.at[i]) for i, (a, b) in enumerate(sources)]
    dots1[...] = sum_of_rows(gathered, 8, 16)
    e2 = coarse_solve(residual_window(me_ref[0], gathered), c2, c3, work)
    copies[0].wait()
    v1 = level1_up(e2, s21[...], r1_ref[2:14], tuple(c1[k] for k in range(COUNT)), work)

    for copy in copies[1:]:
        copy.wait()
    level0_up(v1, s2, w1, vb, c0, m_win, work)

    gamma0, delta0 = dots0[2:3, :], dots0[3:4, :]
    gamma1 = dots1[2:3, :]
    beta = gamma1 / gamma0
    curve = dots1[3:4, :] + beta * dots1[4:5, :] + beta * beta * delta0
    a0 = [of_case(gamma0 / delta0, case) for case in range(2)]
    a1 = [of_case(gamma1 / curve, case) for case in range(2)]
    b1 = [of_case(beta, case) for case in range(2)]

    def update(i):
        writes = []
        for case in range(2):
            p = u1[case, i] + b1[case] * u0[case, i]
            writes.append((p1, (case, i), p))
            writes.append((x2, (case, i), a0[case] * u0[case, i] + a1[case] * p))
            u = u1[case, i] - a1[case] * (m_win[case, i] + b1[case] * m0[case, i])
            writes.append((u2, (case, i), u))
        return writes

    planes(0, 12, update)

    def term(case, k):
        n1 = apply_plane(m_win, case, k + 2, c0, k + 4)
        ww, wv = w0[case, k], w1[case, k + 3]
        s = wv + b1[case] * ww
        w = wv - a1[case] * (n1 + b1[case] * n0[case, k])
        r = force[case, k] - a0[case] * ww - a1[case] * s
        u, p = u2[case, k + 2], p1[case, k + 2]
        return (r * u, w * u, u * s + p * w)

    rows = accumulate(3, term) + [jnp.zeros((5, 128), F32)]
    tile = jnp.concatenate(rows, axis=0)
    talk[...] = jnp.broadcast_to(tile[None], talk.shape)


def last_kernel(gathered, dots0, dots1, u2, p1, x2, mod, free, state, energy, w_win):
    total = add_up([gathered[d] for d in range(gathered.shape[0])])
    gamma0, delta0 = dots0[2:3, :], dots0[3:4, :]
    gamma1 = dots1[2:3, :]
    beta1 = gamma1 / gamma0
    curve1 = dots1[3:4, :] + beta1 * dots1[4:5, :] + beta1 * beta1 * delta0
    gamma2 = total[0:1, :]
    beta2 = gamma2 / gamma1
    curve2 = total[1:2, :] + beta2 * total[2:3, :] + beta2 * beta2 * curve1
    a2 = [of_case(gamma2 / curve2, case) for case in range(2)]
    b2 = [of_case(beta2, case) for case in range(2)]

    def update(i):
        return [
            (w_win, (case, i), x2[case, i] + a2[case] * (u2[case, i] + b2[case] * p1[case, i])) for case in range(2)
        ]

    planes(0, 12, update, 4)
    state[...] = w_win[:, 2:10]

    def hold(i):
        return [(w_win, (case, i), w_win[case, i] * free[i]) for case in range(2)]

    planes(0, 12, hold, 4)
    lane, row = iota((NY, NX), 1), iota((NY, NX), 0)

    def power(i):
        m = mod[i + 1]
        out = jnp.zeros((NY, NX), F32)
        kx = jnp.where(lane > 0, jnp.sqrt(m * roll(m, 1, 1)), 0.0)
        ky = jnp.where(row > 0, jnp.sqrt(m * roll(m, 1, 0)), 0.0)
        kz, kn = jnp.sqrt(m * mod[i]), jnp.sqrt(m * mod[i + 2])
        for case in range(2):
            v = w_win[case, i + 1]
            dx, dy = v - roll(v, 1, 1), v - roll(v, 1, 0)
            dz, dn = v - w_win[case, i], v - w_win[case, i + 2]
            px, py = kx * dx * dx, ky * dy * dy
            out = out + px + roll(px, -1, 1) + py + roll(py, -1, 0) + kz * dz * dz + kn * dn * dn
        return [(energy, (i,), out)]

    planes(0, 10, power, 5)


def sensitivity_kernel(mine, other, scale, passive, out, g, cross, base):
    def gradient(i):
        value = scale[i] * (mine[i] + other[i])
        a, b = filter_parts(value)
        return [(g, (i,), value), (cross, (i,), a), (base, (i,), b)]

    planes(0, 10, gradient, 5)

    def final(k):
        i = k + 1
        value = base[i] + 0.5 * (g[i - 1] + g[i + 1]) + EDGE_WEIGHT * (cross[i - 1] + cross[i + 1])
        return [(out, (k,), jnp.where(passive[k] == 0, value, 0.0))]

    planes(0, 8, final)


def shape(*dims):
    return jax.ShapeDtypeStruct(dims, F32)


def hbm(*dims):
    return pltpu.HBM(dims, F32), pltpu.HBM


def vmem(*dims):
    return shape(*dims), pltpu.VMEM


def call(body, outs, scratch, args, name, sems=0, cost=None):
    pairs = [a if isinstance(a, tuple) else (a, pltpu.VMEM) for a in args]
    scratches = [pltpu.VMEM(s, F32) if isinstance(s, tuple) else s for s in scratch]
    if sems:
        scratches.append(pltpu.SemaphoreType.DMA((sems,)))
    given = [pltpu.with_memory_space_constraint(a, m) if m is pltpu.HBM else a for a, m in pairs]
    return pl.pallas_call(
        body,
        out_shape=[o for o, _ in outs],
        in_specs=[pl.BlockSpec(memory_space=m) for _, m in pairs],
        out_specs=[pl.BlockSpec(memory_space=m) for _, m in outs],
        scratch_shapes=scratches,
        compiler_params=CPARAMS,
        cost_estimate=cost,
        name=name,
    )(*given)


def on_device(design, passive, fixed_mask, load_index):
    members = lax.axis_size("space")
    position = lax.axis_index("space")
    me = position.astype(jnp.int32).reshape(1)
    ahead = [(i, i + 1) for i in range(members - 1)]
    back = [(i + 1, i) for i in range(members - 1)]

    def two_either_side(own, head, tail):
        skip = [(i, i + 2) for i in range(members - 2)]
        skip_back = [(i + 2, i) for i in range(members - 2)]
        away = lax.ppermute(tail, "space", skip), lax.ppermute(head, "space", skip_back)
        if own.ndim == 4:
            own = call(pass_kernel, [vmem(*own.shape)], [], (own,), "pass", cost=LONG)[0]
        return (lax.ppermute(own, "space", ahead), lax.ppermute(own, "space", back)) + away

    def gather(tiles):
        return lax.all_to_all(tiles, "space", 0, 0)

    plane = (NY, NX)
    window = (2, WINDOW) + plane
    block = (2, BLOCK) + plane
    wide = (2, BLOCK + 4) + plane
    wider = (2, BLOCK + 8) + plane
    work = (800, 128)
    t_shape = (2, Q1) + plane
    position_ref = (me, pltpu.SMEM)

    def down_outs(reach, count):
        near = 2 + reach // 2
        return [
            hbm(2, BLOCK + 2 * reach, *plane),
            vmem(4 + 2 * near, R1, 128),
            vmem(Q1, R1, 128),
            vmem(members, count, 128),
        ]

    def far(x):
        return (x, pltpu.HBM)

    case_ref = (lax.axis_index("case").astype(jnp.int32).reshape(1), pltpu.SMEM)
    own, near, head, tail = call(
        collect_kernel,
        [vmem(NEAR, *plane), vmem(NEAR // 2, *plane), vmem(AWAY // 2, *plane), vmem(AWAY // 2, *plane)],
        [(AWAY,) + plane] * 2 + [pltpu.VMEM((BLOCK,) + plane, x.dtype) for x in (design, passive, fixed_mask)],
        (case_ref, far(design), far(passive), far(fixed_mask)),
        "collect",
        3,
    )
    listened = two_either_side(near, head, tail)
    counts = call(
        count_kernel,
        [vmem(*window)],
        [(COUNT_ROWS, 512), (4 * COUNT_ROWS, 128)],
        (position_ref, load_index),
        "counts",
        cost=pl.CostEstimate(flops=3 * 10**10, bytes_accessed=10**7, transcendentals=0),
    )[0]
    listened, counts = lax.optimization_barrier((listened, counts))
    listened += tuple(lax.ppermute(x, "case", [(0, 1), (1, 0)]) for x in listened)
    c0, c1, force, s2, s21, r1, talk, mod, free, scale = call(
        functools.partial(setup_kernel, members),
        [hbm(COUNT0, WINDOW, *plane), hbm(COUNT, Q1, R1, 128), hbm(*window)]
        + down_outs(2, TALK)
        + [hbm(12, *plane), hbm(12, *plane), hbm(10, *plane)],
        [(NEAR,) + plane] * 2
        + [(AWAY,) + plane] * 2
        + [(WINDOW + 2,) + plane] * 3
        + [(COUNT0, WINDOW) + plane, (COUNT, Q1, R1, 128)]
        + [window, (WINDOW,) + plane, (WINDOW,) + plane, (10,) + plane, window, window, t_shape, work]
        + [(Q1, R1, 128)],
        (position_ref, case_ref, own) + listened + (counts,),
        "setup",
        7,
    )

    def up(first, r, s2, s21, r1, talk, more):
        args = (position_ref, gather(talk), far(r), far(s2), s21, r1, far(c0), far(c1)) + tuple(more)
        outs = [vmem(*block), vmem(2, NEXT, *plane), vmem(2, NEXT, *plane)]
        if first:
            outs += [vmem(COUNT, ND, R2, 128), vmem(COUNT, ND, R3, 128)]
        else:
            outs += [vmem(8, 128)]
        scratch = [wide, (2, 10) + plane, (COUNT0, 12) + plane, (COUNT, 10, R1, 128), wide, work, (ND, R2, 128)]
        return call(functools.partial(up_kernel, first), outs, scratch, args, "up", 4)

    u, head, tail, c2, c3 = up(True, force, s2, s21, r1, talk, ())
    u0, w0, s2, s21, r1, talk = call(
        first_kernel,
        [hbm(*wide), hbm(*window)] + down_outs(2, R2),
        [window, window, block, window, window, t_shape, work],
        (u,) + two_either_side(u, head, tail) + (far(force), c0, c1),
        "first",
        4,
    )
    m, head, tail, dots0 = up(False, w0, s2, s21, r1, talk, (c2, c3))
    m0, u1, w1, n0, s2, s21, r1, talk = call(
        second_kernel,
        [hbm(*wide), hbm(*wide), hbm(*window), hbm(*block)] + down_outs(4, R2),
        [window, wide, window, block, wide, window, block, window, window, t_shape, work],
        (m,) + two_either_side(m, head, tail) + (dots0, far(force), far(u0), far(w0), c0, c1),
        "second",
        8,
    )
    u2, p1, x2, talk, dots1 = call(
        third_kernel,
        [vmem(*wide)] * 3 + [vmem(members, 8, 128), vmem(8, 128)],
        [wider, (2, 14) + plane, wider, wide, block, wide, block, wide, block, wide]
        + [(COUNT0, 16) + plane, (COUNT, 12, R1, 128), work],
        (position_ref, gather(talk), dots0, s21, r1, far(c0), far(c1), c2, c3)
        + tuple(far(x) for x in (w1, s2, force, u0, w0, m0, n0, u1)),
        "third",
        10,
    )
    state, energy = call(
        last_kernel,
        [vmem(*block), vmem(10, *plane)],
        [wide],
        (gather(talk), dots0, dots1, u2, p1, x2, mod, free),
        "last",
    )
    other = lax.ppermute(energy, "case", [(0, 1), (1, 0)])
    sensitivity = call(
        sensitivity_kernel,
        [vmem(BLOCK, *plane)],
        [(10,) + plane] * 3,
        (energy, other, scale, passive),
        "sensitivity",
    )[0]
    return state, sensitivity


def solution(mesh):
    placed = (
        P("space", None, None),
        P("space", None, None),
        P("space", None, None),
        P("case", None),
    )
    return jax.shard_map(
        on_device,
        mesh=mesh,
        in_specs=placed,
        out_specs=(P("case", "space", None, None), P("space", None, None)),
        check_vma=False,
    )
```
